128 devices in a mesh: gx: 4 (over y), gy: 4 (over x), zt: 8 (over z, core).
Axes of the slice: x: 4, y: 4, z: 4, core: 2. Of those that a mesh axis runs over, the one named last changes fastest.
Arguments:
- gauge_links: float32 [4, 3, 3, 2, 2, 32, 64, 512], P(None, None, None, None, None, 'zt', 'gy', 'gx'), may hold values from -2 to 2, as said below
- slab_bounds: int32 [2, 9], replicated, may hold values from 0 to 32, as said below
Outputs:
- file_links: float32 [4, 3, 3, 2, 2, 48, 4, 4, 4, 4, 128], P(None, None, None, None, None, 'zt', None, 'gx', None, 'gy')
- plaquette: float32 [2, 32, 64, 512], P(None, 'zt', 'gy', 'gx')
- plaquette_mean: float32 [], replicated
The draws below stay inside these ranges and needn't reach their ends.
Inputs may be any that keep to these rules, and one draw needn't show every extreme that they name: `gauge_links`: every link matrix is strictly diagonally dominant by rows. Each row slab_bounds[t] rises, starts at 0 and ends at 32; each interior slab_bounds[t, w] lies exactly 1 plane from w * 4, on one side in even timeslices and on the other in odd ones; some writer's slab holds 6 z planes.
All inputs are finite; a program needn't handle non-finite values.
Results may differ from the reference program's by a relative error of at most 0.0003.
Values sent between devices are 32-bit elements; how exact they have to be, the bound alone decides.
No kernel may reach another device: no remote copies, remote signals or barrier semaphores. Data moves between devices by JAX's collectives and lax.ppermute only.
A program may use at most 128 MiB of HBM per device.

```python
import jax
import jax.numpy as jnp
from jax import lax

CZ = 4
LT = 2
NX = 512
NY = 64
NZ = 32
WRITERS = 8
SPILL = 1
CAP = 6
RY = 4
RX = 32
N_GX = 4
N_GY = 4


def draw_gauge_links(key, part):
    key = jax.random.fold_in(key, 11)
    angle_key, noise_key = jax.random.split(key)
    position_x = (jnp.arange(NX, dtype=jnp.float32) / NX)[None, None, :]
    position_y = (jnp.arange(NY, dtype=jnp.float32) / NY)[None, :, None]
    position_z = (jnp.arange(NZ, dtype=jnp.float32) / NZ)[:, None, None]
    shape = (4, 3, 3, 2, LT, NZ, NY, NX)
    spread = 0.3 + 2.4 * (position_x + position_y + position_z) / 3.0
    noise = jax.random.uniform(noise_key, shape, jnp.float32, -0.35, 0.35)
    angles = jax.random.uniform(angle_key, (4, 3, LT, NZ, NY, NX), jnp.float32, -1.0, 1.0) * spread
    diagonal = 1.5 * jnp.stack([jnp.cos(angles), jnp.sin(angles)], axis=2)
    identity_matrix = jnp.eye(3, dtype=jnp.float32)[None, :, :, None, None, None, None, None]
    return noise + identity_matrix * diagonal[:, :, None]


def draw_slab_bounds(key, part):
    key = jax.random.fold_in(key, 7)
    sign_key, size_key, place_key = jax.random.split(key, 3)
    positions = jnp.arange(WRITERS + 1, dtype=jnp.int32)
    slices = jnp.arange(LT, dtype=jnp.int32)
    signs = jax.random.randint(sign_key, (WRITERS + 1,), 0, 2, dtype=jnp.int32) * 2 - 1
    sizes = jax.random.randint(size_key, (LT, WRITERS + 1), 1, SPILL + 1, dtype=jnp.int32)
    if WRITERS >= 3:
        chosen = jax.random.randint(place_key, (), 1, WRITERS - 1, dtype=jnp.int32)
        signs = jnp.where(positions == chosen, -1, signs)
        signs = jnp.where(positions == chosen + 1, 1, signs)
        pick = (slices[:, None] == 0) & ((positions[None, :] == chosen) | (positions[None, :] == chosen + 1))
        sizes = jnp.where(pick, SPILL, sizes)
    else:
        forced = jax.random.randint(place_key, (), 0, LT, dtype=jnp.int32)
        sizes = jnp.where(slices[:, None] == forced, SPILL, sizes)
    parity = 1 - 2 * (slices % 2)
    moves = parity[:, None] * signs[None, :] * sizes
    moves = jnp.where((positions[None, :] == 0) | (positions[None, :] == WRITERS), 0, moves)
    return (positions[None, :] * CZ + moves).astype(jnp.int32)


def setup_inputs(seed: int = 0) -> dict:
    seeds = jax.random.split(jax.random.key(seed), 3)
    gauge_links = draw_gauge_links(jax.random.fold_in(seeds[2], 71), 0)
    slab_bounds = draw_slab_bounds(jax.random.fold_in(seeds[2], 71), 0)
    return dict(gauge_links=gauge_links, slab_bounds=slab_bounds)


def complex_product(left_matrix, right_matrix):
    left_real = left_matrix[:, :, 0]
    left_imaginary = left_matrix[:, :, 1]
    right_real = right_matrix[:, :, 0]
    right_imaginary = right_matrix[:, :, 1]
    real_total = 0.0
    imaginary_total = 0.0
    for middle in range(3):
        term_lr = left_real[:, middle:middle + 1]
        term_li = left_imaginary[:, middle:middle + 1]
        term_rr = right_real[middle:middle + 1]
        term_ri = right_imaginary[middle:middle + 1]
        real_total = real_total + (term_lr * term_rr - term_li * term_ri)
        imaginary_total = imaginary_total + (term_lr * term_ri + term_li * term_rr)
    return jnp.stack([real_total, imaginary_total], axis=2)

def reunitarize(gauge_links):
    real_part = gauge_links[:, :, :, 0]
    imaginary = gauge_links[:, :, :, 1]
    top_real = real_part[:, 0]
    top_imaginary = imaginary[:, 0]
    top_norm = jnp.sqrt(lax.optimization_barrier(jnp.sum(top_real * top_real + top_imaginary * top_imaginary, axis=1, keepdims=True)))
    unit_real = top_real / top_norm
    unit_imaginary = top_imaginary / top_norm
    middle_real = real_part[:, 1]
    middle_imaginary = imaginary[:, 1]
    intersection_real = lax.optimization_barrier(jnp.sum(unit_real * middle_real + unit_imaginary * middle_imaginary, axis=1, keepdims=True))
    intersection_imaginary = lax.optimization_barrier(jnp.sum(unit_real * middle_imaginary - unit_imaginary * middle_real, axis=1, keepdims=True))
    ortho_real = middle_real - (intersection_real * unit_real - intersection_imaginary * unit_imaginary)
    ortho_imaginary = middle_imaginary - (intersection_real * unit_imaginary + intersection_imaginary * unit_real)
    middle_norm = jnp.sqrt(lax.optimization_barrier(jnp.sum(ortho_real * ortho_real + ortho_imaginary * ortho_imaginary, axis=1, keepdims=True)))
    second_real = ortho_real / middle_norm
    second_imaginary = ortho_imaginary / middle_norm
    bottom_real = []
    bottom_imaginary = []
    for first_index, second_index in ((1, 2), (2, 0), (0, 1)):
        cross_real = unit_real[:, first_index] * second_real[:, second_index] - unit_imaginary[:, first_index] * second_imaginary[:, second_index] - (unit_real[:, second_index] * second_real[:, first_index] - unit_imaginary[:, second_index] * second_imaginary[:, first_index])
        cross_imaginary = unit_real[:, first_index] * second_imaginary[:, second_index] + unit_imaginary[:, first_index] * second_real[:, second_index] - (unit_real[:, second_index] * second_imaginary[:, first_index] + unit_imaginary[:, second_index] * second_real[:, first_index])
        bottom_real.append(cross_real)
        bottom_imaginary.append(-cross_imaginary)
    bottom_real = jnp.stack(bottom_real, axis=1)
    bottom_imaginary = jnp.stack(bottom_imaginary, axis=1)
    rows_real = jnp.stack([unit_real, second_real, bottom_real], axis=1)
    rows_imaginary = jnp.stack([unit_imaginary, second_imaginary, bottom_imaginary], axis=1)
    return jnp.stack([rows_real, rows_imaginary], axis=3)

def plane_trace(here_mu, ahead_nu, ahead_mu, here_nu):
    loop_one = complex_product(here_mu, ahead_nu)
    loop_two = complex_product(here_nu, ahead_mu)
    return lax.optimization_barrier(jnp.sum(loop_one[:, :, 0] * loop_two[:, :, 0] + loop_one[:, :, 1] * loop_two[:, :, 1], axis=(0, 1))) / 3.0

def reference(gauge_links, slab_bounds):

    def per_time(block):
        unitary = reunitarize(block)
        link_x = unitary[0]
        link_y = unitary[1]
        link_z = unitary[2]
        plane_xy = plane_trace(link_x, jnp.roll(link_y, -1, axis=-1), jnp.roll(link_x, -1, axis=-2), link_y)
        plane_xz = plane_trace(link_x, jnp.roll(link_z, -1, axis=-1), jnp.roll(link_x, -1, axis=-3), link_z)
        plane_yz = plane_trace(link_y, jnp.roll(link_z, -1, axis=-2), jnp.roll(link_y, -1, axis=-3), link_z)
        return (unitary, (plane_xy + plane_xz + plane_yz) / 3.0)
    unitary, plaquette = lax.map(per_time, jnp.moveaxis(gauge_links, 4, 0))
    unitary = jnp.moveaxis(unitary, 0, 4)
    plaquette_mean = jnp.sum(plaquette) / (LT * NZ * NY * NX)
    padded = jnp.pad(unitary, [(0, 0)] * 5 + [(0, CAP), (0, 0), (0, 0)])
    per_slice = []
    for time_index in range(LT):
        slice_links = padded[:, :, :, :, time_index]
        slice_bounds = slab_bounds[time_index]

        def per_writer(writer_index):
            slab_start = slice_bounds[writer_index]
            slab_count = slice_bounds[writer_index + 1] - slab_start
            writer_slab = lax.dynamic_slice_in_dim(slice_links, slab_start.astype(jnp.int32), CAP, 4)
            plane_valid = jnp.arange(CAP, dtype=jnp.int32) < slab_count
            return jnp.where(plane_valid[:, None, None], writer_slab, jnp.float32(0.0))
        slabs = lax.map(per_writer, jnp.arange(WRITERS, dtype=jnp.int32))
        slabs = jnp.moveaxis(slabs, 0, 4).reshape(4, 3, 3, 2, WRITERS * CAP, NY, NX)
        per_slice.append(slabs)
    slabs = jnp.stack(per_slice, axis=4)
    blocked = slabs.reshape(4, 3, 3, 2, LT, WRITERS * CAP, N_GY, N_GX, RY, N_GX, N_GY, RX)
    blocked = blocked.transpose(0, 1, 2, 3, 4, 5, 6, 7, 9, 10, 8, 11)
    file_links = blocked.reshape(4, 3, 3, 2, LT, WRITERS * CAP, N_GY, N_GX, N_GX, N_GY, RY * RX)
    return (file_links, plaquette, plaquette_mean)
```

```python
import jax
import jax.numpy as jnp
from jax import lax
from jax.experimental import pallas as pl
from jax.experimental.pallas import tpu as pltpu
from jax.sharding import PartitionSpec as P

VMEM_LIMIT = 48 * 1024 * 1024
CROSS = ((1, 2), (2, 0), (0, 1))


def passed_along(value, axis, by):
    count = lax.axis_size(axis)
    return lax.ppermute(value, axis, [(i, (i + by) % count) for i in range(count)])


def times(a, b):
    return (a[0] * b[0] - a[1] * b[1], a[0] * b[1] + a[1] * b[0])


def times_conj(a, b):
    return (a[0] * b[0] + a[1] * b[1], a[1] * b[0] - a[0] * b[1])


def minus(a, b):
    return (a[0] - b[0], a[1] - b[1])


def scaled(a, s):
    return (a[0] * s, a[1] * s)


def square(a):
    return a[0] * a[0] + a[1] * a[1]


def last_row(u, v):
    rows = []
    for b, c in CROSS:
        x = minus(times(u[b], v[c]), times(u[c], v[b]))
        rows.append((x[0], -x[1]))
    return rows


def unit_rows(r1, r2):
    n = lax.rsqrt(square(r1[0]) + square(r1[1]) + square(r1[2]))
    u = [scaled(x, n) for x in r1]
    terms = [times_conj(y, x) for x, y in zip(u, r2)]
    c = (terms[0][0] + terms[1][0] + terms[2][0], terms[0][1] + terms[1][1] + terms[2][1])
    v = [minus(y, times(c, x)) for x, y in zip(u, r2)]
    n = lax.rsqrt(square(v[0]) + square(v[1]) + square(v[2]))
    v = [scaled(x, n) for x in v]
    return [u, v, last_row(u, v)]


def angle_value(a):
    t = a[1] / (jnp.abs(a[0]) + jnp.abs(a[1]))
    return jnp.where(a[0] < 0.0, 2.0 - t, t)


def angle_phase(t):
    back = t > 1.0
    y = jnp.where(back, 2.0 - t, t)
    x = 1.0 - jnp.abs(y)
    x = jnp.where(back, -x, x)
    n = lax.rsqrt(x * x + y * y)
    return (x * n, y * n)


def to_parameters(r1, r2):
    inverse = 1.0 / square(r1[0])
    p1 = scaled(times_conj(r1[1], r1[0]), inverse)
    p2 = scaled(times_conj(r1[2], r1[0]), inverse)
    s1 = minus(r2[1], times(r2[0], p1))
    s2 = minus(r2[2], times(r2[0], p2))
    q = scaled(times_conj(s2, s1), 1.0 / square(s1))
    return [p1[0], p1[1], p2[0], p2[1], q[0], q[1], angle_value(r1[0]), angle_value(s1)]


def from_parameters(values):
    p1 = (values[0], values[1])
    p2 = (values[2], values[3])
    q = (values[4], values[5])
    n2 = 1.0 / (1.0 + square(p1) + square(p2))
    a = scaled(angle_phase(values[6]), jnp.sqrt(n2))
    u = [a, times(a, p1), times(a, p2)]
    g = times_conj(q, p2)
    g = ((g[0] + p1[0]) * n2, (g[1] - p1[1]) * n2)
    gp1 = times(g, p1)
    gp2 = times(g, p2)
    v = [(-g[0], -g[1]), (1.0 - gp1[0], -gp1[1]), minus(q, gp2)]
    n = lax.rsqrt(square(v[0]) + square(v[1]) + square(v[2]))
    b = scaled(angle_phase(values[7]), n)
    v = [times(b, x) for x in v]
    return [u, v, last_row(u, v)]


def pairs(parts):
    return [(parts[2 * i], parts[2 * i + 1]) for i in range(len(parts) // 2)]


def moving_times(bounds_ref, w):
    top = jnp.where(bounds_ref[0, w + 1] < 4 * w + 4, 0, 1)
    bottom = jnp.where(bounds_ref[0, w] > 4 * w, 0, 1)
    return top, bottom


def encode_kernel(bounds_ref, links_ref, out_ref):
    w = lax.axis_index("zt")
    top, bottom = moving_times(bounds_ref, w)
    rows = links_ref.reshape(12 * 128, 128)
    out = out_ref.reshape(16 * 64, 128)
    lane = lax.broadcasted_iota(jnp.int32, (8, 128), 1)
    sub = lax.broadcasted_iota(jnp.int32, (8, 128), 0)
    far = (lane & 64) != 0
    near = (lane & 32) != 0
    low = sub < 4
    for pair in range(4):
        t = pair // 2
        if pair % 2 == 0:
            slots = (jnp.where(bottom == t, 1, 3), 4 + 2 * t)
        else:
            slots = (5 + 2 * t, jnp.where(top == t, 0, 2))
        by_row = []
        for r in range(4):
            parts = [rows[pl.ds(c * 128 + pair * 32 + r, 8, stride=4), :] for c in range(12)]
            parts = pairs(parts)
            by_row.append(to_parameters(parts[:3], parts[3:]))
        for p in range(8):
            x = [by_row[r][p] for r in range(4)]
            y = [None] * 4
            for r in (0, 1):
                y[r] = jnp.where(far, pltpu.roll(x[r + 2], 64, 1), x[r])
                y[r + 2] = jnp.where(far, x[r + 2], pltpu.roll(x[r], 64, 1))
            z = [None] * 4
            for r in (0, 2):
                z[r] = jnp.where(near, pltpu.roll(y[r + 1], 32, 1), y[r])
                z[r + 1] = jnp.where(near, y[r + 1], pltpu.roll(y[r], 96, 1))
            for h in (0, 1):
                first = jnp.where(low, z[2 * h], pltpu.roll(z[2 * h + 1], 4, 0))
                second = jnp.where(low, pltpu.roll(z[2 * h], 4, 0), z[2 * h + 1])
                out[pl.ds(h * 512 + slots[0] * 8 + p, 8, stride=64), :] = first
                out[pl.ds(h * 512 + slots[1] * 8 + p, 8, stride=64), :] = second


def encoded(links, bounds):
    return pl.pallas_call(
        encode_kernel,
        grid=(4,),
        in_specs=[
            pl.BlockSpec(memory_space=pltpu.SMEM),
            pl.BlockSpec((1, 2, 3, 2, 2, 4, 16, 128), lambda m: (m, 0, 0, 0, 0, 0, 0, 0)),
        ],
        out_specs=pl.BlockSpec((16, 8, 8, 128), lambda m: (0, 0, m, 0)),
        out_shape=jax.ShapeDtypeStruct((16, 8, 32, 128), jnp.float32),
        compiler_params=pltpu.CompilerParams(vmem_limit_bytes=VMEM_LIMIT),
    )(bounds, links)


def faces_kernel(links_ref, x_ref, y_ref, z_ref):
    m = pl.program_id(0)
    lane = lax.broadcasted_iota(jnp.int32, (8, 128), 1)

    @pl.when(m > 0)
    def _():
        for r in range(2):
            for c in range(3):
                for i in range(2):
                    got = jnp.zeros((8, 128), jnp.float32)
                    for k in range(8):
                        for h in range(2):
                            at = 2 * k + h
                            value = links_ref[0, r, c, i, k // 4, k % 4, pl.ds(8 * h, 8), :]
                            if at:
                                value = pltpu.roll(value, at, 1)
                            got = jnp.where(lane == at, value, got)
                    x_ref[m - 1, r * 6 + c * 2 + i] = got

    @pl.when(m != 1)
    def _():
        for r in range(2):
            for c in range(3):
                for i in range(2):
                    for k in range(8):
                        y_ref[m // 2, r * 6 + c * 2 + i, k, :] = links_ref[0, r, c, i, k // 4, k % 4, 0, :]

    @pl.when(m < 2)
    def _():
        for r in range(2):
            for c in range(3):
                for i in range(2):
                    for t in range(2):
                        z_ref[m, r * 6 + c * 2 + i, t] = links_ref[0, r, c, i, t, 0]


def faces(links):
    whole = lambda n: (lambda m: (0,) * n)
    return pl.pallas_call(
        faces_kernel,
        grid=(3,),
        in_specs=[pl.BlockSpec((1, 2, 3, 2, 2, 4, 16, 128), lambda m: (m, 0, 0, 0, 0, 0, 0, 0))],
        out_specs=[
            pl.BlockSpec((2, 12, 8, 128), whole(4)),
            pl.BlockSpec((2, 12, 8, 128), whole(4)),
            pl.BlockSpec((2, 12, 2, 16, 128), whole(5)),
        ],
        out_shape=[
            jax.ShapeDtypeStruct((2, 12, 8, 128), jnp.float32),
            jax.ShapeDtypeStruct((2, 12, 8, 128), jnp.float32),
            jax.ShapeDtypeStruct((2, 12, 2, 16, 128), jnp.float32),
        ],
        compiler_params=pltpu.CompilerParams(vmem_limit_bytes=VMEM_LIMIT),
    )(links)


def flat_rows(matrix):
    return [part for row in matrix for entry in row for part in entry]


def product_trace(a, b, c, d):
    total = None
    for i in range(3):
        for j in range(3):
            one = two = None
            for k in range(3):
                x = times(a[i][k], b[k][j])
                y = times(c[i][k], d[k][j])
                one = x if one is None else (one[0] + x[0], one[1] + x[1])
                two = y if two is None else (two[0] + y[0], two[1] + y[1])
            term = one[0] * two[0] + one[1] * two[1]
            total = term if total is None else total + term
    return total


def plaquette_kernel(links_ref, x_ref, y_ref, z_ref, out_ref, sum_ref, unit, edge):
    lane = lax.broadcasted_iota(jnp.int32, (8, 128), 1)

    def own(step, carry):
        m = step // 8
        t = (step // 4) % 2
        z = step % 4
        for h in range(2):
            at = pl.ds(8 * h, 8)
            parts = pairs([links_ref[m, r, c, i, t, z, at, :] for r in range(2) for c in range(3) for i in range(2)])
            for c, value in enumerate(flat_rows(unit_rows(parts[:3], parts[3:]))):
                unit[m, c, t, z, at, :] = value
        return carry

    lax.fori_loop(0, 24, own, 0)

    def above(step, carry):
        m = step // 2
        t = step % 2
        for h in range(2):
            at = pl.ds(8 * h, 8)
            parts = pairs([z_ref[m, c, t, at, :] for c in range(12)])
            for c, value in enumerate(flat_rows(unit_rows(parts[:3], parts[3:]))):
                unit[m, c, t, 4, at, :] = value
        return carry

    lax.fori_loop(0, 4, above, 0)
    for m in range(2):
        parts = pairs([y_ref[m, c] for c in range(12)])
        for c, value in enumerate(flat_rows(unit_rows(parts[:3], parts[3:]))):
            for k in range(8):
                unit[2 * m, c, k // 4, k % 4, pl.ds(16, 1), :] = value[k : k + 1]
        parts = pairs([x_ref[m, c] for c in range(12)])
        for c, value in enumerate(flat_rows(unit_rows(parts[:3], parts[3:]))):
            edge[m, c] = value

    def matrix(parts):
        parts = pairs(parts)
        return [parts[3 * i : 3 * i + 3] for i in range(3)]

    def site(step, total):
        t = step // 4
        z = step % 4
        for h in range(2):
            at = pl.ds(8 * h, 8)
            after = pl.ds(8 * h + 1, 8)

            def here(m):
                return matrix([unit[m, c, t, z, at, :] for c in range(18)])

            def next_x(m):
                got = []
                for c in range(18):
                    value = pltpu.roll(unit[m, c, t, z, at, :], 127, 1)
                    beyond = pltpu.roll(edge[m - 1, c], 127 - 2 * step - h, 1)
                    got.append(jnp.where(lane == 127, beyond, value))
                return matrix(got)

            def next_y(m):
                return matrix([unit[m, c, t, z, after, :] for c in range(18)])

            def next_z(m):
                return matrix([unit[m, c, t, z + 1, at, :] for c in range(18)])

            value = product_trace(here(0), next_x(1), here(1), next_y(0))
            value = value + product_trace(here(0), next_x(2), here(2), next_z(0))
            value = value + product_trace(here(1), next_y(2), here(2), next_z(1))
            value = value * (1.0 / 9.0)
            out_ref[t, z, at, :] = value
            total = total + value
        return total

    total = lax.fori_loop(0, 8, site, jnp.zeros((8, 128), jnp.float32))
    sum_ref[...] = jnp.broadcast_to(jnp.sum(total, keepdims=True), (8, 128))


def plaquettes(links, x_face, y_face, z_face):
    whole = lambda n: (lambda m: (0,) * n)
    return pl.pallas_call(
        plaquette_kernel,
        grid=(1,),
        in_specs=[
            pl.BlockSpec((3, 2, 3, 2, 2, 4, 16, 128), whole(8)),
            pl.BlockSpec((2, 12, 8, 128), whole(4)),
            pl.BlockSpec((2, 12, 8, 128), whole(4)),
            pl.BlockSpec((2, 12, 2, 16, 128), whole(5)),
        ],
        out_specs=[pl.BlockSpec((2, 4, 16, 128), whole(4)), pl.BlockSpec((8, 128), whole(2))],
        out_shape=[
            jax.ShapeDtypeStruct((2, 4, 16, 128), jnp.float32),
            jax.ShapeDtypeStruct((8, 128), jnp.float32),
        ],
        scratch_shapes=[
            pltpu.VMEM((3, 18, 2, 5, 24, 128), jnp.float32),
            pltpu.VMEM((2, 18, 8, 128), jnp.float32),
        ],
        compiler_params=pltpu.CompilerParams(vmem_limit_bytes=VMEM_LIMIT),
    )(links, x_face, y_face, z_face)


def decode_kernel(bounds_ref, own_ref, below_ref, above_ref, out_ref, ends):
    w = lax.axis_index("zt")
    top, bottom = moving_times(bounds_ref, w)
    first = [bounds_ref[t, w] - 4 * w for t in range(2)]
    depth = [bounds_ref[t, w + 1] - bounds_ref[t, w] for t in range(2)]
    own = own_ref.reshape(16 * 64, 128)
    below = below_ref.reshape(16 * 8, 128)
    above = above_ref.reshape(16 * 8, 128)

    def taken(part, source, start, stride):
        for h in range(2):
            for p in range(8):
                ends[part, p, pl.ds(8 * h, 8), :] = source[pl.ds(start + p + h * 8 * stride, 8, stride=stride), :]

    @pl.when(w == 0)
    def _():
        taken(0, own, 8, 64)

    @pl.when(w != 0)
    def _():
        taken(0, below, 0, 8)

    @pl.when(w == 7)
    def _():
        taken(1, own, 0, 64)

    @pl.when(w != 7)
    def _():
        taken(1, above, 0, 8)

    def put(t, j, h, values):
        for c, value in enumerate(flat_rows(from_parameters(values))):
            out_ref[c, t, j, pl.ds(8 * h, 8), :] = value

    def start_of(t):
        return jnp.where(t == 0, first[0], first[1])

    low_time = jnp.where(w == 0, bottom, 1 - bottom)
    high_time = jnp.where(w == 7, top, 1 - top)
    high_at = jnp.where(w == 7, 3, 4) - start_of(high_time)
    for h in range(2):
        put(low_time, 0, h, [ends[0, p, pl.ds(8 * h, 8), :] for p in range(8)])
        put(high_time, high_at, h, [ends[1, p, pl.ds(8 * h, 8), :] for p in range(8)])
        for slot in range(2, 8):
            if slot == 2:
                t, z = 1 - top, 3
            elif slot == 3:
                t, z = 1 - bottom, 0
            else:
                t, z = (slot - 4) // 2, 1 + slot % 2
            j = z - start_of(t)
            put(t, j, h, [own[pl.ds(h * 512 + slot * 8 + p, 8, stride=64), :] for p in range(8)])
    for t in range(2):
        for j in range(2, 6):

            @pl.when(j >= depth[t])
            def _(t=t, j=j):
                out_ref[:, t, j] = jnp.zeros((18, 16, 128), jnp.float32)


def decoded(bounds, own, below, above):
    return pl.pallas_call(
        decode_kernel,
        grid=(4,),
        in_specs=[
            pl.BlockSpec(memory_space=pltpu.SMEM),
            pl.BlockSpec((16, 8, 8, 128), lambda m: (0, 0, m, 0)),
            pl.BlockSpec((16, 8, 128), lambda m: (0, m, 0)),
            pl.BlockSpec((16, 8, 128), lambda m: (0, m, 0)),
        ],
        out_specs=pl.BlockSpec((18, 2, 6, 16, 128), lambda m: (m, 0, 0, 0, 0)),
        out_shape=jax.ShapeDtypeStruct((72, 2, 6, 16, 128), jnp.float32),
        scratch_shapes=[pltpu.VMEM((2, 8, 16, 128), jnp.float32)],
        compiler_params=pltpu.CompilerParams(vmem_limit_bytes=VMEM_LIMIT),
    )(bounds, own, below, above)


def local(links, bounds):
    payload = encoded(links, bounds)
    moved = lax.all_to_all(payload, ("gy", "gx"), split_axis=0, concat_axis=0, tiled=True)
    x_face, y_face, z_face = faces(links)
    x_face = passed_along(x_face, "gx", -1)
    y_face = passed_along(y_face, "gy", -1)
    z_face = passed_along(z_face, "zt", -1)
    plaquette, total = plaquettes(links, x_face, y_face, z_face)
    for axis in ("gx", "gy", "zt"):
        count = lax.axis_size(axis)
        by = 1
        while by < count:
            total = total + lax.ppermute(total, axis, [(i, i ^ by) for i in range(count)])
            by *= 2
    below = passed_along(moved[:, 0], "zt", 1)
    above = passed_along(moved[:, 1], "zt", -1)
    file_links = decoded(bounds, moved, below, above)
    sites = plaquette.size * 128
    return (
        file_links.reshape(4, 3, 3, 2, 2, 6, 4, 1, 4, 1, 128),
        plaquette,
        total[0, 0] / sites,
    )


def solution(mesh):
    in_specs = (P(None, None, None, None, None, "zt", "gy", "gx"), P())
    out_specs = (
        P(None, None, None, None, None, "zt", None, "gx", None, "gy", None),
        P(None, "zt", "gy", "gx"),
        P(),
    )
    return jax.shard_map(local, mesh=mesh, in_specs=in_specs, out_specs=out_specs, check_vma=False)
```

```python
import jax
import jax.numpy as jnp
from jax import lax
from jax.experimental import pallas as pl
from jax.experimental.pallas import tpu as pltpu
from jax.sharding import PartitionSpec as P

VMEM_LIMIT = 48 * 1024 * 1024
CROSS = ((1, 2), (2, 0), (0, 1))


def passed_along(value, axis, by):
    count = lax.axis_size(axis)
    return lax.ppermute(value, axis, [(i, (i + by) % count) for i in range(count)])


def times(a, b):
    return (a[0] * b[0] - a[1] * b[1], a[0] * b[1] + a[1] * b[0])


def times_conj(a, b):
    return (a[0] * b[0] + a[1] * b[1], a[1] * b[0] - a[0] * b[1])


def minus(a, b):
    return (a[0] - b[0], a[1] - b[1])


def scaled(a, s):
    return (a[0] * s, a[1] * s)


def square(a):
    return a[0] * a[0] + a[1] * a[1]


def last_row(u, v):
    rows = []
    for b, c in CROSS:
        x = minus(times(u[b], v[c]), times(u[c], v[b]))
        rows.append((x[0], -x[1]))
    return rows


def unit_rows(r1, r2):
    n = lax.rsqrt(square(r1[0]) + square(r1[1]) + square(r1[2]))
    u = [scaled(x, n) for x in r1]
    terms = [times_conj(y, x) for x, y in zip(u, r2)]
    c = (terms[0][0] + terms[1][0] + terms[2][0], terms[0][1] + terms[1][1] + terms[2][1])
    v = [minus(y, times(c, x)) for x, y in zip(u, r2)]
    n = lax.rsqrt(square(v[0]) + square(v[1]) + square(v[2]))
    v = [scaled(x, n) for x in v]
    return [u, v, last_row(u, v)]


def angle_value(a):
    t = a[1] / (jnp.abs(a[0]) + jnp.abs(a[1]))
    return jnp.where(a[0] < 0.0, 2.0 - t, t)


def angle_phase(t):
    back = t > 1.0
    y = jnp.where(back, 2.0 - t, t)
    x = 1.0 - jnp.abs(y)
    x = jnp.where(back, -x, x)
    n = lax.rsqrt(x * x + y * y)
    return (x * n, y * n)


def to_parameters(r1, r2):
    inverse = 1.0 / square(r1[0])
    p1 = scaled(times_conj(r1[1], r1[0]), inverse)
    p2 = scaled(times_conj(r1[2], r1[0]), inverse)
    s1 = minus(r2[1], times(r2[0], p1))
    s2 = minus(r2[2], times(r2[0], p2))
    q = scaled(times_conj(s2, s1), 1.0 / square(s1))
    return [p1[0], p1[1], p2[0], p2[1], q[0], q[1], angle_value(r1[0]), angle_value(s1)]


def from_parameters(values):
    p1 = (values[0], values[1])
    p2 = (values[2], values[3])
    q = (values[4], values[5])
    n2 = 1.0 / (1.0 + square(p1) + square(p2))
    a = scaled(angle_phase(values[6]), jnp.sqrt(n2))
    u = [a, times(a, p1), times(a, p2)]
    g = times_conj(q, p2)
    g = ((g[0] + p1[0]) * n2, (g[1] - p1[1]) * n2)
    gp1 = times(g, p1)
    gp2 = times(g, p2)
    v = [(-g[0], -g[1]), (1.0 - gp1[0], -gp1[1]), minus(q, gp2)]
    n = lax.rsqrt(square(v[0]) + square(v[1]) + square(v[2]))
    b = scaled(angle_phase(values[7]), n)
    v = [times(b, x) for x in v]
    return [u, v, last_row(u, v)]


def pairs(parts):
    return [(parts[2 * i], parts[2 * i + 1]) for i in range(len(parts) // 2)]


def moving_times(bounds_ref, w):
    top = jnp.where(bounds_ref[0, w + 1] < 4 * w + 4, 0, 1)
    bottom = jnp.where(bounds_ref[0, w] > 4 * w, 0, 1)
    return top, bottom


def turned(x, lane):
    odd = (lane & 32) != 0
    far = (lane & 64) != 0
    x = [jnp.where(odd, x[(d + 1) % 4], x[d]) for d in range(4)]
    x = [jnp.where(far, x[(d + 2) % 4], x[d]) for d in range(4)]
    x = [pltpu.roll(x[d], 32 * d, 1) if d else x[d] for d in range(4)]
    x = [jnp.where(odd, x[(1 - g) % 4], x[-g % 4]) for g in range(4)]
    return [jnp.where(far, x[(g + 2) % 4], x[g]) for g in range(4)]


def encode_kernel(links_ref, out_ref, taken, given, in_sem, out_sem):
    lane = lax.broadcasted_iota(jnp.int32, (8, 128), 1)
    low = lax.broadcasted_iota(jnp.int32, (8, 128), 0) < 4

    def copy_in(step):
        return pltpu.make_async_copy(
            links_ref.at[step // 2, pl.ds(0, 2), :, :, step % 2], taken.at[step], in_sem.at[step]
        )

    def copy_out(step):
        at = pl.ds(pl.multiple_of((step % 2) * 32, 32), 32)
        return pltpu.make_async_copy(given.at[step], out_ref.at[:, step // 2, at], out_sem.at[step])

    for step in range(8):
        copy_in(step).start()

    def one(step, carry):
        copy_in(step).wait()
        rows = taken.at[step].reshape(12 * 64, 128)
        out = given.at[step].reshape(16 * 32, 128)
        for pair in range(2):
            by_row = []
            for r in range(4):
                parts = pairs([rows[pl.ds(c * 64 + pair * 32 + r, 8, stride=4), :] for c in range(12)])
                by_row.append(to_parameters(parts[:3], parts[3:]))
            for p in range(8):
                z = turned([by_row[r][p] for r in range(4)], lane)
                for h in (0, 1):
                    first = jnp.where(low, z[2 * h], pltpu.roll(z[2 * h + 1], 4, 0))
                    second = jnp.where(low, pltpu.roll(z[2 * h], 4, 0), z[2 * h + 1])
                    out[pl.ds(h * 256 + 16 * pair + p, 8, stride=32), :] = first
                    out[pl.ds(h * 256 + 16 * pair + 8 + p, 8, stride=32), :] = second
        copy_out(step).start()
        return carry

    lax.fori_loop(0, 8, one, 0)
    for step in range(8):
        copy_out(step).wait()


def encoded(links):
    return pl.pallas_call(
        encode_kernel,
        in_specs=[pl.BlockSpec(memory_space=pltpu.HBM)],
        out_specs=pl.BlockSpec(memory_space=pltpu.HBM),
        out_shape=pltpu.HBM((16, 4, 64, 128), jnp.float32),
        scratch_shapes=[
            pltpu.VMEM((8, 2, 3, 2, 4, 16, 128), jnp.float32),
            pltpu.VMEM((8, 16, 32, 128), jnp.float32),
            pltpu.SemaphoreType.DMA((8,)),
            pltpu.SemaphoreType.DMA((8,)),
        ],
        compiler_params=pltpu.CompilerParams(vmem_limit_bytes=VMEM_LIMIT),
    )(links)


def faces_kernel(links_ref, x_ref, y_ref, z_ref, taken, sem):
    lane = lax.broadcasted_iota(jnp.int32, (8, 128), 1)
    copies = [
        pltpu.make_async_copy(links_ref.at[2, pl.ds(0, 2)], taken.at[1], sem.at[1]),
        pltpu.make_async_copy(links_ref.at[1, pl.ds(0, 2)], taken.at[0], sem.at[0]),
        pltpu.make_async_copy(
            links_ref.at[0, pl.ds(0, 2), :, :, :, :, pl.ds(0, 8)], taken.at[2, :, :, :, :, :, pl.ds(0, 8)], sem.at[2]
        ),
        pltpu.make_async_copy(links_ref.at[pl.ds(0, 2), pl.ds(0, 2), :, :, :, 0], z_ref, sem.at[3]),
    ]
    for copy in copies:
        copy.start()
    entries = [(r, c, i) for r in range(2) for c in range(3) for i in range(2)]
    for m in (1, 0):
        copies[1 - m].wait()
        for e, (r, c, i) in enumerate(entries):
            got = None
            for k in range(8):
                for h in range(2):
                    at = 2 * k + h
                    value = taken[m, r, c, i, k // 4, k % 4, pl.ds(8 * h, 8), :]
                    got = jnp.where(lane == at, pltpu.roll(value, at, 1), got) if at else value
            x_ref[m, e] = got
    copies[2].wait()
    for m in range(2):
        for e, (r, c, i) in enumerate(entries):
            for k in range(8):
                y_ref[m, e, pl.ds(k, 1), :] = taken[2 - m, r, c, i, k // 4, k % 4, pl.ds(0, 1), :]
    copies[3].wait()


def faces(links):
    return pl.pallas_call(
        faces_kernel,
        in_specs=[pl.BlockSpec(memory_space=pltpu.HBM)],
        out_shape=[
            jax.ShapeDtypeStruct((2, 12, 8, 128), jnp.float32),
            jax.ShapeDtypeStruct((2, 12, 8, 128), jnp.float32),
            jax.ShapeDtypeStruct((2, 2, 3, 2, 2, 16, 128), jnp.float32),
        ],
        scratch_shapes=[
            pltpu.VMEM((3, 2, 3, 2, 2, 4, 16, 128), jnp.float32),
            pltpu.SemaphoreType.DMA((4,)),
        ],
        compiler_params=pltpu.CompilerParams(vmem_limit_bytes=VMEM_LIMIT),
    )(links)


def flat_rows(matrix):
    return [part for row in matrix for entry in row for part in entry]


def product_trace(a, b, c, d):
    total = None
    for i in range(3):
        for j in range(3):
            one = two = None
            for k in range(3):
                x = times(a[i][k], b[k][j])
                y = times(c[i][k], d[k][j])
                one = x if one is None else (one[0] + x[0], one[1] + x[1])
                two = y if two is None else (two[0] + y[0], two[1] + y[1])
            term = one[0] * two[0] + one[1] * two[1]
            total = term if total is None else total + term
    return total


def plaquette_kernel(links_ref, x_ref, y_ref, z_ref, out_ref, sum_ref, unit, edge, taken, sem):
    lane = lax.broadcasted_iota(jnp.int32, (8, 128), 1)

    def copy_in(m):
        return pltpu.make_async_copy(links_ref.at[m, pl.ds(0, 2)], taken.at[m], sem.at[m])

    for m in range(3):
        copy_in(m).start()

    def own(step, carry):
        m = step // 8
        t = (step // 4) % 2
        z = step % 4

        @pl.when(step % 8 == 0)
        def _():
            copy_in(m).wait()

        for h in range(2):
            at = pl.ds(8 * h, 8)
            parts = pairs([taken[m, r, c, i, t, z, at, :] for r in range(2) for c in range(3) for i in range(2)])
            for c, value in enumerate(flat_rows(unit_rows(parts[:3], parts[3:]))):
                unit[m, c, t, z, at, :] = value
        return carry

    lax.fori_loop(0, 24, own, 0)

    def above(step, carry):
        m = step // 2
        t = step % 2
        for h in range(2):
            at = pl.ds(8 * h, 8)
            parts = pairs([z_ref[m, r, c, i, t, at, :] for r in range(2) for c in range(3) for i in range(2)])
            for c, value in enumerate(flat_rows(unit_rows(parts[:3], parts[3:]))):
                unit[m, c, t, 4, at, :] = value
        return carry

    lax.fori_loop(0, 4, above, 0)
    for m in range(2):
        parts = pairs([y_ref[m, c] for c in range(12)])
        for c, value in enumerate(flat_rows(unit_rows(parts[:3], parts[3:]))):
            for k in range(8):
                unit[2 * m, c, k // 4, k % 4, pl.ds(16, 1), :] = value[k : k + 1]
        parts = pairs([x_ref[m, c] for c in range(12)])
        for c, value in enumerate(flat_rows(unit_rows(parts[:3], parts[3:]))):
            edge[m, c] = value

    def matrix(parts):
        parts = pairs(parts)
        return [parts[3 * i : 3 * i + 3] for i in range(3)]

    def site(step, total):
        t = step // 4
        z = step % 4
        for h in range(2):
            at = pl.ds(8 * h, 8)
            after = pl.ds(8 * h + 1, 8)

            def here(m):
                return matrix([unit[m, c, t, z, at, :] for c in range(18)])

            def next_x(m):
                got = []
                for c in range(18):
                    value = pltpu.roll(unit[m, c, t, z, at, :], 127, 1)
                    beyond = pltpu.roll(edge[m - 1, c], 127 - 2 * step - h, 1)
                    got.append(jnp.where(lane == 127, beyond, value))
                return matrix(got)

            def next_y(m):
                return matrix([unit[m, c, t, z, after, :] for c in range(18)])

            def next_z(m):
                return matrix([unit[m, c, t, z + 1, at, :] for c in range(18)])

            value = product_trace(here(0), next_x(1), here(1), next_y(0))
            value = value + product_trace(here(0), next_x(2), here(2), next_z(0))
            value = value + product_trace(here(1), next_y(2), here(2), next_z(1))
            value = value * (1.0 / 9.0)
            out_ref[t, z, at, :] = value
            total = total + value
        return total

    total = lax.fori_loop(0, 8, site, jnp.zeros((8, 128), jnp.float32))
    sum_ref[...] = jnp.broadcast_to(jnp.sum(total, keepdims=True), (8, 128))


def plaquettes(links, x_face, y_face, z_face):
    return pl.pallas_call(
        plaquette_kernel,
        in_specs=[pl.BlockSpec(memory_space=pltpu.HBM)] + [pl.BlockSpec(memory_space=pltpu.VMEM)] * 3,
        out_shape=[
            jax.ShapeDtypeStruct((2, 4, 16, 128), jnp.float32),
            jax.ShapeDtypeStruct((8, 128), jnp.float32),
        ],
        scratch_shapes=[
            pltpu.VMEM((3, 18, 2, 5, 24, 128), jnp.float32),
            pltpu.VMEM((2, 18, 8, 128), jnp.float32),
            pltpu.VMEM((3, 2, 3, 2, 2, 4, 16, 128), jnp.float32),
            pltpu.SemaphoreType.DMA((3,)),
        ],
        compiler_params=pltpu.CompilerParams(vmem_limit_bytes=VMEM_LIMIT),
    )(links, x_face, y_face, z_face)


def decode_kernel(bounds_ref, own_ref, out_ref):
    w = lax.axis_index("zt")
    top, bottom = moving_times(bounds_ref, w)
    own = own_ref.reshape(16 * 64, 128)

    def put(t, z, h):
        at = h * 512 + (t * 4 + z) * 8
        j = z + 4 * w - bounds_ref[t, w]
        values = [own[pl.ds(at + p, 8, stride=64), :] for p in range(8)]
        for c, value in enumerate(flat_rows(from_parameters(values))):
            out_ref[c, t, j, pl.ds(8 * h, 8), :] = value

    for h in range(2):
        put(1 - top, 3, h)
        put(1 - bottom, 0, h)
        for t in range(2):
            for z in (1, 2):
                put(t, z, h)
    for t in range(2):
        depth = bounds_ref[t, w + 1] - bounds_ref[t, w]
        for j in range(2, 6):

            @pl.when(j >= depth)
            def _(t=t, j=j):
                out_ref[:, t, j] = jnp.zeros((18, 16, 128), jnp.float32)


def decoded(bounds, own):
    return pl.pallas_call(
        decode_kernel,
        grid=(4,),
        in_specs=[
            pl.BlockSpec(memory_space=pltpu.SMEM),
            pl.BlockSpec((16, 1, 64, 128), lambda m: (0, m, 0, 0)),
        ],
        out_specs=pl.BlockSpec((18, 2, 6, 16, 128), lambda m: (m, 0, 0, 0, 0)),
        out_shape=jax.ShapeDtypeStruct((72, 2, 6, 16, 128), jnp.float32),
        compiler_params=pltpu.CompilerParams(vmem_limit_bytes=VMEM_LIMIT),
    )(bounds, own)


def ends_kernel(bounds_ref, below_ref, above_ref, bottom_ref, top_ref, whole_ref, out_ref, ends, planes, sem):
    w = lax.axis_index("zt")
    top, bottom = moving_times(bounds_ref, w)
    first, last = w == 0, w == 7

    def taken(part, source_ref):
        ends[part] = source_ref[...]

    pl.when(first)(lambda: taken(0, bottom_ref))
    pl.when(jnp.logical_not(first))(lambda: taken(0, below_ref))
    pl.when(last)(lambda: taken(1, top_ref))
    pl.when(jnp.logical_not(last))(lambda: taken(1, above_ref))
    low_time = jnp.where(first, bottom, 1 - bottom)
    high_time = jnp.where(last, top, 1 - top)
    high_at = jnp.where(last, 3, 4) + 4 * w - bounds_ref[high_time, w]
    places = ((low_time, 0), (high_time, high_at))

    def copy_out(part, m):
        t, j = places[part]
        return pltpu.make_async_copy(planes.at[part, m], out_ref.at[pl.ds(18 * m, 18), t, j], sem.at[part, m])

    def one(m, carry):
        for part in range(2):
            rows = ends.at[part].reshape(16 * 32, 128)
            for h in range(2):
                at = h * 256 + m * 8
                values = [rows[pl.ds(at + p, 8, stride=32), :] for p in range(8)]
                for c, value in enumerate(flat_rows(from_parameters(values))):
                    planes[part, m, c, pl.ds(8 * h, 8), :] = value
            copy_out(part, m).start()
        return carry

    lax.fori_loop(0, 4, one, 0)
    for m in range(4):
        for part in range(2):
            copy_out(part, m).wait()


def with_ends(bounds, below, above, bottom, top, whole):
    return pl.pallas_call(
        ends_kernel,
        in_specs=[pl.BlockSpec(memory_space=pltpu.SMEM)]
        + [pl.BlockSpec(memory_space=pltpu.VMEM)] * 4
        + [pl.BlockSpec(memory_space=pltpu.HBM)],
        out_specs=pl.BlockSpec(memory_space=pltpu.HBM),
        out_shape=jax.ShapeDtypeStruct((72, 2, 6, 16, 128), jnp.float32),
        input_output_aliases={5: 0},
        scratch_shapes=[
            pltpu.VMEM((2, 16, 4, 8, 128), jnp.float32),
            pltpu.VMEM((2, 4, 18, 16, 128), jnp.float32),
            pltpu.SemaphoreType.DMA((2, 4)),
        ],
        compiler_params=pltpu.CompilerParams(vmem_limit_bytes=VMEM_LIMIT),
    )(bounds, below, above, bottom, top, whole)


def summed(value, steps):
    for axis, by in steps:
        count = lax.axis_size(axis)
        value = value + lax.ppermute(value, axis, [(i, i ^ by) for i in range(count)])
    return value


def local(links, bounds):
    w = lax.axis_index("zt")
    top, bottom = moving_times(bounds, w)
    links = pltpu.with_memory_space_constraint(links, pltpu.HBM)
    payload = encoded(links)
    moved = lax.all_to_all(payload, ("gy", "gx"), split_axis=0, concat_axis=0, tiled=True)
    x_face, y_face, z_face = faces(links)
    x_face = passed_along(x_face, "gx", -1)
    y_face = passed_along(y_face, "gy", -1)
    z_face = passed_along(z_face, "zt", -1)
    plaquette, total = plaquettes(links, x_face, y_face, z_face)
    total = summed(total, (("gx", 1), ("gx", 3), ("gy", 1), ("gy", 3)))
    moved, total = lax.optimization_barrier((moved, total))
    top_plane = lax.dynamic_slice_in_dim(moved, (top * 4 + 3) * 8, 8, 2)
    bottom_plane = lax.dynamic_slice_in_dim(moved, bottom * 32, 8, 2)
    below = passed_along(top_plane, "zt", 1)
    above = passed_along(bottom_plane, "zt", -1)
    file_links = decoded(bounds, moved)
    total = summed(total, (("zt", 1), ("zt", 2), ("zt", 6)))
    file_links = with_ends(bounds, below, above, bottom_plane, top_plane, file_links)
    sites = plaquette.size * 128
    return (
        file_links.reshape(4, 3, 3, 2, 2, 6, 4, 1, 4, 1, 128),
        plaquette,
        total[0, 0] / sites,
    )


def solution(mesh):
    in_specs = (P(None, None, None, None, None, "zt", "gy", "gx"), P())
    out_specs = (
        P(None, None, None, None, None, "zt", None, "gx", None, "gy", None),
        P(None, "zt", "gy", "gx"),
        P(),
    )
    return jax.shard_map(local, mesh=mesh, in_specs=in_specs, out_specs=out_specs, check_vma=False)
```

```python
import jax
import jax.numpy as jnp
from jax import lax
from jax.experimental import pallas as pl
from jax.experimental.pallas import tpu as pltpu
from jax.sharding import PartitionSpec as P

VMEM_LIMIT = 24 * 1024 * 1024
CROSS = ((1, 2), (2, 0), (0, 1))


def passed_along(value, axis, by):
    count = lax.axis_size(axis)
    return lax.ppermute(value, axis, [(i, (i + by) % count) for i in range(count)])


def times(a, b):
    return (a[0] * b[0] - a[1] * b[1], a[0] * b[1] + a[1] * b[0])


def times_conj(a, b):
    return (a[0] * b[0] + a[1] * b[1], a[1] * b[0] - a[0] * b[1])


def minus(a, b):
    return (a[0] - b[0], a[1] - b[1])


def scaled(a, s):
    return (a[0] * s, a[1] * s)


def square(a):
    return a[0] * a[0] + a[1] * a[1]


def last_row(u, v):
    rows = []
    for b, c in CROSS:
        x = minus(times(u[b], v[c]), times(u[c], v[b]))
        rows.append((x[0], -x[1]))
    return rows


def unit_rows(r1, r2):
    n = lax.rsqrt(square(r1[0]) + square(r1[1]) + square(r1[2]))
    u = [scaled(x, n) for x in r1]
    terms = [times_conj(y, x) for x, y in zip(u, r2)]
    c = (terms[0][0] + terms[1][0] + terms[2][0], terms[0][1] + terms[1][1] + terms[2][1])
    v = [minus(y, times(c, x)) for x, y in zip(u, r2)]
    n = lax.rsqrt(square(v[0]) + square(v[1]) + square(v[2]))
    v = [scaled(x, n) for x in v]
    return [u, v, last_row(u, v)]


def angle_value(a):
    t = a[1] / (jnp.abs(a[0]) + jnp.abs(a[1]))
    return jnp.where(a[0] < 0.0, 2.0 - t, t)


def angle_phase(t):
    back = t > 1.0
    y = jnp.where(back, 2.0 - t, t)
    x = 1.0 - jnp.abs(y)
    x = jnp.where(back, -x, x)
    n = lax.rsqrt(x * x + y * y)
    return (x * n, y * n)


def to_parameters(r1, r2):
    inverse = 1.0 / square(r1[0])
    p1 = scaled(times_conj(r1[1], r1[0]), inverse)
    p2 = scaled(times_conj(r1[2], r1[0]), inverse)
    s1 = minus(r2[1], times(r2[0], p1))
    s2 = minus(r2[2], times(r2[0], p2))
    q = scaled(times_conj(s2, s1), 1.0 / square(s1))
    return [p1[0], p1[1], p2[0], p2[1], q[0], q[1], angle_value(r1[0]), angle_value(s1)]


def from_parameters(values):
    p1 = (values[0], values[1])
    p2 = (values[2], values[3])
    q = (values[4], values[5])
    n2 = 1.0 / (1.0 + square(p1) + square(p2))
    a = scaled(angle_phase(values[6]), jnp.sqrt(n2))
    u = [a, times(a, p1), times(a, p2)]
    g = times_conj(q, p2)
    g = ((g[0] + p1[0]) * n2, (g[1] - p1[1]) * n2)
    gp1 = times(g, p1)
    gp2 = times(g, p2)
    v = [(-g[0], -g[1]), (1.0 - gp1[0], -gp1[1]), minus(q, gp2)]
    n = lax.rsqrt(square(v[0]) + square(v[1]) + square(v[2]))
    b = scaled(angle_phase(values[7]), n)
    v = [times(b, x) for x in v]
    return [u, v, last_row(u, v)]


ENTRIES = [(r, c, i) for r in range(2) for c in range(3) for i in range(2)]


def pairs(parts):
    return [(parts[2 * i], parts[2 * i + 1]) for i in range(len(parts) // 2)]


def moving_times(bounds_ref, w):
    top = jnp.where(bounds_ref[0, w + 1] < 4 * w + 4, 0, 1)
    bottom = jnp.where(bounds_ref[0, w] > 4 * w, 0, 1)
    return top, bottom


def turned(x, lane):
    odd = (lane & 32) != 0
    far = (lane & 64) != 0
    x = [jnp.where(odd, x[(d + 1) % 4], x[d]) for d in range(4)]
    x = [jnp.where(far, x[(d + 2) % 4], x[d]) for d in range(4)]
    x = [pltpu.roll(x[d], 32 * d, 1) if d else x[d] for d in range(4)]
    x = [jnp.where(odd, x[(1 - g) % 4], x[-g % 4]) for g in range(4)]
    return [jnp.where(far, x[(g + 2) % 4], x[g]) for g in range(4)]


def encode_planes(rows, out, stride):
    lane = lax.broadcasted_iota(jnp.int32, (8, 128), 1)
    low = lax.broadcasted_iota(jnp.int32, (8, 128), 0) < 4
    by_row = []
    for r in range(4):
        parts = pairs([rows[pl.ds(c * 32 + r, 8, stride=4), :] for c in range(12)])
        by_row.append(to_parameters(parts[:3], parts[3:]))
    for p in range(8):
        z = turned([by_row[r][p] for r in range(4)], lane)
        for h in (0, 1):
            first = jnp.where(low, z[2 * h], pltpu.roll(z[2 * h + 1], 4, 0))
            second = jnp.where(low, pltpu.roll(z[2 * h], 4, 0), z[2 * h + 1])
            out[pl.ds(h * 8 * stride + p, 8, stride=stride), :] = first
            out[pl.ds(h * 8 * stride + 8 + p, 8, stride=stride), :] = second


def encode_kernel(links_ref, out_ref, taken, given, in_sem, out_sem):
    def copy_in(m, pair):
        if pair == 2:
            source = links_ref.at[m, pl.ds(0, 2), :, :, :, 3]
        else:
            source = links_ref.at[m, pl.ds(0, 2), :, :, pair, pl.ds(0, 2)]
        return pltpu.make_async_copy(source, taken.at[3 * m + pair], in_sem.at[3 * m + pair])

    def copy_out(step):
        at = pl.ds(pl.multiple_of((step % 3) * 16, 16), 16)
        return pltpu.make_async_copy(given.at[step], out_ref.at[:, step // 3, at], out_sem.at[step])

    for m in range(4):
        for pair in range(3):
            copy_in(m, pair).start()

    def one(step, carry):
        pltpu.make_async_copy(taken.at[step], taken.at[step], in_sem.at[step]).wait()
        encode_planes(taken.at[step].reshape(12 * 32, 128), given.at[step].reshape(16 * 16, 128), 16)
        copy_out(step).start()
        return carry

    lax.fori_loop(0, 12, one, 0)
    for step in range(12):
        copy_out(step).wait()


def encoded(links):
    return pl.pallas_call(
        encode_kernel,
        in_specs=[pl.BlockSpec(memory_space=pltpu.HBM)],
        out_specs=pl.BlockSpec(memory_space=pltpu.HBM),
        out_shape=pltpu.HBM((16, 4, 48, 128), jnp.float32),
        scratch_shapes=[
            pltpu.VMEM((12, 2, 3, 2, 2, 16, 128), jnp.float32),
            pltpu.VMEM((12, 16, 16, 128), jnp.float32),
            pltpu.SemaphoreType.DMA((12,)),
            pltpu.SemaphoreType.DMA((12,)),
        ],
        compiler_params=pltpu.CompilerParams(vmem_limit_bytes=VMEM_LIMIT),
    )(links)


def encode_rest_kernel(links_ref, total_ref, out_ref, taken, in_sem):
    def copy_in(m):
        return pltpu.make_async_copy(links_ref.at[m, pl.ds(0, 2), :, :, :, 2], taken.at[m], in_sem.at[m])

    for m in range(4):
        copy_in(m).start()
    out = out_ref.reshape(16 * 72, 128)
    for n in range(16):
        out_ref[n, pl.ds(64, 8), :] = total_ref[...]

    def one(m, carry):
        copy_in(m).wait()
        encode_planes(taken.at[m].reshape(12 * 32, 128), ShiftedRows(out, m * 16), 72)
        return carry

    lax.fori_loop(0, 4, one, 0)


class ShiftedRows:
    def __init__(self, ref, by):
        self.ref = ref
        self.by = by

    def __setitem__(self, at, value):
        self.ref[pl.ds(self.by + at[0].start, at[0].size, stride=at[0].stride), :] = value


def encoded_rest(links, total):
    return pl.pallas_call(
        encode_rest_kernel,
        in_specs=[pl.BlockSpec(memory_space=pltpu.HBM), pl.BlockSpec(memory_space=pltpu.VMEM)],
        out_shape=jax.ShapeDtypeStruct((16, 72, 128), jnp.float32),
        scratch_shapes=[
            pltpu.VMEM((4, 2, 3, 2, 2, 16, 128), jnp.float32),
            pltpu.SemaphoreType.DMA((4,)),
        ],
        compiler_params=pltpu.CompilerParams(vmem_limit_bytes=VMEM_LIMIT),
    )(links, total)


def faces_kernel(links_ref, x_ref, y_ref, z_ref, taken, sem):
    lane = lax.broadcasted_iota(jnp.int32, (8, 128), 1)
    copies = [
        pltpu.make_async_copy(
            links_ref.at[0, pl.ds(0, 2), :, :, :, :, pl.ds(0, 8)], taken.at[2, :, :, :, :, :, pl.ds(0, 8)], sem.at[2]
        ),
        pltpu.make_async_copy(links_ref.at[2, pl.ds(0, 2)], taken.at[1], sem.at[1]),
        pltpu.make_async_copy(links_ref.at[1, pl.ds(0, 2)], taken.at[0], sem.at[0]),
        pltpu.make_async_copy(links_ref.at[pl.ds(0, 2), pl.ds(0, 2), :, :, :, 0], z_ref, sem.at[3]),
    ]
    for copy in copies:
        copy.start()

    def row_face(m):
        rows = [
            jnp.concatenate([taken[2 - m, r, c, i, k // 4, k % 4, pl.ds(0, 1), :] for k in range(8)], axis=0)
            for r, c, i in ENTRIES
        ]
        parts = pairs(rows)
        for p, value in enumerate(to_parameters(parts[:3], parts[3:])):
            y_ref[m, p] = value

    copies[0].wait()
    row_face(0)
    copies[1].wait()
    row_face(1)
    got = [None] * 3
    for m in (1, 0):
        if m == 0:
            copies[2].wait()
        for e, (r, c, i) in enumerate(ENTRIES):
            n = 12 * m + e
            for k in range(8):
                for h in range(2):
                    at = 16 * (n % 8) + 2 * k + h
                    value = taken[m, r, c, i, k // 4, k % 4, pl.ds(8 * h, 8), :]
                    value = pltpu.roll(value, at, 1) if at else value
                    got[n // 8] = value if got[n // 8] is None else jnp.where(lane == at, value, got[n // 8])
    for n in range(3):
        x_ref[n] = got[n]
    copies[3].wait()


def faces(links):
    return pl.pallas_call(
        faces_kernel,
        in_specs=[pl.BlockSpec(memory_space=pltpu.HBM)],
        out_shape=[
            jax.ShapeDtypeStruct((3, 8, 128), jnp.float32),
            jax.ShapeDtypeStruct((2, 8, 8, 128), jnp.float32),
            jax.ShapeDtypeStruct((2, 2, 3, 2, 2, 16, 128), jnp.float32),
        ],
        scratch_shapes=[
            pltpu.VMEM((3, 2, 3, 2, 2, 4, 16, 128), jnp.float32),
            pltpu.SemaphoreType.DMA((4,)),
        ],
        compiler_params=pltpu.CompilerParams(vmem_limit_bytes=VMEM_LIMIT),
    )(links)


def flat_rows(matrix):
    return [part for row in matrix for entry in row for part in entry]


def product_trace(a, b, c, d):
    total = None
    for i in range(3):
        for j in range(3):
            one = two = None
            for k in range(3):
                x = times(a[i][k], b[k][j])
                y = times(c[i][k], d[k][j])
                one = x if one is None else (one[0] + x[0], one[1] + x[1])
                two = y if two is None else (two[0] + y[0], two[1] + y[1])
            term = one[0] * two[0] + one[1] * two[1]
            total = term if total is None else total + term
    return total


def units_kernel(links_ref, out_ref, taken, sem):
    def copy_in(step):
        return pltpu.make_async_copy(
            links_ref.at[step // 2, pl.ds(0, 2), :, :, step % 2], taken.at[step], sem.at[step]
        )

    for step in range(6):
        copy_in(step).start()

    def one(step, carry):
        part = step // 4
        z = step % 4

        @pl.when(z == 0)
        def _():
            copy_in(part).wait()

        for h in range(2):
            at = pl.ds(8 * h, 8)
            parts = pairs([taken[part, r, c, i, z, at, :] for r, c, i in ENTRIES])
            for c, value in enumerate(flat_rows(unit_rows(parts[:3], parts[3:]))):
                out_ref[part // 2, c, part % 2, z, at, :] = value
        return carry

    lax.fori_loop(0, 24, one, 0)


def units(links):
    return pl.pallas_call(
        units_kernel,
        in_specs=[pl.BlockSpec(memory_space=pltpu.HBM)],
        out_specs=pl.BlockSpec(memory_space=pltpu.VMEM),
        out_shape=pltpu.VMEM((3, 18, 2, 4, 16, 128), jnp.float32),
        scratch_shapes=[
            pltpu.VMEM((6, 2, 3, 2, 4, 16, 128), jnp.float32),
            pltpu.SemaphoreType.DMA((6,)),
        ],
        compiler_params=pltpu.CompilerParams(vmem_limit_bytes=VMEM_LIMIT),
    )(links)


def plaquette_kernel(unit, x_ref, y_ref, z_ref, out_ref, sum_ref, x_edge, y_edge, z_edge):
    lane = lax.broadcasted_iota(jnp.int32, (8, 128), 1)
    sub = lax.broadcasted_iota(jnp.int32, (8, 128), 0)

    def above(step, carry):
        m = step // 2
        t = step % 2
        for h in range(2):
            at = pl.ds(8 * h, 8)
            parts = pairs([z_ref[m, r, c, i, t, at, :] for r, c, i in ENTRIES])
            for c, value in enumerate(flat_rows(unit_rows(parts[:3], parts[3:]))):
                z_edge[m, c, t, at, :] = value
        return carry

    lax.fori_loop(0, 4, above, 0)
    for m in range(2):
        for c, value in enumerate(flat_rows(from_parameters([y_ref[m, p] for p in range(8)]))):
            for k in range(8):
                y_edge[m, c, k, pl.ds(0, 1), :] = value[k : k + 1]
        parts = []
        for e in range(12):
            n = 12 * m + e
            value = x_ref[n // 8]
            parts.append(pltpu.roll(value, 128 - 16 * (n % 8), 1) if n % 8 else value)
        parts = pairs(parts)
        for c, value in enumerate(flat_rows(unit_rows(parts[:3], parts[3:]))):
            x_edge[m, c] = value

    def matrix(parts):
        parts = pairs(parts)
        return [parts[3 * i : 3 * i + 3] for i in range(3)]

    def site(t, z, inner):
        k = 4 * t + z
        total = None
        for h in range(2):
            at = pl.ds(8 * h, 8)

            def here(m):
                return matrix([unit[m, c, t, z, at, :] for c in range(18)])

            def next_x(m):
                got = []
                for c in range(18):
                    value = pltpu.roll(unit[m, c, t, z, at, :], 127, 1)
                    beyond = pltpu.roll(x_edge[m - 1, c], 127 - 2 * k - h, 1)
                    got.append(jnp.where(lane == 127, beyond, value))
                return matrix(got)

            def next_y(m):
                if h == 0:
                    return matrix([unit[m, c, t, z, pl.ds(1, 8), :] for c in range(18)])
                got = []
                for c in range(18):
                    value = jnp.where(sub == 0, y_edge[m // 2, c, k], unit[m, c, t, z, at, :])
                    got.append(pltpu.roll(value, 7, 0))
                return matrix(got)

            def next_z(m):
                if inner:
                    return matrix([unit[m, c, t, z + 1, at, :] for c in range(18)])
                return matrix([z_edge[m, c, t, at, :] for c in range(18)])

            value = product_trace(here(0), next_x(1), here(1), next_y(0))
            value = value + product_trace(here(0), next_x(2), here(2), next_z(0))
            value = value + product_trace(here(1), next_y(2), here(2), next_z(1))
            value = value * (1.0 / 9.0)
            out_ref[t, z, at, :] = value
            total = value if total is None else total + value
        return total

    total = jnp.zeros((8, 128), jnp.float32)
    total = lax.fori_loop(0, 6, lambda step, so_far: so_far + site(step // 3, step % 3, True), total)
    total = lax.fori_loop(0, 2, lambda t, so_far: so_far + site(t, 3, False), total)
    sum_ref[...] = jnp.broadcast_to(jnp.sum(total, keepdims=True), (8, 128))


def plaquettes(unit, x_face, y_face, z_face):
    return pl.pallas_call(
        plaquette_kernel,
        in_specs=[pl.BlockSpec(memory_space=pltpu.VMEM)] * 4,
        out_shape=[
            jax.ShapeDtypeStruct((2, 4, 16, 128), jnp.float32),
            jax.ShapeDtypeStruct((8, 128), jnp.float32),
        ],
        scratch_shapes=[
            pltpu.VMEM((2, 18, 8, 128), jnp.float32),
            pltpu.VMEM((2, 18, 8, 8, 128), jnp.float32),
            pltpu.VMEM((2, 18, 2, 16, 128), jnp.float32),
        ],
        compiler_params=pltpu.CompilerParams(vmem_limit_bytes=VMEM_LIMIT),
    )(unit, x_face, y_face, z_face)


def decode_kernel(bounds_ref, own_ref, out_ref):
    w = lax.axis_index("zt")
    top, bottom = moving_times(bounds_ref, w)
    own = own_ref.reshape(16 * 48, 128)

    def put(t, z, slot, h):
        at = h * 384 + slot * 8
        j = z + 4 * w - bounds_ref[t, w]
        values = [own[pl.ds(at + p, 8, stride=48), :] for p in range(8)]
        for c, value in enumerate(flat_rows(from_parameters(values))):
            out_ref[c, t, j, pl.ds(8 * h, 8), :] = value

    for h in range(2):
        put(1 - top, 3, 5 - top, h)
        put(1 - bottom, 0, 2 - 2 * bottom, h)
        for t in range(2):
            put(t, 1, 2 * t + 1, h)
    for t in range(2):
        depth = bounds_ref[t, w + 1] - bounds_ref[t, w]
        for j in range(2, 6):

            @pl.when(j >= depth)
            def _(t=t, j=j):
                out_ref[:, t, j] = jnp.zeros((18, 16, 128), jnp.float32)


def decoded(bounds, own):
    return pl.pallas_call(
        decode_kernel,
        grid=(4,),
        in_specs=[
            pl.BlockSpec(memory_space=pltpu.SMEM),
            pl.BlockSpec((16, 1, 48, 128), lambda m: (0, m, 0, 0)),
        ],
        out_specs=pl.BlockSpec((18, 2, 6, 16, 128), lambda m: (m, 0, 0, 0, 0)),
        out_shape=jax.ShapeDtypeStruct((72, 2, 6, 16, 128), jnp.float32),
        compiler_params=pltpu.CompilerParams(vmem_limit_bytes=VMEM_LIMIT),
    )(bounds, own)


def cut_kernel(bounds_ref, own_ref, top_ref, bottom_ref):
    top, bottom = moving_times(bounds_ref, lax.axis_index("zt"))
    for m in range(4):
        top_ref[:, m] = own_ref[:, m, pl.ds(pl.multiple_of(32 + 8 * top, 8), 8), :]
        bottom_ref[:, m] = own_ref[:, m, pl.ds(pl.multiple_of(16 * bottom, 8), 8), :]


def cut_planes(bounds, own):
    return pl.pallas_call(
        cut_kernel,
        in_specs=[pl.BlockSpec(memory_space=pltpu.SMEM), pl.BlockSpec(memory_space=pltpu.VMEM)],
        out_shape=[jax.ShapeDtypeStruct((16, 4, 8, 128), jnp.float32)] * 2,
        compiler_params=pltpu.CompilerParams(vmem_limit_bytes=VMEM_LIMIT),
    )(bounds, own)


def put_planes(rows, stride, block, places, out_ref, planes, sem):
    def copy_out(part, m):
        t, j = places[part]
        return pltpu.make_async_copy(planes.at[part, m], out_ref.at[pl.ds(18 * m, 18), t, j], sem.at[part, m])

    def one(m, carry):
        for part in range(2):
            for h in range(2):
                at = h * 8 * stride + m * block + part * (block - 8)
                values = [rows[part][pl.ds(at + p, 8, stride=stride), :] for p in range(8)]
                for c, value in enumerate(flat_rows(from_parameters(values))):
                    planes[part, m, c, pl.ds(8 * h, 8), :] = value
            copy_out(part, m).start()
        return carry

    lax.fori_loop(0, 4, one, 0)
    for m in range(4):
        for part in range(2):
            copy_out(part, m).wait()


PLANE_SCRATCH = [pltpu.VMEM((2, 4, 18, 16, 128), jnp.float32), pltpu.SemaphoreType.DMA((2, 4))]


def ends_kernel(bounds_ref, below_ref, above_ref, bottom_ref, top_ref, whole_ref, out_ref, ends, planes, sem):
    w = lax.axis_index("zt")
    top, bottom = moving_times(bounds_ref, w)
    first, last = w == 0, w == 7

    def taken(part, source_ref):
        ends[part] = source_ref[...]

    pl.when(first)(lambda: taken(0, bottom_ref))
    pl.when(jnp.logical_not(first))(lambda: taken(0, below_ref))
    pl.when(last)(lambda: taken(1, top_ref))
    pl.when(jnp.logical_not(last))(lambda: taken(1, above_ref))
    low_time = jnp.where(first, bottom, 1 - bottom)
    high_time = jnp.where(last, top, 1 - top)
    high_at = jnp.where(last, 3, 4) + 4 * w - bounds_ref[high_time, w]
    rows = [ends.at[part].reshape(16 * 32, 128) for part in range(2)]
    put_planes(rows, 32, 8, ((low_time, 0), (high_time, high_at)), out_ref, planes, sem)


def with_ends(bounds, below, above, bottom, top, whole):
    return pl.pallas_call(
        ends_kernel,
        in_specs=[pl.BlockSpec(memory_space=pltpu.SMEM)]
        + [pl.BlockSpec(memory_space=pltpu.VMEM)] * 4
        + [pl.BlockSpec(memory_space=pltpu.HBM)],
        out_specs=pl.BlockSpec(memory_space=pltpu.HBM),
        out_shape=jax.ShapeDtypeStruct((72, 2, 6, 16, 128), jnp.float32),
        input_output_aliases={5: 0},
        scratch_shapes=[pltpu.VMEM((2, 16, 4, 8, 128), jnp.float32)] + PLANE_SCRATCH,
        compiler_params=pltpu.CompilerParams(vmem_limit_bytes=VMEM_LIMIT),
    )(bounds, below, above, bottom, top, whole)


def rest_kernel(count, bounds_ref, own_ref, whole_ref, out_ref, mean_ref, planes, sem):
    w = lax.axis_index("zt")
    rows = own_ref.reshape(16 * 72, 128)
    places = [(t, 2 + 4 * w - bounds_ref[t, w]) for t in range(2)]
    put_planes([rows, rows], 72, 16, places, out_ref, planes, sem)
    total = own_ref[0, pl.ds(64, 8), :]
    for n in range(1, 16):
        total = total + own_ref[n, pl.ds(64, 8), :]
    mean_ref[0, 0] = jnp.max(total) * (1.0 / count)


def with_rest(bounds, own, whole, count):
    return pl.pallas_call(
        lambda *refs: rest_kernel(count, *refs),
        in_specs=[
            pl.BlockSpec(memory_space=pltpu.SMEM),
            pl.BlockSpec(memory_space=pltpu.VMEM),
            pl.BlockSpec(memory_space=pltpu.HBM),
        ],
        out_specs=[pl.BlockSpec(memory_space=pltpu.HBM), pl.BlockSpec(memory_space=pltpu.SMEM)],
        out_shape=[
            jax.ShapeDtypeStruct((72, 2, 6, 16, 128), jnp.float32),
            jax.ShapeDtypeStruct((1, 1), jnp.float32),
        ],
        input_output_aliases={2: 0},
        scratch_shapes=PLANE_SCRATCH,
        compiler_params=pltpu.CompilerParams(vmem_limit_bytes=VMEM_LIMIT),
    )(bounds, own, whole)


def summed(value, steps):
    for axis, by in steps:
        count = lax.axis_size(axis)
        value = value + lax.ppermute(value, axis, [(i, i ^ by) for i in range(count)])
    return value


def spread(payload):
    return lax.all_to_all(payload, ("gy", "gx"), split_axis=0, concat_axis=0, tiled=True)


def local(links, bounds):
    held = pltpu.with_memory_space_constraint(links, pltpu.HBM)
    x_face, y_face, z_face = faces(held)
    x_face, y_face, z_face, links = lax.optimization_barrier((x_face, y_face, z_face, links))
    y_face = passed_along(y_face, "gy", -1)
    x_face = passed_along(x_face, "gx", -1)
    held = pltpu.with_memory_space_constraint(links, pltpu.HBM)
    payload = encoded(held)
    payload, links, x_face, y_face, z_face = lax.optimization_barrier((payload, links, x_face, y_face, z_face))
    moved = spread(payload)
    z_face = passed_along(z_face, "zt", -1)
    held = pltpu.with_memory_space_constraint(links, pltpu.HBM)
    plaquette, total = plaquettes(units(held), x_face, y_face, z_face)
    total = summed(total, (("zt", 1), ("zt", 2), ("zt", 6)))
    rest = encoded_rest(held, total)
    moved, rest = lax.optimization_barrier((moved, rest))
    moved_rest = spread(rest)
    top_plane, bottom_plane = cut_planes(bounds, moved)
    below = passed_along(top_plane, "zt", 1)
    above = passed_along(bottom_plane, "zt", -1)
    file_links = decoded(bounds, moved)
    file_links = with_ends(bounds, below, above, bottom_plane, top_plane, file_links)
    file_links, mean = with_rest(bounds, moved_rest, file_links, plaquette.size * 128)
    return file_links.reshape(4, 3, 3, 2, 2, 6, 4, 1, 4, 1, 128), plaquette, mean[0, 0]


def solution(mesh):
    in_specs = (P(None, None, None, None, None, "zt", "gy", "gx"), P())
    out_specs = (
        P(None, None, None, None, None, "zt", None, "gx", None, "gy", None),
        P(None, "zt", "gy", "gx"),
        P(),
    )
    return jax.shard_map(local, mesh=mesh, in_specs=in_specs, out_specs=out_specs, check_vma=False)
```

```python
import jax
import jax.numpy as jnp
from jax import lax
from jax.experimental import pallas as pl
from jax.experimental.pallas import tpu as pltpu
from jax.sharding import PartitionSpec as P

VMEM_LIMIT = 24 * 1024 * 1024
CROSS = ((1, 2), (2, 0), (0, 1))


def passed_along(value, axis, by):
    count = lax.axis_size(axis)
    return lax.ppermute(value, axis, [(i, (i + by) % count) for i in range(count)])


def times(a, b):
    return (a[0] * b[0] - a[1] * b[1], a[0] * b[1] + a[1] * b[0])


def times_conj(a, b):
    return (a[0] * b[0] + a[1] * b[1], a[1] * b[0] - a[0] * b[1])


def minus(a, b):
    return (a[0] - b[0], a[1] - b[1])


def scaled(a, s):
    return (a[0] * s, a[1] * s)


def square(a):
    return a[0] * a[0] + a[1] * a[1]


def last_row(u, v):
    rows = []
    for b, c in CROSS:
        x = minus(times(u[b], v[c]), times(u[c], v[b]))
        rows.append((x[0], -x[1]))
    return rows


def unit_rows(r1, r2):
    n = lax.rsqrt(square(r1[0]) + square(r1[1]) + square(r1[2]))
    u = [scaled(x, n) for x in r1]
    terms = [times_conj(y, x) for x, y in zip(u, r2)]
    c = (terms[0][0] + terms[1][0] + terms[2][0], terms[0][1] + terms[1][1] + terms[2][1])
    v = [minus(y, times(c, x)) for x, y in zip(u, r2)]
    n = lax.rsqrt(square(v[0]) + square(v[1]) + square(v[2]))
    v = [scaled(x, n) for x in v]
    return [u, v, last_row(u, v)]


def angle_value(a):
    t = a[1] / (jnp.abs(a[0]) + jnp.abs(a[1]))
    return jnp.where(a[0] < 0.0, 2.0 - t, t)


def angle_phase(t):
    back = t > 1.0
    y = jnp.where(back, 2.0 - t, t)
    x = 1.0 - jnp.abs(y)
    x = jnp.where(back, -x, x)
    n = lax.rsqrt(x * x + y * y)
    return (x * n, y * n)


def to_parameters(r1, r2):
    inverse = 1.0 / square(r1[0])
    p1 = scaled(times_conj(r1[1], r1[0]), inverse)
    p2 = scaled(times_conj(r1[2], r1[0]), inverse)
    s1 = minus(r2[1], times(r2[0], p1))
    s2 = minus(r2[2], times(r2[0], p2))
    q = scaled(times_conj(s2, s1), 1.0 / square(s1))
    return [p1[0], p1[1], p2[0], p2[1], q[0], q[1], angle_value(r1[0]), angle_value(s1)]


def from_parameters(values):
    p1 = (values[0], values[1])
    p2 = (values[2], values[3])
    q = (values[4], values[5])
    n2 = 1.0 / (1.0 + square(p1) + square(p2))
    a = scaled(angle_phase(values[6]), jnp.sqrt(n2))
    u = [a, times(a, p1), times(a, p2)]
    g = times_conj(q, p2)
    g = ((g[0] + p1[0]) * n2, (g[1] - p1[1]) * n2)
    gp1 = times(g, p1)
    gp2 = times(g, p2)
    v = [(-g[0], -g[1]), (1.0 - gp1[0], -gp1[1]), minus(q, gp2)]
    n = lax.rsqrt(square(v[0]) + square(v[1]) + square(v[2]))
    b = scaled(angle_phase(values[7]), n)
    v = [times(b, x) for x in v]
    return [u, v, last_row(u, v)]


ENTRIES = [(r, c, i) for r in range(2) for c in range(3) for i in range(2)]


def pairs(parts):
    return [(parts[2 * i], parts[2 * i + 1]) for i in range(len(parts) // 2)]


def moving_times(bounds_ref, w):
    top = jnp.where(bounds_ref[0, w + 1] < 4 * w + 4, 0, 1)
    bottom = jnp.where(bounds_ref[0, w] > 4 * w, 0, 1)
    return top, bottom


def turned(x, lane):
    odd = (lane & 32) != 0
    far = (lane & 64) != 0
    x = [jnp.where(odd, x[(d + 1) % 4], x[d]) for d in range(4)]
    x = [jnp.where(far, x[(d + 2) % 4], x[d]) for d in range(4)]
    x = [pltpu.roll(x[d], 32 * d, 1) if d else x[d] for d in range(4)]
    x = [jnp.where(odd, x[(1 - g) % 4], x[-g % 4]) for g in range(4)]
    return [jnp.where(far, x[(g + 2) % 4], x[g]) for g in range(4)]


def encode_planes(rows, out, stride):
    lane = lax.broadcasted_iota(jnp.int32, (8, 128), 1)
    low = lax.broadcasted_iota(jnp.int32, (8, 128), 0) < 4
    by_row = []
    for r in range(4):
        parts = pairs([rows[pl.ds(c * 32 + r, 8, stride=4), :] for c in range(12)])
        by_row.append(to_parameters(parts[:3], parts[3:]))
    for p in range(8):
        z = turned([by_row[r][p] for r in range(4)], lane)
        for h in (0, 1):
            first = jnp.where(low, z[2 * h], pltpu.roll(z[2 * h + 1], 4, 0))
            second = jnp.where(low, pltpu.roll(z[2 * h], 4, 0), z[2 * h + 1])
            out[pl.ds(h * 8 * stride + p, 8, stride=stride), :] = first
            out[pl.ds(h * 8 * stride + 8 + p, 8, stride=stride), :] = second


def encode_kernel(taken, out_ref, given, out_sem):
    def copy_out(step):
        at = pl.ds(pl.multiple_of((step % 3) * 16, 16), 16)
        return pltpu.make_async_copy(given.at[step], out_ref.at[:, step // 3, at], out_sem.at[step])

    def one(step, carry):
        encode_planes(taken.at[step].reshape(12 * 32, 128), given.at[step].reshape(16 * 16, 128), 16)
        copy_out(step).start()
        return carry

    lax.fori_loop(0, 12, one, 0)
    for step in range(12):
        copy_out(step).wait()


def encoded(taken):
    return pl.pallas_call(
        encode_kernel,
        in_specs=[pl.BlockSpec(memory_space=pltpu.VMEM)],
        out_specs=pl.BlockSpec(memory_space=pltpu.HBM),
        out_shape=pltpu.HBM((16, 4, 48, 128), jnp.float32),
        scratch_shapes=[pltpu.VMEM((12, 16, 16, 128), jnp.float32), pltpu.SemaphoreType.DMA((12,))],
        compiler_params=pltpu.CompilerParams(vmem_limit_bytes=VMEM_LIMIT),
    )(taken)


class ShiftedRows:
    def __init__(self, ref, by):
        self.ref = ref
        self.by = by

    def __setitem__(self, at, value):
        self.ref[pl.ds(self.by + at[0].start, at[0].size, stride=at[0].stride), :] = value


def encode_rest_kernel(rest, total_ref, out_ref, given, out_sem):
    out = given.reshape(16 * 72, 128)
    for n in range(16):
        given[n, pl.ds(64, 8), :] = total_ref[...]

    def copy_out(m, size):
        at = pl.ds(pl.multiple_of(m * 16, 8), size)
        return pltpu.make_async_copy(given.at[:, at], out_ref.at[:, at], out_sem.at[m])

    copy_out(4, 8).start()

    def one(m, carry):
        encode_planes(rest.at[m].reshape(12 * 32, 128), ShiftedRows(out, m * 16), 72)
        copy_out(m, 16).start()
        return carry

    lax.fori_loop(0, 4, one, 0)
    for m in range(4):
        copy_out(m, 16).wait()
    copy_out(4, 8).wait()


def encoded_rest(rest, total):
    return pl.pallas_call(
        encode_rest_kernel,
        in_specs=[pl.BlockSpec(memory_space=pltpu.VMEM)] * 2,
        out_specs=pl.BlockSpec(memory_space=pltpu.HBM),
        out_shape=pltpu.HBM((16, 72, 128), jnp.float32),
        scratch_shapes=[pltpu.VMEM((16, 72, 128), jnp.float32), pltpu.SemaphoreType.DMA((5,))],
        compiler_params=pltpu.CompilerParams(vmem_limit_bytes=VMEM_LIMIT),
    )(rest, total)


def take_kernel(links_ref, x_ref, y_ref, z_ref, taken, rest, in_sem, rest_sem, z_sem):
    def copy_in(m, pair):
        if pair == 2:
            source = links_ref.at[m, pl.ds(0, 2), :, :, :, 3]
        else:
            source = links_ref.at[m, pl.ds(0, 2), :, :, pair, pl.ds(0, 2)]
        return pltpu.make_async_copy(source, taken.at[3 * m + pair], in_sem.at[3 * m + pair])

    def copy_rest(m):
        return pltpu.make_async_copy(links_ref.at[m, pl.ds(0, 2), :, :, :, 2], rest.at[m], rest_sem.at[m])

    def copies(m):
        return [copy_in(m, pair) for pair in range(3)] + [copy_rest(m)]

    copy_z = pltpu.make_async_copy(links_ref.at[pl.ds(0, 2), pl.ds(0, 2), :, :, :, 0], z_ref, z_sem)
    order = (2, 1, 0, 3)
    for m in order:
        for copy in copies(m):
            copy.start()
    copy_z.start()

    def rows(m, r, c, i, k, start, size):
        t, z = k // 4, k % 4
        at = pl.ds(start, size)
        if z == 2:
            return rest[m, r, c, i, t, at, :]
        if z == 3:
            return taken[3 * m + 2, r, c, i, t, at, :]
        return taken[3 * m + t, r, c, i, z, at, :]

    def row_face(m):
        parts = pairs([jnp.concatenate([rows(m, *e, k, 0, 1) for k in range(8)], axis=0) for e in ENTRIES])
        for p, value in enumerate(to_parameters(parts[:3], parts[3:])):
            y_ref[m // 2, p] = value

    lane = lax.broadcasted_iota(jnp.int32, (8, 128), 1)
    got = [None] * 3

    def column_face(m):
        for e, entry in enumerate(ENTRIES):
            n = 12 * (m - 1) + e
            for k in range(8):
                for h in range(2):
                    at = 16 * (n % 8) + 2 * k + h
                    value = rows(m, *entry, k, 8 * h, 8)
                    value = pltpu.roll(value, at, 1) if at else value
                    got[n // 8] = value if got[n // 8] is None else jnp.where(lane == at, value, got[n // 8])

    for m in order:
        for copy in copies(m):
            copy.wait()
        if m in (1, 2):
            column_face(m)
        if m in (0, 2):
            row_face(m)
    for n in range(3):
        x_ref[n] = got[n]
    copy_z.wait()


def taken_links(links):
    kept = pl.BlockSpec(memory_space=pltpu.VMEM)
    return pl.pallas_call(
        take_kernel,
        in_specs=[pl.BlockSpec(memory_space=pltpu.HBM)],
        out_specs=[kept] * 5,
        out_shape=[
            pltpu.VMEM((3, 8, 128), jnp.float32),
            pltpu.VMEM((2, 8, 8, 128), jnp.float32),
            pltpu.VMEM((2, 2, 3, 2, 2, 16, 128), jnp.float32),
            pltpu.VMEM((12, 2, 3, 2, 2, 16, 128), jnp.float32),
            pltpu.VMEM((4, 2, 3, 2, 2, 16, 128), jnp.float32),
        ],
        scratch_shapes=[
            pltpu.SemaphoreType.DMA((12,)),
            pltpu.SemaphoreType.DMA((4,)),
            pltpu.SemaphoreType.DMA,
        ],
        compiler_params=pltpu.CompilerParams(vmem_limit_bytes=VMEM_LIMIT),
    )(links)


def flat_rows(matrix):
    return [part for row in matrix for entry in row for part in entry]


def product_trace(a, b, c, d):
    total = None
    for i in range(3):
        for j in range(3):
            one = two = None
            for k in range(3):
                x = times(a[i][k], b[k][j])
                y = times(c[i][k], d[k][j])
                one = x if one is None else (one[0] + x[0], one[1] + x[1])
                two = y if two is None else (two[0] + y[0], two[1] + y[1])
            term = one[0] * two[0] + one[1] * two[1]
            total = term if total is None else total + term
    return total


class Sites:
    def __init__(self, unit, x_edge, y_edge, z_edge, out_ref):
        self.unit, self.x_edge, self.y_edge, self.z_edge = unit, x_edge, y_edge, z_edge
        self.out_ref = out_ref
        self.last_lane = lax.broadcasted_iota(jnp.int32, (8, 128), 1) == 127
        self.first_row = lax.broadcasted_iota(jnp.int32, (8, 128), 0) == 0

    def matrix(self, parts):
        parts = pairs(parts)
        return [parts[3 * i : 3 * i + 3] for i in range(3)]

    def here(self, m, t, z, h):
        return self.matrix([self.unit[m, c, t, z, pl.ds(8 * h, 8), :] for c in range(18)])

    def next_x(self, m, t, z, h):
        got = []
        for c in range(18):
            value = pltpu.roll(self.unit[m, c, t, z, pl.ds(8 * h, 8), :], 127, 1)
            beyond = pltpu.roll(self.x_edge[m - 1, c], 127 - 2 * (4 * t + z) - h, 1)
            got.append(jnp.where(self.last_lane, beyond, value))
        return self.matrix(got)

    def next_y(self, m, t, z, h):
        if h == 0:
            return self.matrix([self.unit[m, c, t, z, pl.ds(1, 8), :] for c in range(18)])
        got = []
        for c in range(18):
            value = self.unit[m, c, t, z, pl.ds(8, 8), :]
            value = jnp.where(self.first_row, self.y_edge[m // 2, c, 4 * t + z], value)
            got.append(pltpu.roll(value, 7, 0))
        return self.matrix(got)

    def next_z(self, m, t, z, h):
        if self.z_edge is None:
            return self.here(m, t, z + 1, h)
        return self.matrix([self.z_edge[m, c, t, pl.ds(8 * h, 8), :] for c in range(18)])

    def plane(self, t, z):
        total = None
        for h in range(2):
            at = (t, z, h)
            value = product_trace(self.here(0, *at), self.next_x(1, *at), self.here(1, *at), self.next_y(0, *at))
            value = value + product_trace(
                self.here(0, *at), self.next_x(2, *at), self.here(2, *at), self.next_z(0, *at)
            )
            value = value + product_trace(
                self.here(1, *at), self.next_y(2, *at), self.here(2, *at), self.next_z(1, *at)
            )
            value = value * (1.0 / 9.0)
            self.out_ref[t, z, pl.ds(8 * h, 8), :] = value
            total = value if total is None else total + value
        return total


def inner_kernel(links_ref, x_ref, y_ref, out_ref, sum_ref, unit, x_edge, y_edge, taken, sem):
    def copy_in(step):
        return pltpu.make_async_copy(
            links_ref.at[step // 2, pl.ds(0, 2), :, :, step % 2], taken.at[step], sem.at[step]
        )

    for step in range(6):
        copy_in(step).start()
    for m in range(2):
        for c, value in enumerate(flat_rows(from_parameters([y_ref[m, p] for p in range(8)]))):
            for k in range(8):
                y_edge[m, c, k, pl.ds(0, 1), :] = value[k : k + 1]
        parts = []
        for e in range(12):
            n = 12 * m + e
            value = x_ref[n // 8]
            parts.append(pltpu.roll(value, 128 - 16 * (n % 8), 1) if n % 8 else value)
        parts = pairs(parts)
        for c, value in enumerate(flat_rows(unit_rows(parts[:3], parts[3:]))):
            x_edge[m, c] = value

    def own(step, carry):
        part = step // 4
        z = step % 4

        @pl.when(z == 0)
        def _():
            copy_in(part).wait()

        for h in range(2):
            at = pl.ds(8 * h, 8)
            parts = pairs([taken[part, r, c, i, z, at, :] for r, c, i in ENTRIES])
            for c, value in enumerate(flat_rows(unit_rows(parts[:3], parts[3:]))):
                unit[part // 2, c, part % 2, z, at, :] = value
        return carry

    lax.fori_loop(0, 24, own, 0)
    sites = Sites(unit, x_edge, y_edge, None, out_ref)
    zero = jnp.zeros((8, 128), jnp.float32)
    sum_ref[...] = lax.fori_loop(0, 6, lambda step, total: total + sites.plane(step // 3, step % 3), zero)


def inner_plaquettes(links, x_face, y_face):
    kept = pl.BlockSpec(memory_space=pltpu.VMEM)
    return pl.pallas_call(
        inner_kernel,
        in_specs=[pl.BlockSpec(memory_space=pltpu.HBM)] + [kept] * 2,
        out_specs=[kept] * 5,
        out_shape=[
            pltpu.VMEM((2, 4, 16, 128), jnp.float32),
            pltpu.VMEM((8, 128), jnp.float32),
            pltpu.VMEM((3, 18, 2, 4, 16, 128), jnp.float32),
            pltpu.VMEM((2, 18, 8, 128), jnp.float32),
            pltpu.VMEM((2, 18, 8, 8, 128), jnp.float32),
        ],
        scratch_shapes=[
            pltpu.VMEM((6, 2, 3, 2, 4, 16, 128), jnp.float32),
            pltpu.SemaphoreType.DMA((6,)),
        ],
        compiler_params=pltpu.CompilerParams(vmem_limit_bytes=VMEM_LIMIT),
    )(links, x_face, y_face)


def outer_kernel(inner_ref, part_ref, unit, x_edge, y_edge, z_ref, out_ref, sum_ref, z_edge):
    for t in range(2):
        for z in range(3):
            out_ref[t, z] = inner_ref[t, z]

    def above(step, carry):
        m = step // 2
        t = step % 2
        for h in range(2):
            at = pl.ds(8 * h, 8)
            parts = pairs([z_ref[m, r, c, i, t, at, :] for r, c, i in ENTRIES])
            for c, value in enumerate(flat_rows(unit_rows(parts[:3], parts[3:]))):
                z_edge[m, c, t, at, :] = value
        return carry

    lax.fori_loop(0, 4, above, 0)
    sites = Sites(unit, x_edge, y_edge, z_edge, out_ref)
    total = lax.fori_loop(0, 2, lambda t, total: total + sites.plane(t, 3), part_ref[...])
    sum_ref[...] = jnp.broadcast_to(jnp.sum(total, keepdims=True), (8, 128))


def outer_plaquettes(inner, part, unit, x_edge, y_edge, z_face):
    kept = pl.BlockSpec(memory_space=pltpu.VMEM)
    return pl.pallas_call(
        outer_kernel,
        in_specs=[kept] * 6,
        out_shape=[
            jax.ShapeDtypeStruct((2, 4, 16, 128), jnp.float32),
            jax.ShapeDtypeStruct((8, 128), jnp.float32),
        ],
        scratch_shapes=[pltpu.VMEM((2, 18, 2, 16, 128), jnp.float32)],
        compiler_params=pltpu.CompilerParams(vmem_limit_bytes=VMEM_LIMIT),
    )(inner, part, unit, x_edge, y_edge, z_face)


def put_planes(sources, places, out_ref, planes, sem):
    def copy_out(part, m):
        t, j = places[part]
        return pltpu.make_async_copy(planes.at[part, m], out_ref.at[pl.ds(18 * m, 18), t, j], sem.at[part, m])

    def one(m, carry):
        for part, (rows, stride, start, step) in enumerate(sources):
            for h in range(2):
                at = h * 8 * stride + start + m * step
                values = [rows[pl.ds(at + p, 8, stride=stride), :] for p in range(8)]
                for c, value in enumerate(flat_rows(from_parameters(values))):
                    planes[part, m, c, pl.ds(8 * h, 8), :] = value
            copy_out(part, m).start()
        return carry

    lax.fori_loop(0, 4, one, 0)
    for m in range(4):
        for part in range(len(sources)):
            copy_out(part, m).wait()


PLANE_SCRATCH = [pltpu.VMEM((4, 4, 18, 16, 128), jnp.float32), pltpu.SemaphoreType.DMA((4, 4))]


def decode_kernel(bounds_ref, own_ref, out_ref, planes, sem, zeros, zero_sem):
    w = lax.axis_index("zt")
    top, bottom = moving_times(bounds_ref, w)
    zeros[...] = jnp.zeros((18, 16, 128), jnp.float32)

    def fill(t, j, m):
        return pltpu.make_async_copy(zeros, out_ref.at[pl.ds(18 * m, 18), t, j], zero_sem.at[t, j - 2])

    def every_empty(act):
        for t in range(2):
            depth = bounds_ref[t, w + 1] - bounds_ref[t, w]
            for j in range(2, 6):

                @pl.when(j >= depth)
                def _(t=t, j=j):
                    for m in range(4):
                        act(fill(t, j, m))

    every_empty(lambda copy: copy.start())
    rows = own_ref.reshape(16 * 192, 128)
    planes_in = ((1 - top, 3, 5 - top), (1 - bottom, 0, 2 - 2 * bottom), (0, 1, 1), (1, 1, 3))
    sources = [(rows, 192, 8 * slot, 48) for t, z, slot in planes_in]
    places = [(t, z + 4 * w - bounds_ref[t, w]) for t, z, slot in planes_in]
    put_planes(sources, places, out_ref, planes, sem)
    every_empty(lambda copy: copy.wait())


def decoded(bounds, own):
    return pl.pallas_call(
        decode_kernel,
        in_specs=[pl.BlockSpec(memory_space=pltpu.SMEM), pl.BlockSpec(memory_space=pltpu.VMEM)],
        out_specs=pl.BlockSpec(memory_space=pltpu.HBM),
        out_shape=jax.ShapeDtypeStruct((72, 2, 6, 16, 128), jnp.float32),
        scratch_shapes=PLANE_SCRATCH
        + [pltpu.VMEM((18, 16, 128), jnp.float32), pltpu.SemaphoreType.DMA((2, 4))],
        compiler_params=pltpu.CompilerParams(vmem_limit_bytes=VMEM_LIMIT),
    )(bounds, own)


def cut_kernel(bounds_ref, own_ref, first_ref, second_ref):
    w = lax.axis_index("zt")
    top, bottom = moving_times(bounds_ref, w)
    even = w % 2 == 0
    top = 32 + 8 * top
    bottom = 16 * bottom
    first = pl.multiple_of(jnp.where(even, top, bottom), 8)
    second = pl.multiple_of(jnp.where(even, bottom, top), 8)
    for m in range(4):
        first_ref[:, m] = own_ref[:, m, pl.ds(first, 8), :]
        second_ref[:, m] = own_ref[:, m, pl.ds(second, 8), :]


def cut_planes(bounds, own):
    return pl.pallas_call(
        cut_kernel,
        in_specs=[pl.BlockSpec(memory_space=pltpu.SMEM), pl.BlockSpec(memory_space=pltpu.VMEM)],
        out_shape=[jax.ShapeDtypeStruct((16, 4, 8, 128), jnp.float32)] * 2,
        compiler_params=pltpu.CompilerParams(vmem_limit_bytes=VMEM_LIMIT),
    )(bounds, own)


def rest_kernel(count, bounds_ref, first_ref, second_ref, rest_ref, whole_ref, out_ref, mean_ref, planes, sem):
    w = lax.axis_index("zt")
    top, bottom = moving_times(bounds_ref, w)
    even = w % 2 == 0
    low_time = jnp.where(w == 0, bottom, 1 - bottom)
    high_time = jnp.where(w == 7, top, 1 - top)
    high_at = jnp.where(w == 7, 3, 4) + 4 * w - bounds_ref[high_time, w]
    low_at = jnp.int32(0)
    rows = rest_ref.reshape(16 * 72, 128)
    sources = [(ref.reshape(16 * 32, 128), 32, 0, 8) for ref in (first_ref, second_ref)]
    sources += [(rows, 72, 8 * t, 16) for t in range(2)]
    places = [
        (jnp.where(even, high_time, low_time), jnp.where(even, high_at, low_at)),
        (jnp.where(even, low_time, high_time), jnp.where(even, low_at, high_at)),
    ]
    places += [(t, 2 + 4 * w - bounds_ref[t, w]) for t in range(2)]
    total = rest_ref[0, pl.ds(64, 8), :]
    for n in range(1, 16):
        total = total + rest_ref[n, pl.ds(64, 8), :]
    mean_ref[0, 0] = jnp.max(total) * (1.0 / count)
    put_planes(sources, places, out_ref, planes, sem)


def with_rest(bounds, first, second, rest, whole, count):
    kept = pl.BlockSpec(memory_space=pltpu.VMEM)
    return pl.pallas_call(
        lambda *refs: rest_kernel(count, *refs),
        in_specs=[pl.BlockSpec(memory_space=pltpu.SMEM)] + [kept] * 3 + [pl.BlockSpec(memory_space=pltpu.HBM)],
        out_specs=[pl.BlockSpec(memory_space=pltpu.HBM), pl.BlockSpec(memory_space=pltpu.SMEM)],
        out_shape=[
            jax.ShapeDtypeStruct((72, 2, 6, 16, 128), jnp.float32),
            jax.ShapeDtypeStruct((1, 1), jnp.float32),
        ],
        input_output_aliases={4: 0},
        scratch_shapes=PLANE_SCRATCH,
        compiler_params=pltpu.CompilerParams(vmem_limit_bytes=VMEM_LIMIT),
    )(bounds, first, second, rest, whole)


def summed(value, steps):
    for axis, by in steps:
        count = lax.axis_size(axis)
        value = value + lax.ppermute(value, axis, [(i, i ^ by) for i in range(count)])
    return value


def spread(payload):
    return lax.all_to_all(payload, ("gy", "gx"), split_axis=0, concat_axis=0, tiled=True)


def local(links, bounds):
    held = pltpu.with_memory_space_constraint(links, pltpu.HBM)
    x_face, y_face, z_face, taken, rest = taken_links(held)
    y_face = passed_along(y_face, "gy", -1)
    x_face = passed_along(x_face, "gx", -1)
    payload = encoded(taken)
    payload, links, x_face, y_face, z_face = lax.optimization_barrier((payload, links, x_face, y_face, z_face))
    moved = spread(payload)
    z_face = passed_along(z_face, "zt", -1)
    held = pltpu.with_memory_space_constraint(links, pltpu.HBM)
    plaquette, total = outer_plaquettes(*inner_plaquettes(held, x_face, y_face), z_face)
    total = summed(total, (("zt", 1), ("zt", 2), ("zt", 6)))
    rest = encoded_rest(rest, total)
    moved, rest = lax.optimization_barrier((moved, rest))
    moved_rest = spread(rest)
    first, second = cut_planes(bounds, moved)
    first = lax.ppermute(first, "zt", [(i, i ^ 1) for i in range(8)])
    second = lax.ppermute(second, "zt", [(0, 0), (7, 7)] + [(i, (i + 1 ^ 1) - 1) for i in range(1, 7)])
    file_links = decoded(bounds, moved)
    file_links, mean = with_rest(bounds, first, second, moved_rest, file_links, plaquette.size * 128)
    return file_links.reshape(4, 3, 3, 2, 2, 6, 4, 1, 4, 1, 128), plaquette, mean[0, 0]


def solution(mesh):
    in_specs = (P(None, None, None, None, None, "zt", "gy", "gx"), P())
    out_specs = (
        P(None, None, None, None, None, "zt", None, "gx", None, "gy", None),
        P(None, "zt", "gy", "gx"),
        P(),
    )
    return jax.shard_map(local, mesh=mesh, in_specs=in_specs, out_specs=out_specs, check_vma=False)
```

```python
import jax
import jax.numpy as jnp
from jax import lax
from jax.experimental import pallas as pl
from jax.experimental.pallas import tpu as pltpu
from jax.sharding import PartitionSpec as P

VMEM_LIMIT = 24 * 1024 * 1024
CROSS = ((1, 2), (2, 0), (0, 1))


def passed_along(value, axis, by):
    count = lax.axis_size(axis)
    return lax.ppermute(value, axis, [(i, (i + by) % count) for i in range(count)])


def times(a, b):
    return (a[0] * b[0] - a[1] * b[1], a[0] * b[1] + a[1] * b[0])


def times_conj(a, b):
    return (a[0] * b[0] + a[1] * b[1], a[1] * b[0] - a[0] * b[1])


def minus(a, b):
    return (a[0] - b[0], a[1] - b[1])


def scaled(a, s):
    return (a[0] * s, a[1] * s)


def square(a):
    return a[0] * a[0] + a[1] * a[1]


def last_row(u, v):
    rows = []
    for b, c in CROSS:
        x = minus(times(u[b], v[c]), times(u[c], v[b]))
        rows.append((x[0], -x[1]))
    return rows


def unit_rows(r1, r2):
    n = lax.rsqrt(square(r1[0]) + square(r1[1]) + square(r1[2]))
    u = [scaled(x, n) for x in r1]
    terms = [times_conj(y, x) for x, y in zip(u, r2)]
    c = (terms[0][0] + terms[1][0] + terms[2][0], terms[0][1] + terms[1][1] + terms[2][1])
    v = [minus(y, times(c, x)) for x, y in zip(u, r2)]
    n = lax.rsqrt(square(v[0]) + square(v[1]) + square(v[2]))
    v = [scaled(x, n) for x in v]
    return [u, v, last_row(u, v)]


def angle_value(a):
    t = a[1] / (jnp.abs(a[0]) + jnp.abs(a[1]))
    return jnp.where(a[0] < 0.0, 2.0 - t, t)


def angle_phase(t):
    back = t > 1.0
    y = jnp.where(back, 2.0 - t, t)
    x = 1.0 - jnp.abs(y)
    x = jnp.where(back, -x, x)
    n = lax.rsqrt(x * x + y * y)
    return (x * n, y * n)


def to_parameters(r1, r2):
    inverse = 1.0 / square(r1[0])
    p1 = scaled(times_conj(r1[1], r1[0]), inverse)
    p2 = scaled(times_conj(r1[2], r1[0]), inverse)
    s1 = minus(r2[1], times(r2[0], p1))
    s2 = minus(r2[2], times(r2[0], p2))
    q = scaled(times_conj(s2, s1), 1.0 / square(s1))
    return [p1[0], p1[1], p2[0], p2[1], q[0], q[1], angle_value(r1[0]), angle_value(s1)]


def from_parameters(values):
    p1 = (values[0], values[1])
    p2 = (values[2], values[3])
    q = (values[4], values[5])
    n2 = 1.0 / (1.0 + square(p1) + square(p2))
    a = scaled(angle_phase(values[6]), jnp.sqrt(n2))
    u = [a, times(a, p1), times(a, p2)]
    g = times_conj(q, p2)
    g = ((g[0] + p1[0]) * n2, (g[1] - p1[1]) * n2)
    gp1 = times(g, p1)
    gp2 = times(g, p2)
    v = [(-g[0], -g[1]), (1.0 - gp1[0], -gp1[1]), minus(q, gp2)]
    n = lax.rsqrt(square(v[0]) + square(v[1]) + square(v[2]))
    b = scaled(angle_phase(values[7]), n)
    v = [times(b, x) for x in v]
    return [u, v, last_row(u, v)]


ENTRIES = [(r, c, i) for r in range(2) for c in range(3) for i in range(2)]


def pairs(parts):
    return [(parts[2 * i], parts[2 * i + 1]) for i in range(len(parts) // 2)]


def moving_times(bounds_ref, w):
    top = jnp.where(bounds_ref[0, w + 1] < 4 * w + 4, 0, 1)
    bottom = jnp.where(bounds_ref[0, w] > 4 * w, 0, 1)
    return top, bottom


def turned(x, lane):
    odd = (lane & 32) != 0
    far = (lane & 64) != 0
    x = [jnp.where(odd, x[(d + 1) % 4], x[d]) for d in range(4)]
    x = [jnp.where(far, x[(d + 2) % 4], x[d]) for d in range(4)]
    x = [pltpu.roll(x[d], 32 * d, 1) if d else x[d] for d in range(4)]
    x = [jnp.where(odd, x[(1 - g) % 4], x[-g % 4]) for g in range(4)]
    return [jnp.where(far, x[(g + 2) % 4], x[g]) for g in range(4)]


def encode_planes(rows, out, stride):
    lane = lax.broadcasted_iota(jnp.int32, (8, 128), 1)
    low = lax.broadcasted_iota(jnp.int32, (8, 128), 0) < 4
    by_row = []
    for r in range(4):
        parts = pairs([rows[pl.ds(c * 32 + r, 8, stride=4), :] for c in range(12)])
        by_row.append(to_parameters(parts[:3], parts[3:]))
    for p in range(8):
        z = turned([by_row[r][p] for r in range(4)], lane)
        for h in (0, 1):
            first = jnp.where(low, z[2 * h], pltpu.roll(z[2 * h + 1], 4, 0))
            second = jnp.where(low, pltpu.roll(z[2 * h], 4, 0), z[2 * h + 1])
            out[pl.ds(h * 8 * stride + p, 8, stride=stride), :] = first
            out[pl.ds(h * 8 * stride + 8 + p, 8, stride=stride), :] = second


def block_half(h):
    return pl.multiple_of(8 * (h ^ (lax.axis_index("zt") % 2)), 8)


def encode_kernel(taken, out_ref, given, out_sem):
    def copy_out(step, h):
        at = pl.ds(pl.multiple_of((step % 3) * 16, 16), 16)
        return pltpu.make_async_copy(
            given.at[step, pl.ds(8 * h, 8)], out_ref.at[pl.ds(block_half(h), 8), step // 3, at], out_sem.at[h, step]
        )

    def one(step, carry):
        encode_planes(taken.at[step].reshape(12 * 32, 128), given.at[step].reshape(16 * 16, 128), 16)
        copy_out(step, 0).start()
        copy_out(step, 1).start()
        return carry

    lax.fori_loop(0, 12, one, 0)
    for step in range(12):
        copy_out(step, 0).wait()
        copy_out(step, 1).wait()


def encoded(taken):
    return pl.pallas_call(
        encode_kernel,
        in_specs=[pl.BlockSpec(memory_space=pltpu.VMEM)],
        out_specs=pl.BlockSpec(memory_space=pltpu.HBM),
        out_shape=pltpu.HBM((16, 4, 48, 128), jnp.float32),
        scratch_shapes=[pltpu.VMEM((12, 16, 16, 128), jnp.float32), pltpu.SemaphoreType.DMA((2, 12))],
        compiler_params=pltpu.CompilerParams(vmem_limit_bytes=VMEM_LIMIT),
    )(taken)


class ShiftedRows:
    def __init__(self, ref, by):
        self.ref = ref
        self.by = by

    def __setitem__(self, at, value):
        self.ref[pl.ds(self.by + at[0].start, at[0].size, stride=at[0].stride), :] = value


def encode_rest_kernel(rest, total_ref, out_ref, given, out_sem):
    out = given.reshape(16 * 72, 128)
    for n in range(16):
        given[n, pl.ds(64, 8), :] = total_ref[...]

    def copy_out(m, size, h):
        at = pl.ds(pl.multiple_of(m * 16, 8), size)
        return pltpu.make_async_copy(
            given.at[pl.ds(8 * h, 8), at], out_ref.at[pl.ds(block_half(h), 8), at], out_sem.at[h, m]
        )

    copy_out(4, 8, 0).start()
    copy_out(4, 8, 1).start()

    def one(m, carry):
        encode_planes(rest.at[m].reshape(12 * 32, 128), ShiftedRows(out, m * 16), 72)
        copy_out(m, 16, 0).start()
        copy_out(m, 16, 1).start()
        return carry

    lax.fori_loop(0, 4, one, 0)
    for h in range(2):
        for m in range(4):
            copy_out(m, 16, h).wait()
        copy_out(4, 8, h).wait()


def encoded_rest(rest, total):
    return pl.pallas_call(
        encode_rest_kernel,
        in_specs=[pl.BlockSpec(memory_space=pltpu.VMEM)] * 2,
        out_specs=pl.BlockSpec(memory_space=pltpu.HBM),
        out_shape=pltpu.HBM((16, 72, 128), jnp.float32),
        scratch_shapes=[pltpu.VMEM((16, 72, 128), jnp.float32), pltpu.SemaphoreType.DMA((2, 5))],
        compiler_params=pltpu.CompilerParams(vmem_limit_bytes=VMEM_LIMIT),
    )(rest, total)


def take_kernel(links_ref, x_ref, y_ref, z_ref, taken, rest, in_sem, rest_sem, z_sem):
    def copy_in(m, pair):
        if pair == 2:
            source = links_ref.at[m, pl.ds(0, 2), :, :, :, 3]
        else:
            source = links_ref.at[m, pl.ds(0, 2), :, :, pair, pl.ds(0, 2)]
        return pltpu.make_async_copy(source, taken.at[3 * m + pair], in_sem.at[3 * m + pair])

    def copy_rest(m):
        return pltpu.make_async_copy(links_ref.at[m, pl.ds(0, 2), :, :, :, 2], rest.at[m], rest_sem.at[m])

    def copies(m):
        return [copy_in(m, pair) for pair in range(3)] + [copy_rest(m)]

    copy_z = pltpu.make_async_copy(links_ref.at[pl.ds(0, 2), pl.ds(0, 2), :, :, :, 0], z_ref, z_sem)
    order = (2, 1, 0, 3)
    for m in order:
        for copy in copies(m):
            copy.start()
    copy_z.start()

    def rows(m, r, c, i, k, start, size):
        t, z = k // 4, k % 4
        at = pl.ds(start, size)
        if z == 2:
            return rest[m, r, c, i, t, at, :]
        if z == 3:
            return taken[3 * m + 2, r, c, i, t, at, :]
        return taken[3 * m + t, r, c, i, z, at, :]

    def row_face(m):
        parts = pairs([jnp.concatenate([rows(m, *e, k, 0, 1) for k in range(8)], axis=0) for e in ENTRIES])
        for p, value in enumerate(to_parameters(parts[:3], parts[3:])):
            y_ref[m // 2, p] = value

    lane = lax.broadcasted_iota(jnp.int32, (8, 128), 1)
    got = [None] * 3

    def column_face(m):
        for e, entry in enumerate(ENTRIES):
            n = 12 * (m - 1) + e
            for k in range(8):
                for h in range(2):
                    at = 16 * (n % 8) + 2 * k + h
                    value = rows(m, *entry, k, 8 * h, 8)
                    value = pltpu.roll(value, at, 1) if at else value
                    got[n // 8] = value if got[n // 8] is None else jnp.where(lane == at, value, got[n // 8])

    for m in order:
        for copy in copies(m):
            copy.wait()
        if m in (1, 2):
            column_face(m)
        if m in (0, 2):
            row_face(m)
    for n in range(3):
        x_ref[n] = got[n]
    copy_z.wait()


def taken_links(links):
    kept = pl.BlockSpec(memory_space=pltpu.VMEM)
    return pl.pallas_call(
        take_kernel,
        in_specs=[pl.BlockSpec(memory_space=pltpu.HBM)],
        out_specs=[kept] * 5,
        out_shape=[
            pltpu.VMEM((3, 8, 128), jnp.float32),
            pltpu.VMEM((2, 8, 8, 128), jnp.float32),
            pltpu.VMEM((2, 2, 3, 2, 2, 16, 128), jnp.float32),
            pltpu.VMEM((12, 2, 3, 2, 2, 16, 128), jnp.float32),
            pltpu.VMEM((4, 2, 3, 2, 2, 16, 128), jnp.float32),
        ],
        scratch_shapes=[
            pltpu.SemaphoreType.DMA((12,)),
            pltpu.SemaphoreType.DMA((4,)),
            pltpu.SemaphoreType.DMA,
        ],
        compiler_params=pltpu.CompilerParams(vmem_limit_bytes=VMEM_LIMIT),
    )(links)


def flat_rows(matrix):
    return [part for row in matrix for entry in row for part in entry]


def product_trace(a, b, c, d):
    total = None
    for i in range(3):
        for j in range(3):
            one = two = None
            for k in range(3):
                x = times(a[i][k], b[k][j])
                y = times(c[i][k], d[k][j])
                one = x if one is None else (one[0] + x[0], one[1] + x[1])
                two = y if two is None else (two[0] + y[0], two[1] + y[1])
            term = one[0] * two[0] + one[1] * two[1]
            total = term if total is None else total + term
    return total


class Sites:
    def __init__(self, unit, x_edge, y_edge, z_edge, out_ref):
        self.unit, self.x_edge, self.y_edge, self.z_edge = unit, x_edge, y_edge, z_edge
        self.out_ref = out_ref
        self.last_lane = lax.broadcasted_iota(jnp.int32, (8, 128), 1) == 127
        self.first_row = lax.broadcasted_iota(jnp.int32, (8, 128), 0) == 0

    def matrix(self, parts):
        parts = pairs(parts)
        return [parts[3 * i : 3 * i + 3] for i in range(3)]

    def here(self, m, t, z, h):
        return self.matrix([self.unit[m, c, t, z, pl.ds(8 * h, 8), :] for c in range(18)])

    def next_x(self, m, t, z, h):
        got = []
        for c in range(18):
            value = pltpu.roll(self.unit[m, c, t, z, pl.ds(8 * h, 8), :], 127, 1)
            beyond = pltpu.roll(self.x_edge[m - 1, c], 127 - 2 * (4 * t + z) - h, 1)
            got.append(jnp.where(self.last_lane, beyond, value))
        return self.matrix(got)

    def next_y(self, m, t, z, h):
        if h == 0:
            return self.matrix([self.unit[m, c, t, z, pl.ds(1, 8), :] for c in range(18)])
        got = []
        for c in range(18):
            value = self.unit[m, c, t, z, pl.ds(8, 8), :]
            beyond = self.y_edge[m // 2, c, pl.ds(4 * t + z, 1), :]
            value = jnp.where(self.first_row, beyond, value)
            got.append(pltpu.roll(value, 7, 0))
        return self.matrix(got)

    def next_z(self, m, t, z, h):
        if self.z_edge is None:
            return self.here(m, t, z + 1, h)
        return self.matrix([self.z_edge[m, c, t, pl.ds(8 * h, 8), :] for c in range(18)])

    def plane(self, t, z):
        total = None
        for h in range(2):
            at = (t, z, h)
            value = product_trace(self.here(0, *at), self.next_x(1, *at), self.here(1, *at), self.next_y(0, *at))
            value = value + product_trace(
                self.here(0, *at), self.next_x(2, *at), self.here(2, *at), self.next_z(0, *at)
            )
            value = value + product_trace(
                self.here(1, *at), self.next_y(2, *at), self.here(2, *at), self.next_z(1, *at)
            )
            value = value * (1.0 / 9.0)
            self.out_ref[t, z, pl.ds(8 * h, 8), :] = value
            total = value if total is None else total + value
        return total


def inner_kernel(links_ref, x_ref, y_ref, out_ref, sum_ref, unit, x_edge, y_edge, taken, sem):
    def copy_in(step):
        return pltpu.make_async_copy(
            links_ref.at[step // 2, pl.ds(0, 2), :, :, step % 2], taken.at[step], sem.at[step]
        )

    for step in range(6):
        copy_in(step).start()
    for m in range(2):
        for c, value in enumerate(flat_rows(from_parameters([y_ref[m, p] for p in range(8)]))):
            y_edge[m, c] = value
        parts = []
        for e in range(12):
            n = 12 * m + e
            value = x_ref[n // 8]
            parts.append(pltpu.roll(value, 128 - 16 * (n % 8), 1) if n % 8 else value)
        parts = pairs(parts)
        for c, value in enumerate(flat_rows(unit_rows(parts[:3], parts[3:]))):
            x_edge[m, c] = value

    def own(step, carry):
        part = step // 4
        z = step % 4

        @pl.when(z == 0)
        def _():
            copy_in(part).wait()

        for h in range(2):
            at = pl.ds(8 * h, 8)
            parts = pairs([taken[part, r, c, i, z, at, :] for r, c, i in ENTRIES])
            for c, value in enumerate(flat_rows(unit_rows(parts[:3], parts[3:]))):
                unit[part // 2, c, part % 2, z, at, :] = value
        return carry

    lax.fori_loop(0, 24, own, 0)
    sites = Sites(unit, x_edge, y_edge, None, out_ref)
    zero = jnp.zeros((8, 128), jnp.float32)
    sum_ref[...] = lax.fori_loop(0, 6, lambda step, total: total + sites.plane(step // 3, step % 3), zero)


def inner_plaquettes(links, x_face, y_face):
    kept = pl.BlockSpec(memory_space=pltpu.VMEM)
    return pl.pallas_call(
        inner_kernel,
        in_specs=[pl.BlockSpec(memory_space=pltpu.HBM)] + [kept] * 2,
        out_specs=[kept] * 5,
        out_shape=[
            pltpu.VMEM((2, 4, 16, 128), jnp.float32),
            pltpu.VMEM((8, 128), jnp.float32),
            pltpu.VMEM((3, 18, 2, 4, 16, 128), jnp.float32),
            pltpu.VMEM((2, 18, 8, 128), jnp.float32),
            pltpu.VMEM((2, 18, 8, 128), jnp.float32),
        ],
        scratch_shapes=[
            pltpu.VMEM((6, 2, 3, 2, 4, 16, 128), jnp.float32),
            pltpu.SemaphoreType.DMA((6,)),
        ],
        compiler_params=pltpu.CompilerParams(vmem_limit_bytes=VMEM_LIMIT),
    )(links, x_face, y_face)


def outer_kernel(inner_ref, part_ref, unit, x_edge, y_edge, z_ref, out_ref, sum_ref, z_edge):
    for t in range(2):
        for z in range(3):
            out_ref[t, z] = inner_ref[t, z]

    def above(step, carry):
        m = step // 2
        t = step % 2
        for h in range(2):
            at = pl.ds(8 * h, 8)
            parts = pairs([z_ref[m, r, c, i, t, at, :] for r, c, i in ENTRIES])
            for c, value in enumerate(flat_rows(unit_rows(parts[:3], parts[3:]))):
                z_edge[m, c, t, at, :] = value
        return carry

    lax.fori_loop(0, 4, above, 0)
    sites = Sites(unit, x_edge, y_edge, z_edge, out_ref)
    total = lax.fori_loop(0, 2, lambda t, total: total + sites.plane(t, 3), part_ref[...])
    sum_ref[...] = jnp.broadcast_to(jnp.sum(total, keepdims=True), (8, 128))


def outer_plaquettes(inner, part, unit, x_edge, y_edge, z_face):
    kept = pl.BlockSpec(memory_space=pltpu.VMEM)
    return pl.pallas_call(
        outer_kernel,
        in_specs=[kept] * 6,
        out_shape=[
            jax.ShapeDtypeStruct((2, 4, 16, 128), jnp.float32),
            jax.ShapeDtypeStruct((8, 128), jnp.float32),
        ],
        scratch_shapes=[pltpu.VMEM((2, 18, 2, 16, 128), jnp.float32)],
        compiler_params=pltpu.CompilerParams(vmem_limit_bytes=VMEM_LIMIT),
    )(inner, part, unit, x_edge, y_edge, z_face)


def put_planes(sources, places, out_ref, planes, sem):
    def copy_out(part, m):
        t, j = places[part]
        return pltpu.make_async_copy(planes.at[part, m], out_ref.at[pl.ds(18 * m, 18), t, j], sem.at[part, m])

    def one(m, carry):
        for part, (rows, stride, start, step, half) in enumerate(sources):
            for h in range(2):
                at = half(h) * stride + start + m * step
                values = [rows[pl.ds(at + p, 8, stride=stride), :] for p in range(8)]
                for c, value in enumerate(flat_rows(from_parameters(values))):
                    planes[part, m, c, pl.ds(8 * h, 8), :] = value
            copy_out(part, m).start()
        return carry

    lax.fori_loop(0, 4, one, 0)
    for m in range(4):
        for part in range(len(sources)):
            copy_out(part, m).wait()


PLANE_SCRATCH = [pltpu.VMEM((4, 4, 18, 16, 128), jnp.float32), pltpu.SemaphoreType.DMA((4, 4))]


def decode_kernel(bounds_ref, own_ref, out_ref, planes, sem, zeros, zero_sem):
    w = lax.axis_index("zt")
    top, bottom = moving_times(bounds_ref, w)
    zeros[...] = jnp.zeros((18, 16, 128), jnp.float32)

    def fill(t, j, m):
        return pltpu.make_async_copy(zeros, out_ref.at[pl.ds(18 * m, 18), t, j], zero_sem.at[t, j - 2])

    def every_empty(act):
        for t in range(2):
            depth = bounds_ref[t, w + 1] - bounds_ref[t, w]
            for j in range(2, 6):

                @pl.when(j >= depth)
                def _(t=t, j=j):
                    for m in range(4):
                        act(fill(t, j, m))

    every_empty(lambda copy: copy.start())
    rows = own_ref.reshape(16 * 192, 128)
    planes_in = ((1 - top, 3, 5 - top), (1 - bottom, 0, 2 - 2 * bottom), (0, 1, 1), (1, 1, 3))
    sources = [(rows, 192, 8 * slot, 48, block_half) for t, z, slot in planes_in]
    places = [(t, z + 4 * w - bounds_ref[t, w]) for t, z, slot in planes_in]
    put_planes(sources, places, out_ref, planes, sem)
    every_empty(lambda copy: copy.wait())


def decoded(bounds, own):
    return pl.pallas_call(
        decode_kernel,
        in_specs=[pl.BlockSpec(memory_space=pltpu.SMEM), pl.BlockSpec(memory_space=pltpu.VMEM)],
        out_specs=pl.BlockSpec(memory_space=pltpu.HBM),
        out_shape=jax.ShapeDtypeStruct((72, 2, 6, 16, 128), jnp.float32),
        scratch_shapes=PLANE_SCRATCH
        + [pltpu.VMEM((18, 16, 128), jnp.float32), pltpu.SemaphoreType.DMA((2, 4))],
        compiler_params=pltpu.CompilerParams(vmem_limit_bytes=VMEM_LIMIT),
    )(bounds, own)


def cut_kernel(bounds_ref, own_ref, first_ref, second_ref):
    w = lax.axis_index("zt")
    top, bottom = moving_times(bounds_ref, w)
    even = w % 2 == 0
    top = 32 + 8 * top
    bottom = 16 * bottom
    first = pl.multiple_of(jnp.where(even, top, bottom), 8)
    second = pl.multiple_of(jnp.where(even, bottom, top), 8)
    for h in range(2):
        here = pl.ds(8 * h, 8)
        there = pl.ds(block_half(h), 8)
        for m in range(4):
            first_ref[here, m] = own_ref[there, m, pl.ds(first, 8), :]
            second_ref[here, m] = own_ref[there, m, pl.ds(second, 8), :]


def cut_planes(bounds, own):
    return pl.pallas_call(
        cut_kernel,
        in_specs=[pl.BlockSpec(memory_space=pltpu.SMEM), pl.BlockSpec(memory_space=pltpu.VMEM)],
        out_shape=[jax.ShapeDtypeStruct((16, 4, 8, 128), jnp.float32)] * 2,
        compiler_params=pltpu.CompilerParams(vmem_limit_bytes=VMEM_LIMIT),
    )(bounds, own)


def rest_kernel(count, bounds_ref, first_ref, second_ref, rest_ref, whole_ref, out_ref, mean_ref, planes, sem):
    w = lax.axis_index("zt")
    top, bottom = moving_times(bounds_ref, w)
    even = w % 2 == 0
    low_time = jnp.where(w == 0, bottom, 1 - bottom)
    high_time = jnp.where(w == 7, top, 1 - top)
    high_at = jnp.where(w == 7, 3, 4) + 4 * w - bounds_ref[high_time, w]
    low_at = jnp.int32(0)
    rows = rest_ref.reshape(16 * 72, 128)
    sources = [(ref.reshape(16 * 32, 128), 32, 0, 8, lambda h: 8 * h) for ref in (first_ref, second_ref)]
    sources += [(rows, 72, 8 * t, 16, block_half) for t in range(2)]
    places = [
        (jnp.where(even, high_time, low_time), jnp.where(even, high_at, low_at)),
        (jnp.where(even, low_time, high_time), jnp.where(even, low_at, high_at)),
    ]
    places += [(t, 2 + 4 * w - bounds_ref[t, w]) for t in range(2)]
    totals = []
    for h in range(2):
        part = rest_ref[block_half(h), pl.ds(64, 8), :]
        for n in range(1, 8):
            part = part + rest_ref[block_half(h) + n, pl.ds(64, 8), :]
        totals.append(part)
    total = totals[0] + totals[1]
    mean_ref[0, 0] = jnp.max(total) * (1.0 / count)
    put_planes(sources, places, out_ref, planes, sem)


def with_rest(bounds, first, second, rest, whole, count):
    kept = pl.BlockSpec(memory_space=pltpu.VMEM)
    return pl.pallas_call(
        lambda *refs: rest_kernel(count, *refs),
        in_specs=[pl.BlockSpec(memory_space=pltpu.SMEM)] + [kept] * 3 + [pl.BlockSpec(memory_space=pltpu.HBM)],
        out_specs=[pl.BlockSpec(memory_space=pltpu.HBM), pl.BlockSpec(memory_space=pltpu.SMEM)],
        out_shape=[
            jax.ShapeDtypeStruct((72, 2, 6, 16, 128), jnp.float32),
            jax.ShapeDtypeStruct((1, 1), jnp.float32),
        ],
        input_output_aliases={4: 0},
        scratch_shapes=PLANE_SCRATCH,
        compiler_params=pltpu.CompilerParams(vmem_limit_bytes=VMEM_LIMIT),
    )(bounds, first, second, rest, whole)


def summed(value, steps):
    for axis, by in steps:
        count = lax.axis_size(axis)
        value = value + lax.ppermute(value, axis, [(i, i ^ by) for i in range(count)])
    return value


def spread(payload):
    places = [(gx, gy) for gy in range(4) for gx in range(4)]
    groups = [[(gx * 4 + gy) * 8 + w for gx, gy in places[8 * (w % 2) :] + places[: 8 * (w % 2)]] for w in range(8)]
    return lax.all_to_all(
        payload, ("gx", "gy", "zt"), split_axis=0, concat_axis=0, axis_index_groups=groups, tiled=True
    )


def local(links, bounds):
    held = pltpu.with_memory_space_constraint(links, pltpu.HBM)
    x_face, y_face, z_face, taken, rest = taken_links(held)
    y_face = passed_along(y_face, "gy", -1)
    x_face = passed_along(x_face, "gx", -1)
    payload = encoded(taken)
    payload, links, x_face, y_face, z_face = lax.optimization_barrier((payload, links, x_face, y_face, z_face))
    held = pltpu.with_memory_space_constraint(links, pltpu.HBM)
    moved = spread(payload)
    z_face = passed_along(z_face, "zt", -1)
    plaquette, total = outer_plaquettes(*inner_plaquettes(held, x_face, y_face), z_face)
    total = summed(total, (("zt", 1), ("zt", 2), ("zt", 6)))
    rest = encoded_rest(rest, total)
    moved, rest = lax.optimization_barrier((moved, rest))
    moved_rest = spread(rest)
    first, second = cut_planes(bounds, moved)
    first = lax.ppermute(first, "zt", [(i, i ^ 1) for i in range(8)])
    second = lax.ppermute(second, "zt", [(0, 0), (7, 7)] + [(i, (i + 1 ^ 1) - 1) for i in range(1, 7)])
    file_links = decoded(bounds, moved)
    file_links, mean = with_rest(bounds, first, second, moved_rest, file_links, plaquette.size * 128)
    return file_links.reshape(4, 3, 3, 2, 2, 6, 4, 1, 4, 1, 128), plaquette, mean[0, 0]


def solution(mesh):
    in_specs = (P(None, None, None, None, None, "zt", "gy", "gx"), P())
    out_specs = (
        P(None, None, None, None, None, "zt", None, "gx", None, "gy", None),
        P(None, "zt", "gy", "gx"),
        P(),
    )
    return jax.shard_map(local, mesh=mesh, in_specs=in_specs, out_specs=out_specs, check_vma=False)
```

```python
import jax
import jax.numpy as jnp
from jax import lax
from jax.experimental import pallas as pl
from jax.experimental.pallas import tpu as pltpu
from jax.sharding import PartitionSpec as P

VMEM_LIMIT = 24 * 1024 * 1024
CROSS = ((1, 2), (2, 0), (0, 1))


def passed_along(value, axis, by):
    count = lax.axis_size(axis)
    return lax.ppermute(value, axis, [(i, (i + by) % count) for i in range(count)])


def times(a, b):
    return (a[0] * b[0] - a[1] * b[1], a[0] * b[1] + a[1] * b[0])


def times_conj(a, b):
    return (a[0] * b[0] + a[1] * b[1], a[1] * b[0] - a[0] * b[1])


def minus(a, b):
    return (a[0] - b[0], a[1] - b[1])


def scaled(a, s):
    return (a[0] * s, a[1] * s)


def square(a):
    return a[0] * a[0] + a[1] * a[1]


def last_row(u, v):
    rows = []
    for b, c in CROSS:
        x = minus(times(u[b], v[c]), times(u[c], v[b]))
        rows.append((x[0], -x[1]))
    return rows


def unit_rows(r1, r2):
    n = lax.rsqrt(square(r1[0]) + square(r1[1]) + square(r1[2]))
    u = [scaled(x, n) for x in r1]
    terms = [times_conj(y, x) for x, y in zip(u, r2)]
    c = (terms[0][0] + terms[1][0] + terms[2][0], terms[0][1] + terms[1][1] + terms[2][1])
    v = [minus(y, times(c, x)) for x, y in zip(u, r2)]
    n = lax.rsqrt(square(v[0]) + square(v[1]) + square(v[2]))
    v = [scaled(x, n) for x in v]
    return [u, v, last_row(u, v)]


def angle_value(a):
    t = a[1] / (jnp.abs(a[0]) + jnp.abs(a[1]))
    return jnp.where(a[0] < 0.0, 2.0 - t, t)


def angle_point(t):
    back = t > 1.0
    y = jnp.where(back, 2.0 - t, t)
    x = 1.0 - jnp.abs(y)
    x = jnp.where(back, -x, x)
    return (x, y), x * x + y * y


def to_parameters(r1, r2):
    inverse = 1.0 / square(r1[0])
    p1 = scaled(times_conj(r1[1], r1[0]), inverse)
    p2 = scaled(times_conj(r1[2], r1[0]), inverse)
    s1 = minus(r2[1], times(r2[0], p1))
    s2 = minus(r2[2], times(r2[0], p2))
    q = scaled(times_conj(s2, s1), 1.0 / square(s1))
    return [p1[0], p1[1], p2[0], p2[1], q[0], q[1], angle_value(r1[0]), angle_value(s1)]


def from_parameters(values):
    p1 = (values[0], values[1])
    p2 = (values[2], values[3])
    q = (values[4], values[5])
    size = 1.0 + square(p1) + square(p2)
    g = times_conj(q, p2)
    g = (g[0] + p1[0], g[1] - p1[1])
    gp1 = times(g, p1)
    gp2 = times(g, p2)
    v = [(-g[0], -g[1]), (size - gp1[0], -gp1[1]), (size * q[0] - gp2[0], size * q[1] - gp2[1])]
    a, a2 = angle_point(values[6])
    a = scaled(a, lax.rsqrt(a2 * size))
    b, b2 = angle_point(values[7])
    b = scaled(b, lax.rsqrt(b2 * (square(v[0]) + square(v[1]) + square(v[2]))))
    u = [a, times(a, p1), times(a, p2)]
    v = [times(b, x) for x in v]
    k = scaled(times(a, b), size)
    first = times(k, minus(times(p1, q), p2))
    second = times(k, q)
    return [u, v, [(first[0], -first[1]), (-second[0], second[1]), (k[0], -k[1])]]


ENTRIES = [(r, c, i) for r in range(2) for c in range(3) for i in range(2)]


def pairs(parts):
    return [(parts[2 * i], parts[2 * i + 1]) for i in range(len(parts) // 2)]


def moving_times(bounds_ref, w):
    top = jnp.where(bounds_ref[0, w + 1] < 4 * w + 4, 0, 1)
    bottom = jnp.where(bounds_ref[0, w] > 4 * w, 0, 1)
    return top, bottom


def turned(x, lane):
    odd = (lane & 32) != 0
    far = (lane & 64) != 0
    x = [jnp.where(odd, x[(d + 1) % 4], x[d]) for d in range(4)]
    x = [jnp.where(far, x[(d + 2) % 4], x[d]) for d in range(4)]
    x = [pltpu.roll(x[d], 32 * d, 1) if d else x[d] for d in range(4)]
    x = [jnp.where(odd, x[(1 - g) % 4], x[-g % 4]) for g in range(4)]
    return [jnp.where(far, x[(g + 2) % 4], x[g]) for g in range(4)]


def encode_planes(rows, out, stride):
    lane = lax.broadcasted_iota(jnp.int32, (8, 128), 1)
    low = lax.broadcasted_iota(jnp.int32, (8, 128), 0) < 4
    by_row = []
    for r in range(4):
        parts = pairs([rows[pl.ds(c * 32 + r, 8, stride=4), :] for c in range(12)])
        by_row.append(to_parameters(parts[:3], parts[3:]))
    for p in range(8):
        z = turned([by_row[r][p] for r in range(4)], lane)
        for h in (0, 1):
            first = jnp.where(low, z[2 * h], pltpu.roll(z[2 * h + 1], 4, 0))
            second = jnp.where(low, pltpu.roll(z[2 * h], 4, 0), z[2 * h + 1])
            out[pl.ds(h * 8 * stride + p, 8, stride=stride), :] = first
            out[pl.ds(h * 8 * stride + 8 + p, 8, stride=stride), :] = second


def block_half(h):
    return pl.multiple_of(8 * (h ^ (lax.axis_index("zt") % 2)), 8)


def encode_kernel(taken, out_ref, given, out_sem):
    def copy_out(step, h):
        at = pl.ds(pl.multiple_of((step % 3) * 16, 16), 16)
        return pltpu.make_async_copy(
            given.at[step, pl.ds(8 * h, 8)], out_ref.at[pl.ds(block_half(h), 8), step // 3, at], out_sem.at[h, step]
        )

    def one(step, carry):
        encode_planes(taken.at[step].reshape(12 * 32, 128), given.at[step].reshape(16 * 16, 128), 16)
        copy_out(step, 0).start()
        copy_out(step, 1).start()
        return carry

    lax.fori_loop(0, 12, one, 0)
    for step in range(12):
        copy_out(step, 0).wait()
        copy_out(step, 1).wait()


def encoded(taken):
    return pl.pallas_call(
        encode_kernel,
        in_specs=[pl.BlockSpec(memory_space=pltpu.VMEM)],
        out_specs=pl.BlockSpec(memory_space=pltpu.HBM),
        out_shape=pltpu.HBM((16, 4, 48, 128), jnp.float32),
        scratch_shapes=[pltpu.VMEM((12, 16, 16, 128), jnp.float32), pltpu.SemaphoreType.DMA((2, 12))],
        compiler_params=pltpu.CompilerParams(vmem_limit_bytes=VMEM_LIMIT),
    )(taken)


class ShiftedRows:
    def __init__(self, ref, by):
        self.ref = ref
        self.by = by

    def __setitem__(self, at, value):
        self.ref[pl.ds(self.by + at[0].start, at[0].size, stride=at[0].stride), :] = value


def encode_rest_kernel(rest, total_ref, out_ref, given, out_sem):
    out = given.reshape(16 * 72, 128)
    for n in range(16):
        given[n, pl.ds(64, 8), :] = total_ref[...]

    def copy_out(m, size, h):
        at = pl.ds(pl.multiple_of(m * 16, 8), size)
        return pltpu.make_async_copy(
            given.at[pl.ds(8 * h, 8), at], out_ref.at[pl.ds(block_half(h), 8), at], out_sem.at[h, m]
        )

    copy_out(4, 8, 0).start()
    copy_out(4, 8, 1).start()

    def one(m, carry):
        encode_planes(rest.at[m].reshape(12 * 32, 128), ShiftedRows(out, m * 16), 72)
        copy_out(m, 16, 0).start()
        copy_out(m, 16, 1).start()
        return carry

    lax.fori_loop(0, 4, one, 0)
    for h in range(2):
        for m in range(4):
            copy_out(m, 16, h).wait()
        copy_out(4, 8, h).wait()


def encoded_rest(rest, total):
    return pl.pallas_call(
        encode_rest_kernel,
        in_specs=[pl.BlockSpec(memory_space=pltpu.VMEM)] * 2,
        out_specs=pl.BlockSpec(memory_space=pltpu.HBM),
        out_shape=pltpu.HBM((16, 72, 128), jnp.float32),
        scratch_shapes=[pltpu.VMEM((16, 72, 128), jnp.float32), pltpu.SemaphoreType.DMA((2, 5))],
        compiler_params=pltpu.CompilerParams(vmem_limit_bytes=VMEM_LIMIT),
    )(rest, total)


def take_kernel(links_ref, x_ref, y_ref, z_ref, taken, rest, in_sem, rest_sem, z_sem):
    def copy_in(m, pair):
        if pair == 2:
            source = links_ref.at[m, pl.ds(0, 2), :, :, :, 3]
        else:
            source = links_ref.at[m, pl.ds(0, 2), :, :, pair, pl.ds(0, 2)]
        return pltpu.make_async_copy(source, taken.at[3 * m + pair], in_sem.at[3 * m + pair])

    def copy_rest(m):
        return pltpu.make_async_copy(links_ref.at[m, pl.ds(0, 2), :, :, :, 2], rest.at[m], rest_sem.at[m])

    def copies(m):
        return [copy_in(m, pair) for pair in range(3)] + [copy_rest(m)]

    copy_z = pltpu.make_async_copy(links_ref.at[pl.ds(0, 2), pl.ds(0, 2), :, :, :, 0], z_ref, z_sem)
    order = (2, 1, 0, 3)
    for m in order:
        for copy in copies(m):
            copy.start()
    copy_z.start()

    def rows(m, r, c, i, k, start, size):
        t, z = k // 4, k % 4
        at = pl.ds(start, size)
        if z == 2:
            return rest[m, r, c, i, t, at, :]
        if z == 3:
            return taken[3 * m + 2, r, c, i, t, at, :]
        return taken[3 * m + t, r, c, i, z, at, :]

    def row_face(m):
        parts = pairs([jnp.concatenate([rows(m, *e, k, 0, 1) for k in range(8)], axis=0) for e in ENTRIES])
        for p, value in enumerate(to_parameters(parts[:3], parts[3:])):
            y_ref[m // 2, p] = value

    lane = lax.broadcasted_iota(jnp.int32, (8, 128), 1)
    got = [None] * 3

    def column_face(m):
        for e, entry in enumerate(ENTRIES):
            n = 12 * (m - 1) + e
            for k in range(8):
                for h in range(2):
                    at = 16 * (n % 8) + 2 * k + h
                    value = rows(m, *entry, k, 8 * h, 8)
                    value = pltpu.roll(value, at, 1) if at else value
                    got[n // 8] = value if got[n // 8] is None else jnp.where(lane == at, value, got[n // 8])

    for m in order:
        for copy in copies(m):
            copy.wait()
        if m in (1, 2):
            column_face(m)
        if m in (0, 2):
            row_face(m)
    for n in range(3):
        x_ref[n] = got[n]
    copy_z.wait()


def taken_links(links):
    kept = pl.BlockSpec(memory_space=pltpu.VMEM)
    return pl.pallas_call(
        take_kernel,
        in_specs=[pl.BlockSpec(memory_space=pltpu.HBM)],
        out_specs=[kept] * 5,
        out_shape=[
            pltpu.VMEM((3, 8, 128), jnp.float32),
            pltpu.VMEM((2, 8, 8, 128), jnp.float32),
            pltpu.VMEM((2, 2, 3, 2, 2, 16, 128), jnp.float32),
            pltpu.VMEM((12, 2, 3, 2, 2, 16, 128), jnp.float32),
            pltpu.VMEM((4, 2, 3, 2, 2, 16, 128), jnp.float32),
        ],
        scratch_shapes=[
            pltpu.SemaphoreType.DMA((12,)),
            pltpu.SemaphoreType.DMA((4,)),
            pltpu.SemaphoreType.DMA,
        ],
        compiler_params=pltpu.CompilerParams(vmem_limit_bytes=VMEM_LIMIT),
    )(links)


def flat_rows(matrix):
    return [part for row in matrix for entry in row for part in entry]


def product_trace(a, b, c, d):
    total = None
    for i in range(3):
        for j in range(3):
            one = two = None
            for k in range(3):
                x = times(a[i][k], b[k][j])
                y = times(c[i][k], d[k][j])
                one = x if one is None else (one[0] + x[0], one[1] + x[1])
                two = y if two is None else (two[0] + y[0], two[1] + y[1])
            term = one[0] * two[0] + one[1] * two[1]
            total = term if total is None else total + term
    return total


class Sites:
    def __init__(self, unit, x_edge, y_edge, z_edge, out_ref):
        self.unit, self.x_edge, self.y_edge, self.z_edge = unit, x_edge, y_edge, z_edge
        self.out_ref = out_ref
        self.last_lane = lax.broadcasted_iota(jnp.int32, (8, 128), 1) == 127
        self.first_row = lax.broadcasted_iota(jnp.int32, (8, 128), 0) == 0

    def matrix(self, parts):
        parts = pairs(parts)
        return [parts[3 * i : 3 * i + 3] for i in range(3)]

    def here(self, m, t, z, h):
        return self.matrix([self.unit[m, c, t, z, pl.ds(8 * h, 8), :] for c in range(18)])

    def next_x(self, m, t, z, h):
        got = []
        for c in range(18):
            value = pltpu.roll(self.unit[m, c, t, z, pl.ds(8 * h, 8), :], 127, 1)
            beyond = pltpu.roll(self.x_edge[m - 1, c], 127 - 2 * (4 * t + z) - h, 1)
            got.append(jnp.where(self.last_lane, beyond, value))
        return self.matrix(got)

    def next_y(self, m, t, z, h):
        if h == 0:
            return self.matrix([self.unit[m, c, t, z, pl.ds(1, 8), :] for c in range(18)])
        got = []
        for c in range(18):
            value = self.unit[m, c, t, z, pl.ds(8, 8), :]
            beyond = self.y_edge[m // 2, c, pl.ds(4 * t + z, 1), :]
            value = jnp.where(self.first_row, beyond, value)
            got.append(pltpu.roll(value, 7, 0))
        return self.matrix(got)

    def next_z(self, m, t, z, h):
        if self.z_edge is None:
            return self.here(m, t, z + 1, h)
        return self.matrix([self.z_edge[m, c, t, pl.ds(8 * h, 8), :] for c in range(18)])

    def plane(self, t, z):
        total = None
        for h in range(2):
            at = (t, z, h)
            value = product_trace(self.here(0, *at), self.next_x(1, *at), self.here(1, *at), self.next_y(0, *at))
            value = value + product_trace(
                self.here(0, *at), self.next_x(2, *at), self.here(2, *at), self.next_z(0, *at)
            )
            value = value + product_trace(
                self.here(1, *at), self.next_y(2, *at), self.here(2, *at), self.next_z(1, *at)
            )
            value = value * (1.0 / 9.0)
            self.out_ref[t, z, pl.ds(8 * h, 8), :] = value
            total = value if total is None else total + value
        return total


def inner_kernel(links_ref, x_ref, y_ref, out_ref, sum_ref, unit, x_edge, y_edge, taken, sem):
    def copy_in(step):
        return pltpu.make_async_copy(
            links_ref.at[step // 2, pl.ds(0, 2), :, :, step % 2], taken.at[step], sem.at[step]
        )

    for step in range(6):
        copy_in(step).start()
    for m in range(2):
        for c, value in enumerate(flat_rows(from_parameters([y_ref[m, p] for p in range(8)]))):
            y_edge[m, c] = value
        parts = []
        for e in range(12):
            n = 12 * m + e
            value = x_ref[n // 8]
            parts.append(pltpu.roll(value, 128 - 16 * (n % 8), 1) if n % 8 else value)
        parts = pairs(parts)
        for c, value in enumerate(flat_rows(unit_rows(parts[:3], parts[3:]))):
            x_edge[m, c] = value

    def own(step, carry):
        part = step // 4
        z = step % 4

        @pl.when(z == 0)
        def _():
            copy_in(part).wait()

        for h in range(2):
            at = pl.ds(8 * h, 8)
            parts = pairs([taken[part, r, c, i, z, at, :] for r, c, i in ENTRIES])
            for c, value in enumerate(flat_rows(unit_rows(parts[:3], parts[3:]))):
                unit[part // 2, c, part % 2, z, at, :] = value
        return carry

    lax.fori_loop(0, 24, own, 0)
    sites = Sites(unit, x_edge, y_edge, None, out_ref)
    zero = jnp.zeros((8, 128), jnp.float32)
    sum_ref[...] = lax.fori_loop(0, 6, lambda step, total: total + sites.plane(step // 3, step % 3), zero)


def inner_plaquettes(links, x_face, y_face):
    kept = pl.BlockSpec(memory_space=pltpu.VMEM)
    return pl.pallas_call(
        inner_kernel,
        in_specs=[pl.BlockSpec(memory_space=pltpu.HBM)] + [kept] * 2,
        out_specs=[kept] * 5,
        out_shape=[
            pltpu.VMEM((2, 4, 16, 128), jnp.float32),
            pltpu.VMEM((8, 128), jnp.float32),
            pltpu.VMEM((3, 18, 2, 4, 16, 128), jnp.float32),
            pltpu.VMEM((2, 18, 8, 128), jnp.float32),
            pltpu.VMEM((2, 18, 8, 128), jnp.float32),
        ],
        scratch_shapes=[
            pltpu.VMEM((6, 2, 3, 2, 4, 16, 128), jnp.float32),
            pltpu.SemaphoreType.DMA((6,)),
        ],
        compiler_params=pltpu.CompilerParams(vmem_limit_bytes=VMEM_LIMIT),
    )(links, x_face, y_face)


def outer_kernel(inner_ref, part_ref, unit, x_edge, y_edge, z_ref, out_ref, sum_ref, z_edge):
    for t in range(2):
        for z in range(3):
            out_ref[t, z] = inner_ref[t, z]

    def above(step, carry):
        m = step // 2
        t = step % 2
        for h in range(2):
            at = pl.ds(8 * h, 8)
            parts = pairs([z_ref[m, r, c, i, t, at, :] for r, c, i in ENTRIES])
            for c, value in enumerate(flat_rows(unit_rows(parts[:3], parts[3:]))):
                z_edge[m, c, t, at, :] = value
        return carry

    lax.fori_loop(0, 4, above, 0)
    sites = Sites(unit, x_edge, y_edge, z_edge, out_ref)
    total = lax.fori_loop(0, 2, lambda t, total: total + sites.plane(t, 3), part_ref[...])
    sum_ref[...] = jnp.broadcast_to(jnp.sum(total, keepdims=True), (8, 128))


def outer_plaquettes(inner, part, unit, x_edge, y_edge, z_face):
    kept = pl.BlockSpec(memory_space=pltpu.VMEM)
    return pl.pallas_call(
        outer_kernel,
        in_specs=[kept] * 6,
        out_shape=[
            jax.ShapeDtypeStruct((2, 4, 16, 128), jnp.float32),
            jax.ShapeDtypeStruct((8, 128), jnp.float32),
        ],
        scratch_shapes=[pltpu.VMEM((2, 18, 2, 16, 128), jnp.float32)],
        compiler_params=pltpu.CompilerParams(vmem_limit_bytes=VMEM_LIMIT),
    )(inner, part, unit, x_edge, y_edge, z_face)


def put_planes(sources, bounds, placed, out_ref, planes, sem):
    def copy_out(places, part, m):
        t, j = places[part]
        return pltpu.make_async_copy(planes.at[part, m], out_ref.at[pl.ds(18 * m, 18), t, j], sem.at[part, m])

    def decode(part, m):
        rows, stride, start, step, half = sources[part]
        for h in range(2):
            at = half(h) * stride + start + m * step
            values = [rows[pl.ds(at + p, 8, stride=stride), :] for p in range(8)]
            for c, value in enumerate(flat_rows(from_parameters(values))):
                planes[part, m, c, pl.ds(8 * h, 8), :] = value

    parts = range(len(sources))
    for part in parts:
        decode(part, 0)
    if bounds is not None:
        bounds.wait()
    places = placed()
    for part in parts:
        copy_out(places, part, 0).start()

    def one(m, carry):
        for part in parts:
            decode(part, m)
            copy_out(places, part, m).start()
        return carry

    lax.fori_loop(1, 4, one, 0)
    for m in range(4):
        for part in parts:
            copy_out(places, part, m).wait()


PLANE_SCRATCH = [
    pltpu.VMEM((4, 4, 18, 16, 128), jnp.float32),
    pltpu.SemaphoreType.DMA((4, 4)),
    pltpu.SMEM((2, 9), jnp.int32),
    pltpu.SemaphoreType.DMA,
]


def decode_kernel(bounds_in, own_ref, out_ref, planes, sem, bounds_ref, bounds_sem, zeros, zero_sem):
    bounds = pltpu.make_async_copy(bounds_in, bounds_ref, bounds_sem)
    bounds.start()
    w = lax.axis_index("zt")
    zeros[...] = jnp.zeros((18, 16, 128), jnp.float32)

    def fill(t, j, m):
        return pltpu.make_async_copy(zeros, out_ref.at[pl.ds(18 * m, 18), t, j], zero_sem.at[t, j - 2])

    def every_empty(act):
        for t in range(2):
            depth = bounds_ref[t, w + 1] - bounds_ref[t, w]
            for j in range(2, 6):

                @pl.when(j >= depth)
                def _(t=t, j=j):
                    for m in range(4):
                        act(fill(t, j, m))

    bounds.wait()
    every_empty(lambda copy: copy.start())
    top, bottom = moving_times(bounds_ref, w)
    rows = own_ref.reshape(16 * 192, 128)
    planes_in = ((1 - top, 3, 5 - top), (1 - bottom, 0, 2 - 2 * bottom), (0, 1, 1), (1, 1, 3))
    sources = [(rows, 192, 8 * slot, 48, block_half) for t, z, slot in planes_in]
    places = [(t, z + 4 * w - bounds_ref[t, w]) for t, z, slot in planes_in]
    put_planes(sources, None, lambda: places, out_ref, planes, sem)
    every_empty(lambda copy: copy.wait())


def decoded(bounds, own):
    return pl.pallas_call(
        decode_kernel,
        in_specs=[pl.BlockSpec(memory_space=pl.ANY), pl.BlockSpec(memory_space=pltpu.VMEM)],
        out_specs=pl.BlockSpec(memory_space=pltpu.HBM),
        out_shape=jax.ShapeDtypeStruct((72, 2, 6, 16, 128), jnp.float32),
        scratch_shapes=PLANE_SCRATCH
        + [pltpu.VMEM((18, 16, 128), jnp.float32), pltpu.SemaphoreType.DMA((2, 4))],
        compiler_params=pltpu.CompilerParams(vmem_limit_bytes=VMEM_LIMIT),
    )(bounds, own)


def cut_kernel(bounds_ref, own_ref, first_ref, second_ref):
    w = lax.axis_index("zt")
    top, bottom = moving_times(bounds_ref, w)
    even = w % 2 == 0
    top = 32 + 8 * top
    bottom = 16 * bottom
    first = pl.multiple_of(jnp.where(even, top, bottom), 8)
    second = pl.multiple_of(jnp.where(even, bottom, top), 8)
    for h in range(2):
        here = pl.ds(8 * h, 8)
        there = pl.ds(block_half(h), 8)
        for m in range(4):
            first_ref[here, m] = own_ref[there, m, pl.ds(first, 8), :]
            second_ref[here, m] = own_ref[there, m, pl.ds(second, 8), :]


def cut_planes(bounds, own):
    return pl.pallas_call(
        cut_kernel,
        in_specs=[pl.BlockSpec(memory_space=pltpu.SMEM), pl.BlockSpec(memory_space=pltpu.VMEM)],
        out_shape=[jax.ShapeDtypeStruct((16, 4, 8, 128), jnp.float32)] * 2,
        compiler_params=pltpu.CompilerParams(vmem_limit_bytes=VMEM_LIMIT),
    )(bounds, own)


def rest_kernel(
    count,
    bounds_in,
    first_ref,
    second_ref,
    rest_ref,
    whole_ref,
    out_ref,
    mean_ref,
    planes,
    sem,
    bounds_ref,
    bounds_sem,
    mean,
    mean_sem,
):
    bounds = pltpu.make_async_copy(bounds_in, bounds_ref, bounds_sem)
    bounds.start()
    w = lax.axis_index("zt")
    totals = []
    for h in range(2):
        part = rest_ref[block_half(h), pl.ds(64, 8), :]
        for n in range(1, 8):
            part = part + rest_ref[block_half(h) + n, pl.ds(64, 8), :]
        totals.append(part)
    mean[0, 0] = jnp.max(totals[0] + totals[1]) * (1.0 / count)
    mean_out = pltpu.make_async_copy(mean, mean_ref, mean_sem)
    mean_out.start()
    rows = rest_ref.reshape(16 * 72, 128)
    sources = [(ref.reshape(16 * 32, 128), 32, 0, 8, lambda h: 8 * h) for ref in (first_ref, second_ref)]
    sources += [(rows, 72, 8 * t, 16, block_half) for t in range(2)]

    def placed():
        top, bottom = moving_times(bounds_ref, w)
        even = w % 2 == 0
        low_time = jnp.where(w == 0, bottom, 1 - bottom)
        high_time = jnp.where(w == 7, top, 1 - top)
        high_at = jnp.where(w == 7, 3, 4) + 4 * w - bounds_ref[high_time, w]
        low_at = jnp.int32(0)
        places = [
            (jnp.where(even, high_time, low_time), jnp.where(even, high_at, low_at)),
            (jnp.where(even, low_time, high_time), jnp.where(even, low_at, high_at)),
        ]
        return places + [(t, 2 + 4 * w - bounds_ref[t, w]) for t in range(2)]

    put_planes(sources, bounds, placed, out_ref, planes, sem)
    mean_out.wait()


def with_rest(bounds, first, second, rest, whole, count):
    kept = pl.BlockSpec(memory_space=pltpu.VMEM)
    there = pl.BlockSpec(memory_space=pltpu.HBM)
    return pl.pallas_call(
        lambda *refs: rest_kernel(count, *refs),
        in_specs=[pl.BlockSpec(memory_space=pl.ANY)] + [kept] * 3 + [there],
        out_specs=[there, there],
        out_shape=[
            jax.ShapeDtypeStruct((72, 2, 6, 16, 128), jnp.float32),
            jax.ShapeDtypeStruct((1, 1), jnp.float32),
        ],
        input_output_aliases={4: 0},
        scratch_shapes=PLANE_SCRATCH + [pltpu.SMEM((1, 1), jnp.float32), pltpu.SemaphoreType.DMA],
        compiler_params=pltpu.CompilerParams(vmem_limit_bytes=VMEM_LIMIT),
    )(bounds, first, second, rest, whole)


def summed(value, steps):
    for axis, by in steps:
        count = lax.axis_size(axis)
        value = value + lax.ppermute(value, axis, [(i, i ^ by) for i in range(count)])
    return value


def spread(payload):
    places = [(gx, gy) for gy in range(4) for gx in range(4)]
    groups = [[(gx * 4 + gy) * 8 + w for gx, gy in places[8 * (w % 2) :] + places[: 8 * (w % 2)]] for w in range(8)]
    return lax.all_to_all(
        payload, ("gx", "gy", "zt"), split_axis=0, concat_axis=0, axis_index_groups=groups, tiled=True
    )


def local(links, bounds):
    held = pltpu.with_memory_space_constraint(links, pltpu.HBM)
    x_face, y_face, z_face, taken, rest = taken_links(held)
    y_face = passed_along(y_face, "gy", -1)
    x_face = passed_along(x_face, "gx", -1)
    payload = encoded(taken)
    payload, links, x_face, y_face, z_face = lax.optimization_barrier((payload, links, x_face, y_face, z_face))
    held = pltpu.with_memory_space_constraint(links, pltpu.HBM)
    moved = spread(payload)
    z_face = passed_along(z_face, "zt", -1)
    plaquette, total = outer_plaquettes(*inner_plaquettes(held, x_face, y_face), z_face)
    total = summed(total, (("zt", 1), ("zt", 2), ("zt", 6)))
    rest = encoded_rest(rest, total)
    moved, rest = lax.optimization_barrier((moved, rest))
    moved_rest = spread(rest)
    first, second = cut_planes(bounds, moved)
    first = lax.ppermute(first, "zt", [(i, i ^ 1) for i in range(8)])
    second = lax.ppermute(second, "zt", [(0, 0), (7, 7)] + [(i, (i + 1 ^ 1) - 1) for i in range(1, 7)])
    file_links = decoded(bounds, moved)
    file_links, mean = with_rest(bounds, first, second, moved_rest, file_links, plaquette.size * 128)
    return file_links.reshape(4, 3, 3, 2, 2, 6, 4, 1, 4, 1, 128), plaquette, mean[0, 0]


def solution(mesh):
    in_specs = (P(None, None, None, None, None, "zt", "gy", "gx"), P())
    out_specs = (
        P(None, None, None, None, None, "zt", None, "gx", None, "gy", None),
        P(None, "zt", "gy", "gx"),
        P(),
    )
    return jax.shard_map(local, mesh=mesh, in_specs=in_specs, out_specs=out_specs, check_vma=False)
```

```python
import jax
import jax.numpy as jnp
from jax import lax
from jax.experimental import pallas as pl
from jax.experimental.pallas import tpu as pltpu
from jax.sharding import PartitionSpec as P

VMEM_LIMIT = 24 * 1024 * 1024
CROSS = ((1, 2), (2, 0), (0, 1))


def passed_along(value, axis, by):
    count = lax.axis_size(axis)
    return lax.ppermute(value, axis, [(i, (i + by) % count) for i in range(count)])


def times(a, b):
    return (a[0] * b[0] - a[1] * b[1], a[0] * b[1] + a[1] * b[0])


def times_conj(a, b):
    return (a[0] * b[0] + a[1] * b[1], a[1] * b[0] - a[0] * b[1])


def minus(a, b):
    return (a[0] - b[0], a[1] - b[1])


def scaled(a, s):
    return (a[0] * s, a[1] * s)


def square(a):
    return a[0] * a[0] + a[1] * a[1]


def last_row(u, v):
    rows = []
    for b, c in CROSS:
        x = minus(times(u[b], v[c]), times(u[c], v[b]))
        rows.append((x[0], -x[1]))
    return rows


def unit_rows(r1, r2):
    n = lax.rsqrt(square(r1[0]) + square(r1[1]) + square(r1[2]))
    u = [scaled(x, n) for x in r1]
    terms = [times_conj(y, x) for x, y in zip(u, r2)]
    c = (terms[0][0] + terms[1][0] + terms[2][0], terms[0][1] + terms[1][1] + terms[2][1])
    v = [minus(y, times(c, x)) for x, y in zip(u, r2)]
    n = lax.rsqrt(square(v[0]) + square(v[1]) + square(v[2]))
    v = [scaled(x, n) for x in v]
    return [u, v, last_row(u, v)]


def angle_value(a):
    t = a[1] / (jnp.abs(a[0]) + jnp.abs(a[1]))
    return jnp.where(a[0] < 0.0, 2.0 - t, t)


def angle_point(t):
    back = t > 1.0
    y = jnp.where(back, 2.0 - t, t)
    x = 1.0 - jnp.abs(y)
    x = jnp.where(back, -x, x)
    return (x, y), x * x + y * y


def to_parameters(r1, r2):
    inverse = 1.0 / square(r1[0])
    p1 = scaled(times_conj(r1[1], r1[0]), inverse)
    p2 = scaled(times_conj(r1[2], r1[0]), inverse)
    s1 = minus(r2[1], times(r2[0], p1))
    s2 = minus(r2[2], times(r2[0], p2))
    q = scaled(times_conj(s2, s1), 1.0 / square(s1))
    return [p1[0], p1[1], p2[0], p2[1], q[0], q[1], angle_value(r1[0]), angle_value(s1)]


def from_parameters(values):
    p1 = (values[0], values[1])
    p2 = (values[2], values[3])
    q = (values[4], values[5])
    size = 1.0 + square(p1) + square(p2)
    g = times_conj(q, p2)
    g = (g[0] + p1[0], g[1] - p1[1])
    gp1 = times(g, p1)
    gp2 = times(g, p2)
    v = [(-g[0], -g[1]), (size - gp1[0], -gp1[1]), (size * q[0] - gp2[0], size * q[1] - gp2[1])]
    a, a2 = angle_point(values[6])
    a = scaled(a, lax.rsqrt(a2 * size))
    b, b2 = angle_point(values[7])
    b = scaled(b, lax.rsqrt(b2 * (square(v[0]) + square(v[1]) + square(v[2]))))
    u = [a, times(a, p1), times(a, p2)]
    v = [times(b, x) for x in v]
    k = scaled(times(a, b), size)
    first = times(k, minus(times(p1, q), p2))
    second = times(k, q)
    return [u, v, [(first[0], -first[1]), (-second[0], second[1]), (k[0], -k[1])]]


ENTRIES = [(r, c, i) for r in range(2) for c in range(3) for i in range(2)]


def pairs(parts):
    return [(parts[2 * i], parts[2 * i + 1]) for i in range(len(parts) // 2)]


def moving_times(bounds_ref, w):
    top = jnp.where(bounds_ref[0, w + 1] < 4 * w + 4, 0, 1)
    bottom = jnp.where(bounds_ref[0, w] > 4 * w, 0, 1)
    return top, bottom


def turned(x, lane):
    odd = (lane & 32) != 0
    far = (lane & 64) != 0
    x = [jnp.where(odd, x[(d + 1) % 4], x[d]) for d in range(4)]
    x = [jnp.where(far, x[(d + 2) % 4], x[d]) for d in range(4)]
    x = [pltpu.roll(x[d], 32 * d, 1) if d else x[d] for d in range(4)]
    x = [jnp.where(odd, x[(1 - g) % 4], x[-g % 4]) for g in range(4)]
    return [jnp.where(far, x[(g + 2) % 4], x[g]) for g in range(4)]


def encode_planes(rows, out, stride):
    lane = lax.broadcasted_iota(jnp.int32, (8, 128), 1)
    low = lax.broadcasted_iota(jnp.int32, (8, 128), 0) < 4
    by_row = []
    for r in range(4):
        parts = pairs([rows[pl.ds(c * 32 + r, 8, stride=4), :] for c in range(12)])
        by_row.append(to_parameters(parts[:3], parts[3:]))
    for p in range(8):
        z = turned([by_row[r][p] for r in range(4)], lane)
        for h in (0, 1):
            first = jnp.where(low, z[2 * h], pltpu.roll(z[2 * h + 1], 4, 0))
            second = jnp.where(low, pltpu.roll(z[2 * h], 4, 0), z[2 * h + 1])
            out[pl.ds(h * 8 * stride + p, 8, stride=stride), :] = first
            out[pl.ds(h * 8 * stride + 8 + p, 8, stride=stride), :] = second


def block_half(h):
    return pl.multiple_of(8 * (h ^ (lax.axis_index("zt") % 2)), 8)


def copies_in(links_ref, m, taken, rest, sem, n):
    rows = pl.ds(0, 2)
    sources = [links_ref.at[m, rows, :, :, t, pl.ds(0, 2)] for t in range(2)] + [links_ref.at[m, rows, :, :, :, 3]]
    copies = [pltpu.make_async_copy(x, taken.at[3 * n + i], sem.at[n, i]) for i, x in enumerate(sources)]
    return copies + [pltpu.make_async_copy(links_ref.at[m, rows, :, :, :, 2], rest.at[n], sem.at[n, 3])]


def encode_kernel(links_ref, taken, out_ref, z_ref, rest_3, taken_3, given, in_sem, z_sem, out_sem):
    copies = copies_in(links_ref, 3, taken_3, rest_3, in_sem, 0)
    copies += [pltpu.make_async_copy(links_ref.at[pl.ds(0, 2), pl.ds(0, 2), :, :, :, 0], z_ref, z_sem)]
    for copy in copies:
        copy.start()

    def copy_out(step, h):
        at = pl.ds(pl.multiple_of((step % 3) * 16, 16), 16)
        return pltpu.make_async_copy(
            given.at[step, pl.ds(8 * h, 8)], out_ref.at[pl.ds(block_half(h), 8), step // 3, at], out_sem.at[h, step]
        )

    def one(source, step):
        encode_planes(source.reshape(12 * 32, 128), given.at[step].reshape(16 * 16, 128), 16)
        copy_out(step, 0).start()
        copy_out(step, 1).start()

    def first(step, carry):
        one(taken.at[step], step)
        return carry

    def second(pair, carry):
        one(taken_3.at[pair], 9 + pair)
        return carry

    lax.fori_loop(0, 9, first, 0)
    for copy in copies:
        copy.wait()
    lax.fori_loop(0, 3, second, 0)
    for step in range(12):
        copy_out(step, 0).wait()
        copy_out(step, 1).wait()


def encoded(links, taken):
    kept = pl.BlockSpec(memory_space=pltpu.VMEM)
    return pl.pallas_call(
        encode_kernel,
        in_specs=[pl.BlockSpec(memory_space=pltpu.HBM), kept],
        out_specs=[pl.BlockSpec(memory_space=pltpu.HBM), kept, kept],
        out_shape=[
            pltpu.HBM((16, 4, 48, 128), jnp.float32),
            pltpu.VMEM((2, 2, 3, 2, 2, 16, 128), jnp.float32),
            pltpu.VMEM((1, 2, 3, 2, 2, 16, 128), jnp.float32),
        ],
        scratch_shapes=[
            pltpu.VMEM((3, 2, 3, 2, 2, 16, 128), jnp.float32),
            pltpu.VMEM((12, 16, 16, 128), jnp.float32),
            pltpu.SemaphoreType.DMA((1, 4)),
            pltpu.SemaphoreType.DMA,
            pltpu.SemaphoreType.DMA((2, 12)),
        ],
        compiler_params=pltpu.CompilerParams(vmem_limit_bytes=VMEM_LIMIT),
    )(links, taken)


class ShiftedRows:
    def __init__(self, ref, by):
        self.ref = ref
        self.by = by

    def __setitem__(self, at, value):
        self.ref[pl.ds(self.by + at[0].start, at[0].size, stride=at[0].stride), :] = value


def encode_rest_kernel(rest, rest_3, total_ref, out_ref, given, out_sem):
    out = given.reshape(16 * 72, 128)
    for n in range(16):
        given[n, pl.ds(64, 8), :] = total_ref[...]

    def copy_out(m, size, h):
        at = pl.ds(pl.multiple_of(m * 16, 8), size)
        return pltpu.make_async_copy(
            given.at[pl.ds(8 * h, 8), at], out_ref.at[pl.ds(block_half(h), 8), at], out_sem.at[h, m]
        )

    copy_out(4, 8, 0).start()
    copy_out(4, 8, 1).start()

    def one(source, m):
        encode_planes(source.reshape(12 * 32, 128), ShiftedRows(out, m * 16), 72)
        copy_out(m, 16, 0).start()
        copy_out(m, 16, 1).start()

    def first(m, carry):
        one(rest.at[m], m)
        return carry

    lax.fori_loop(0, 3, first, 0)
    one(rest_3.at[0], 3)
    for h in range(2):
        for m in range(4):
            copy_out(m, 16, h).wait()
        copy_out(4, 8, h).wait()


def encoded_rest(rest, rest_3, total):
    return pl.pallas_call(
        encode_rest_kernel,
        in_specs=[pl.BlockSpec(memory_space=pltpu.VMEM)] * 3,
        out_specs=pl.BlockSpec(memory_space=pltpu.HBM),
        out_shape=pltpu.HBM((16, 72, 128), jnp.float32),
        scratch_shapes=[pltpu.VMEM((16, 72, 128), jnp.float32), pltpu.SemaphoreType.DMA((2, 5))],
        compiler_params=pltpu.CompilerParams(vmem_limit_bytes=VMEM_LIMIT),
    )(rest, rest_3, total)


def take_kernel(links_ref, x_ref, y_ref, taken, rest, in_sem):
    order = (2, 1, 0)
    copies = {m: copies_in(links_ref, m, taken, rest, in_sem, m) for m in order}
    for m in order:
        for copy in copies[m]:
            copy.start()

    def rows(m, r, c, i, k, start, size):
        t, z = k // 4, k % 4
        at = pl.ds(start, size)
        if z == 2:
            return rest[m, r, c, i, t, at, :]
        if z == 3:
            return taken[3 * m + 2, r, c, i, t, at, :]
        return taken[3 * m + t, r, c, i, z, at, :]

    def row_face(m):
        parts = pairs([jnp.concatenate([rows(m, *e, k, 0, 1) for k in range(8)], axis=0) for e in ENTRIES])
        for p, value in enumerate(to_parameters(parts[:3], parts[3:])):
            y_ref[m // 2, p] = value

    lane = lax.broadcasted_iota(jnp.int32, (8, 128), 1)
    got = [None] * 3

    def column_face(m):
        for e, entry in enumerate(ENTRIES):
            n = 12 * (m - 1) + e
            for k in range(8):
                for h in range(2):
                    at = 16 * (n % 8) + 2 * k + h
                    value = rows(m, *entry, k, 8 * h, 8)
                    value = pltpu.roll(value, at, 1) if at else value
                    got[n // 8] = value if got[n // 8] is None else jnp.where(lane == at, value, got[n // 8])

    for m in order:
        for copy in copies[m]:
            copy.wait()
        if m in (1, 2):
            column_face(m)
        if m in (0, 2):
            row_face(m)
    for n in range(3):
        x_ref[n] = got[n]


def taken_links(links):
    kept = pl.BlockSpec(memory_space=pltpu.VMEM)
    return pl.pallas_call(
        take_kernel,
        in_specs=[pl.BlockSpec(memory_space=pltpu.HBM)],
        out_specs=[kept] * 4,
        out_shape=[
            pltpu.VMEM((3, 8, 128), jnp.float32),
            pltpu.VMEM((2, 8, 8, 128), jnp.float32),
            pltpu.VMEM((9, 2, 3, 2, 2, 16, 128), jnp.float32),
            pltpu.VMEM((3, 2, 3, 2, 2, 16, 128), jnp.float32),
        ],
        scratch_shapes=[pltpu.SemaphoreType.DMA((3, 4))],
        compiler_params=pltpu.CompilerParams(vmem_limit_bytes=VMEM_LIMIT),
    )(links)


def flat_rows(matrix):
    return [part for row in matrix for entry in row for part in entry]


def product_trace(a, b, c, d):
    total = None
    for i in range(3):
        for j in range(3):
            one = two = None
            for k in range(3):
                x = times(a[i][k], b[k][j])
                y = times(c[i][k], d[k][j])
                one = x if one is None else (one[0] + x[0], one[1] + x[1])
                two = y if two is None else (two[0] + y[0], two[1] + y[1])
            term = one[0] * two[0] + one[1] * two[1]
            total = term if total is None else total + term
    return total


class Sites:
    def __init__(self, unit, x_edge, y_edge, z_edge, out_ref):
        self.unit, self.x_edge, self.y_edge, self.z_edge = unit, x_edge, y_edge, z_edge
        self.out_ref = out_ref
        self.last_lane = lax.broadcasted_iota(jnp.int32, (8, 128), 1) == 127
        self.first_row = lax.broadcasted_iota(jnp.int32, (8, 128), 0) == 0

    def matrix(self, parts):
        parts = pairs(parts)
        return [parts[3 * i : 3 * i + 3] for i in range(3)]

    def here(self, m, t, z, h):
        return self.matrix([self.unit[m, c, t, z, pl.ds(8 * h, 8), :] for c in range(18)])

    def next_x(self, m, t, z, h):
        got = []
        for c in range(18):
            value = pltpu.roll(self.unit[m, c, t, z, pl.ds(8 * h, 8), :], 127, 1)
            beyond = pltpu.roll(self.x_edge[m - 1, c], 127 - 2 * (4 * t + z) - h, 1)
            got.append(jnp.where(self.last_lane, beyond, value))
        return self.matrix(got)

    def next_y(self, m, t, z, h):
        if h == 0:
            return self.matrix([self.unit[m, c, t, z, pl.ds(1, 8), :] for c in range(18)])
        got = []
        for c in range(18):
            value = self.unit[m, c, t, z, pl.ds(8, 8), :]
            beyond = self.y_edge[m // 2, c, pl.ds(4 * t + z, 1), :]
            value = jnp.where(self.first_row, beyond, value)
            got.append(pltpu.roll(value, 7, 0))
        return self.matrix(got)

    def next_z(self, m, t, z, h):
        if self.z_edge is None:
            return self.here(m, t, z + 1, h)
        return self.matrix([self.z_edge[m, c, t, pl.ds(8 * h, 8), :] for c in range(18)])

    def plane(self, t, z):
        total = None
        for h in range(2):
            at = (t, z, h)
            value = product_trace(self.here(0, *at), self.next_x(1, *at), self.here(1, *at), self.next_y(0, *at))
            value = value + product_trace(
                self.here(0, *at), self.next_x(2, *at), self.here(2, *at), self.next_z(0, *at)
            )
            value = value + product_trace(
                self.here(1, *at), self.next_y(2, *at), self.here(2, *at), self.next_z(1, *at)
            )
            value = value * (1.0 / 9.0)
            self.out_ref[t, z, pl.ds(8 * h, 8), :] = value
            total = value if total is None else total + value
        return total


def inner_kernel(links_ref, x_ref, y_ref, out_ref, sum_ref, unit, x_edge, y_edge, taken, sem):
    def copy_in(step):
        return pltpu.make_async_copy(
            links_ref.at[step // 2, pl.ds(0, 2), :, :, step % 2], taken.at[step], sem.at[step]
        )

    for step in range(6):
        copy_in(step).start()
    for m in range(2):
        for c, value in enumerate(flat_rows(from_parameters([y_ref[m, p] for p in range(8)]))):
            y_edge[m, c] = value
        parts = []
        for e in range(12):
            n = 12 * m + e
            value = x_ref[n // 8]
            parts.append(pltpu.roll(value, 128 - 16 * (n % 8), 1) if n % 8 else value)
        parts = pairs(parts)
        for c, value in enumerate(flat_rows(unit_rows(parts[:3], parts[3:]))):
            x_edge[m, c] = value

    def own(step, carry):
        part = step // 4
        z = step % 4

        @pl.when(z == 0)
        def _():
            copy_in(part).wait()

        for h in range(2):
            at = pl.ds(8 * h, 8)
            parts = pairs([taken[part, r, c, i, z, at, :] for r, c, i in ENTRIES])
            for c, value in enumerate(flat_rows(unit_rows(parts[:3], parts[3:]))):
                unit[part // 2, c, part % 2, z, at, :] = value
        return carry

    lax.fori_loop(0, 24, own, 0)
    sites = Sites(unit, x_edge, y_edge, None, out_ref)
    zero = jnp.zeros((8, 128), jnp.float32)
    sum_ref[...] = lax.fori_loop(0, 6, lambda step, total: total + sites.plane(step // 3, step % 3), zero)


def inner_plaquettes(links, x_face, y_face):
    kept = pl.BlockSpec(memory_space=pltpu.VMEM)
    return pl.pallas_call(
        inner_kernel,
        in_specs=[pl.BlockSpec(memory_space=pltpu.HBM)] + [kept] * 2,
        out_specs=[kept] * 5,
        out_shape=[
            pltpu.VMEM((2, 4, 16, 128), jnp.float32),
            pltpu.VMEM((8, 128), jnp.float32),
            pltpu.VMEM((3, 18, 2, 4, 16, 128), jnp.float32),
            pltpu.VMEM((2, 18, 8, 128), jnp.float32),
            pltpu.VMEM((2, 18, 8, 128), jnp.float32),
        ],
        scratch_shapes=[
            pltpu.VMEM((6, 2, 3, 2, 4, 16, 128), jnp.float32),
            pltpu.SemaphoreType.DMA((6,)),
        ],
        compiler_params=pltpu.CompilerParams(vmem_limit_bytes=VMEM_LIMIT),
    )(links, x_face, y_face)


def outer_kernel(inner_ref, part_ref, unit, x_edge, y_edge, z_ref, out_ref, sum_ref, z_edge):
    for t in range(2):
        for z in range(3):
            out_ref[t, z] = inner_ref[t, z]

    def above(step, carry):
        m = step // 2
        t = step % 2
        for h in range(2):
            at = pl.ds(8 * h, 8)
            parts = pairs([z_ref[m, r, c, i, t, at, :] for r, c, i in ENTRIES])
            for c, value in enumerate(flat_rows(unit_rows(parts[:3], parts[3:]))):
                z_edge[m, c, t, at, :] = value
        return carry

    lax.fori_loop(0, 4, above, 0)
    sites = Sites(unit, x_edge, y_edge, z_edge, out_ref)
    total = lax.fori_loop(0, 2, lambda t, total: total + sites.plane(t, 3), part_ref[...])
    sum_ref[...] = jnp.broadcast_to(jnp.sum(total, keepdims=True), (8, 128))


def outer_plaquettes(inner, part, unit, x_edge, y_edge, z_face):
    kept = pl.BlockSpec(memory_space=pltpu.VMEM)
    return pl.pallas_call(
        outer_kernel,
        in_specs=[kept] * 6,
        out_shape=[
            jax.ShapeDtypeStruct((2, 4, 16, 128), jnp.float32),
            jax.ShapeDtypeStruct((8, 128), jnp.float32),
        ],
        scratch_shapes=[pltpu.VMEM((2, 18, 2, 16, 128), jnp.float32)],
        compiler_params=pltpu.CompilerParams(vmem_limit_bytes=VMEM_LIMIT),
    )(inner, part, unit, x_edge, y_edge, z_face)


def put_planes(sources, bounds, placed, out_ref, planes, sem):
    def copy_out(places, part, m):
        t, j = places[part]
        return pltpu.make_async_copy(planes.at[part, m], out_ref.at[pl.ds(18 * m, 18), t, j], sem.at[part, m])

    def decode(part, m):
        rows, stride, start, step, half = sources[part]
        for h in range(2):
            at = half(h) * stride + start + m * step
            values = [rows[pl.ds(at + p, 8, stride=stride), :] for p in range(8)]
            for c, value in enumerate(flat_rows(from_parameters(values))):
                planes[part, m, c, pl.ds(8 * h, 8), :] = value

    parts = range(len(sources))
    for part in parts:
        decode(part, 0)
    if bounds is not None:
        bounds.wait()
    places = placed()
    for part in parts:
        copy_out(places, part, 0).start()

    def one(m, carry):
        for part in parts:
            decode(part, m)
            copy_out(places, part, m).start()
        return carry

    lax.fori_loop(1, 4, one, 0)
    for m in range(4):
        for part in parts:
            copy_out(places, part, m).wait()


PLANE_SCRATCH = [
    pltpu.VMEM((4, 4, 18, 16, 128), jnp.float32),
    pltpu.SemaphoreType.DMA((4, 4)),
    pltpu.SMEM((2, 9), jnp.int32),
    pltpu.SemaphoreType.DMA,
]


def decode_kernel(bounds_in, own_ref, out_ref, planes, sem, bounds_ref, bounds_sem, zeros, zero_sem):
    bounds = pltpu.make_async_copy(bounds_in, bounds_ref, bounds_sem)
    bounds.start()
    w = lax.axis_index("zt")
    zeros[...] = jnp.zeros((18, 16, 128), jnp.float32)

    def fill(t, j, m):
        return pltpu.make_async_copy(zeros, out_ref.at[pl.ds(18 * m, 18), t, j], zero_sem.at[t, j - 2])

    def every_empty(act):
        for t in range(2):
            depth = bounds_ref[t, w + 1] - bounds_ref[t, w]
            for j in range(2, 6):

                @pl.when(j >= depth)
                def _(t=t, j=j):
                    for m in range(4):
                        act(fill(t, j, m))

    bounds.wait()
    every_empty(lambda copy: copy.start())
    top, bottom = moving_times(bounds_ref, w)
    rows = own_ref.reshape(16 * 192, 128)
    planes_in = ((1 - top, 3, 5 - top), (1 - bottom, 0, 2 - 2 * bottom), (0, 1, 1), (1, 1, 3))
    sources = [(rows, 192, 8 * slot, 48, block_half) for t, z, slot in planes_in]
    places = [(t, z + 4 * w - bounds_ref[t, w]) for t, z, slot in planes_in]
    put_planes(sources, None, lambda: places, out_ref, planes, sem)
    every_empty(lambda copy: copy.wait())


def decoded(bounds, own):
    return pl.pallas_call(
        decode_kernel,
        in_specs=[pl.BlockSpec(memory_space=pl.ANY), pl.BlockSpec(memory_space=pltpu.VMEM)],
        out_specs=pl.BlockSpec(memory_space=pltpu.HBM),
        out_shape=jax.ShapeDtypeStruct((72, 2, 6, 16, 128), jnp.float32),
        scratch_shapes=PLANE_SCRATCH
        + [pltpu.VMEM((18, 16, 128), jnp.float32), pltpu.SemaphoreType.DMA((2, 4))],
        compiler_params=pltpu.CompilerParams(vmem_limit_bytes=VMEM_LIMIT),
    )(bounds, own)


def cut_kernel(bounds_ref, own_ref, first_ref, second_ref):
    w = lax.axis_index("zt")
    top, bottom = moving_times(bounds_ref, w)
    even = w % 2 == 0
    top = 32 + 8 * top
    bottom = 16 * bottom
    first = pl.multiple_of(jnp.where(even, top, bottom), 8)
    second = pl.multiple_of(jnp.where(even, bottom, top), 8)
    for h in range(2):
        here = pl.ds(8 * h, 8)
        there = pl.ds(block_half(h), 8)
        for m in range(4):
            first_ref[here, m] = own_ref[there, m, pl.ds(first, 8), :]
            second_ref[here, m] = own_ref[there, m, pl.ds(second, 8), :]


def cut_planes(bounds, own):
    return pl.pallas_call(
        cut_kernel,
        in_specs=[pl.BlockSpec(memory_space=pltpu.SMEM), pl.BlockSpec(memory_space=pltpu.VMEM)],
        out_shape=[jax.ShapeDtypeStruct((16, 4, 8, 128), jnp.float32)] * 2,
        compiler_params=pltpu.CompilerParams(vmem_limit_bytes=VMEM_LIMIT),
    )(bounds, own)


def rest_kernel(
    count,
    bounds_in,
    first_ref,
    second_ref,
    rest_ref,
    whole_ref,
    out_ref,
    mean_ref,
    planes,
    sem,
    bounds_ref,
    bounds_sem,
    mean,
    mean_sem,
):
    bounds = pltpu.make_async_copy(bounds_in, bounds_ref, bounds_sem)
    bounds.start()
    w = lax.axis_index("zt")
    totals = []
    for h in range(2):
        part = rest_ref[block_half(h), pl.ds(64, 8), :]
        for n in range(1, 8):
            part = part + rest_ref[block_half(h) + n, pl.ds(64, 8), :]
        totals.append(part)
    mean[0, 0] = jnp.max(totals[0] + totals[1]) * (1.0 / count)
    mean_out = pltpu.make_async_copy(mean, mean_ref, mean_sem)
    mean_out.start()
    rows = rest_ref.reshape(16 * 72, 128)
    sources = [(ref.reshape(16 * 32, 128), 32, 0, 8, lambda h: 8 * h) for ref in (first_ref, second_ref)]
    sources += [(rows, 72, 8 * t, 16, block_half) for t in range(2)]

    def placed():
        top, bottom = moving_times(bounds_ref, w)
        even = w % 2 == 0
        low_time = jnp.where(w == 0, bottom, 1 - bottom)
        high_time = jnp.where(w == 7, top, 1 - top)
        high_at = jnp.where(w == 7, 3, 4) + 4 * w - bounds_ref[high_time, w]
        low_at = jnp.int32(0)
        places = [
            (jnp.where(even, high_time, low_time), jnp.where(even, high_at, low_at)),
            (jnp.where(even, low_time, high_time), jnp.where(even, low_at, high_at)),
        ]
        return places + [(t, 2 + 4 * w - bounds_ref[t, w]) for t in range(2)]

    put_planes(sources, bounds, placed, out_ref, planes, sem)
    mean_out.wait()


def with_rest(bounds, first, second, rest, whole, count):
    kept = pl.BlockSpec(memory_space=pltpu.VMEM)
    there = pl.BlockSpec(memory_space=pltpu.HBM)
    return pl.pallas_call(
        lambda *refs: rest_kernel(count, *refs),
        in_specs=[pl.BlockSpec(memory_space=pl.ANY)] + [kept] * 3 + [there],
        out_specs=[there, there],
        out_shape=[
            jax.ShapeDtypeStruct((72, 2, 6, 16, 128), jnp.float32),
            jax.ShapeDtypeStruct((1, 1), jnp.float32),
        ],
        input_output_aliases={4: 0},
        scratch_shapes=PLANE_SCRATCH + [pltpu.SMEM((1, 1), jnp.float32), pltpu.SemaphoreType.DMA],
        compiler_params=pltpu.CompilerParams(vmem_limit_bytes=VMEM_LIMIT),
    )(bounds, first, second, rest, whole)


def summed(value, steps):
    for axis, by in steps:
        count = lax.axis_size(axis)
        value = value + lax.ppermute(value, axis, [(i, i ^ by) for i in range(count)])
    return value


def spread(payload):
    places = [(gx, gy) for gy in range(4) for gx in range(4)]
    groups = [[(gx * 4 + gy) * 8 + w for gx, gy in places[8 * (w % 2) :] + places[: 8 * (w % 2)]] for w in range(8)]
    return lax.all_to_all(
        payload, ("gx", "gy", "zt"), split_axis=0, concat_axis=0, axis_index_groups=groups, tiled=True
    )


def local(links, bounds):
    held = pltpu.with_memory_space_constraint(links, pltpu.HBM)
    x_face, y_face, taken, rest = taken_links(held)
    y_face = passed_along(y_face, "gy", -1)
    x_face = passed_along(x_face, "gx", -1)
    payload, z_face, rest_3 = encoded(held, taken)
    payload, links, x_face, y_face, z_face = lax.optimization_barrier((payload, links, x_face, y_face, z_face))
    held = pltpu.with_memory_space_constraint(links, pltpu.HBM)
    moved = spread(payload)
    z_face = passed_along(z_face, "zt", -1)
    plaquette, total = outer_plaquettes(*inner_plaquettes(held, x_face, y_face), z_face)
    total = summed(total, (("zt", 1), ("zt", 2), ("zt", 6)))
    rest = encoded_rest(rest, rest_3, total)
    moved, rest = lax.optimization_barrier((moved, rest))
    moved_rest = spread(rest)
    first, second = cut_planes(bounds, moved)
    first = lax.ppermute(first, "zt", [(i, i ^ 1) for i in range(8)])
    second = lax.ppermute(second, "zt", [(0, 0), (7, 7)] + [(i, (i + 1 ^ 1) - 1) for i in range(1, 7)])
    file_links = decoded(bounds, moved)
    file_links, mean = with_rest(bounds, first, second, moved_rest, file_links, plaquette.size * 128)
    return file_links.reshape(4, 3, 3, 2, 2, 6, 4, 1, 4, 1, 128), plaquette, mean[0, 0]


def solution(mesh):
    in_specs = (P(None, None, None, None, None, "zt", "gy", "gx"), P())
    out_specs = (
        P(None, None, None, None, None, "zt", None, "gx", None, "gy", None),
        P(None, "zt", "gy", "gx"),
        P(),
    )
    return jax.shard_map(local, mesh=mesh, in_specs=in_specs, out_specs=out_specs, check_vma=False)
```

```python
import jax
import jax.numpy as jnp
from jax import lax
from jax.experimental import pallas as pl
from jax.experimental.pallas import tpu as pltpu
from jax.sharding import PartitionSpec as P

VMEM_LIMIT = 24 * 1024 * 1024
CROSS = ((1, 2), (2, 0), (0, 1))


def passed_along(value, axis, by):
    count = lax.axis_size(axis)
    return lax.ppermute(value, axis, [(i, (i + by) % count) for i in range(count)])


def times(a, b):
    return (a[0] * b[0] - a[1] * b[1], a[0] * b[1] + a[1] * b[0])


def times_conj(a, b):
    return (a[0] * b[0] + a[1] * b[1], a[1] * b[0] - a[0] * b[1])


def minus(a, b):
    return (a[0] - b[0], a[1] - b[1])


def scaled(a, s):
    return (a[0] * s, a[1] * s)


def square(a):
    return a[0] * a[0] + a[1] * a[1]


def last_row(u, v):
    rows = []
    for b, c in CROSS:
        x = minus(times(u[b], v[c]), times(u[c], v[b]))
        rows.append((x[0], -x[1]))
    return rows


def unit_rows(r1, r2):
    n = lax.rsqrt(square(r1[0]) + square(r1[1]) + square(r1[2]))
    u = [scaled(x, n) for x in r1]
    terms = [times_conj(y, x) for x, y in zip(u, r2)]
    c = (terms[0][0] + terms[1][0] + terms[2][0], terms[0][1] + terms[1][1] + terms[2][1])
    v = [minus(y, times(c, x)) for x, y in zip(u, r2)]
    n = lax.rsqrt(square(v[0]) + square(v[1]) + square(v[2]))
    v = [scaled(x, n) for x in v]
    return [u, v, last_row(u, v)]


def angle_value(a):
    t = a[1] / (jnp.abs(a[0]) + jnp.abs(a[1]))
    return jnp.where(a[0] < 0.0, 2.0 - t, t)


def angle_point(t):
    back = t > 1.0
    y = jnp.where(back, 2.0 - t, t)
    x = 1.0 - jnp.abs(y)
    x = jnp.where(back, -x, x)
    return (x, y), x * x + y * y


def to_parameters(r1, r2):
    inverse = 1.0 / square(r1[0])
    p1 = scaled(times_conj(r1[1], r1[0]), inverse)
    p2 = scaled(times_conj(r1[2], r1[0]), inverse)
    s1 = minus(r2[1], times(r2[0], p1))
    s2 = minus(r2[2], times(r2[0], p2))
    q = scaled(times_conj(s2, s1), 1.0 / square(s1))
    return [p1[0], p1[1], p2[0], p2[1], q[0], q[1], angle_value(r1[0]), angle_value(s1)]


def from_parameters(values):
    p1 = (values[0], values[1])
    p2 = (values[2], values[3])
    q = (values[4], values[5])
    size = 1.0 + square(p1) + square(p2)
    g = times_conj(q, p2)
    g = (g[0] + p1[0], g[1] - p1[1])
    gp1 = times(g, p1)
    gp2 = times(g, p2)
    v = [(-g[0], -g[1]), (size - gp1[0], -gp1[1]), (size * q[0] - gp2[0], size * q[1] - gp2[1])]
    a, a2 = angle_point(values[6])
    a = scaled(a, lax.rsqrt(a2 * size))
    b, b2 = angle_point(values[7])
    b = scaled(b, lax.rsqrt(b2 * (square(v[0]) + square(v[1]) + square(v[2]))))
    u = [a, times(a, p1), times(a, p2)]
    v = [times(b, x) for x in v]
    k = scaled(times(a, b), size)
    first = times(k, minus(times(p1, q), p2))
    second = times(k, q)
    return [u, v, [(first[0], -first[1]), (-second[0], second[1]), (k[0], -k[1])]]


ENTRIES = [(r, c, i) for r in range(2) for c in range(3) for i in range(2)]


def pairs(parts):
    return [(parts[2 * i], parts[2 * i + 1]) for i in range(len(parts) // 2)]


def moving_times(bounds_ref, w):
    top = jnp.where(bounds_ref[0, w + 1] < 4 * w + 4, 0, 1)
    bottom = jnp.where(bounds_ref[0, w] > 4 * w, 0, 1)
    return top, bottom


def turned(x, lane):
    odd = (lane & 32) != 0
    far = (lane & 64) != 0
    x = [jnp.where(odd, x[(d + 1) % 4], x[d]) for d in range(4)]
    x = [jnp.where(far, x[(d + 2) % 4], x[d]) for d in range(4)]
    x = [pltpu.roll(x[d], 32 * d, 1) if d else x[d] for d in range(4)]
    x = [jnp.where(odd, x[(1 - g) % 4], x[-g % 4]) for g in range(4)]
    return [jnp.where(far, x[(g + 2) % 4], x[g]) for g in range(4)]


def encode_planes(rows, out, stride):
    lane = lax.broadcasted_iota(jnp.int32, (8, 128), 1)
    low = lax.broadcasted_iota(jnp.int32, (8, 128), 0) < 4
    by_row = []
    for r in range(4):
        parts = pairs([rows[pl.ds(c * 32 + r, 8, stride=4), :] for c in range(12)])
        by_row.append(to_parameters(parts[:3], parts[3:]))
    for p in range(8):
        z = turned([by_row[r][p] for r in range(4)], lane)
        for h in (0, 1):
            first = jnp.where(low, z[2 * h], pltpu.roll(z[2 * h + 1], 4, 0))
            second = jnp.where(low, pltpu.roll(z[2 * h], 4, 0), z[2 * h + 1])
            out[pl.ds(h * 8 * stride + p, 8, stride=stride), :] = first
            out[pl.ds(h * 8 * stride + 8 + p, 8, stride=stride), :] = second


def block_half(h):
    return pl.multiple_of(8 * (h ^ (lax.axis_index("zt") % 2)), 8)


def copies_in(links_ref, m, taken, rest, sem, n):
    rows = pl.ds(0, 2)
    sources = [links_ref.at[m, rows, :, :, t, pl.ds(0, 2)] for t in range(2)] + [links_ref.at[m, rows, :, :, :, 3]]
    copies = [pltpu.make_async_copy(x, taken.at[3 * n + i], sem.at[n, i]) for i, x in enumerate(sources)]
    return copies + [pltpu.make_async_copy(links_ref.at[m, rows, :, :, :, 2], rest.at[n], sem.at[n, 3])]


def encode_kernel(links_ref, taken, out_ref, z_ref, rest_3, taken_3, given, in_sem, z_sem, out_sem):
    copies = copies_in(links_ref, 3, taken_3, rest_3, in_sem, 0)
    copies += [pltpu.make_async_copy(links_ref.at[pl.ds(0, 2), pl.ds(0, 2), :, :, :, 0], z_ref, z_sem)]
    for copy in copies:
        copy.start()

    def copy_out(step, h):
        at = pl.ds(pl.multiple_of((step % 3) * 16, 16), 16)
        return pltpu.make_async_copy(
            given.at[step, pl.ds(8 * h, 8)], out_ref.at[pl.ds(block_half(h), 8), step // 3, at], out_sem.at[h, step]
        )

    def one(source, step):
        encode_planes(source.reshape(12 * 32, 128), given.at[step].reshape(16 * 16, 128), 16)
        copy_out(step, 0).start()
        copy_out(step, 1).start()

    def first(step, carry):
        one(taken.at[step], step)
        return carry

    def second(pair, carry):
        one(taken_3.at[pair], 9 + pair)
        return carry

    lax.fori_loop(0, 9, first, 0)
    for copy in copies:
        copy.wait()
    lax.fori_loop(0, 3, second, 0)
    for step in range(12):
        copy_out(step, 0).wait()
        copy_out(step, 1).wait()


def encoded(links, taken):
    kept = pl.BlockSpec(memory_space=pltpu.VMEM)
    return pl.pallas_call(
        encode_kernel,
        in_specs=[pl.BlockSpec(memory_space=pltpu.HBM), kept],
        out_specs=[pl.BlockSpec(memory_space=pltpu.HBM), kept, kept],
        out_shape=[
            pltpu.HBM((16, 4, 48, 128), jnp.float32),
            pltpu.VMEM((2, 2, 3, 2, 2, 16, 128), jnp.float32),
            pltpu.VMEM((1, 2, 3, 2, 2, 16, 128), jnp.float32),
        ],
        scratch_shapes=[
            pltpu.VMEM((3, 2, 3, 2, 2, 16, 128), jnp.float32),
            pltpu.VMEM((12, 16, 16, 128), jnp.float32),
            pltpu.SemaphoreType.DMA((1, 4)),
            pltpu.SemaphoreType.DMA,
            pltpu.SemaphoreType.DMA((2, 12)),
        ],
        compiler_params=pltpu.CompilerParams(vmem_limit_bytes=VMEM_LIMIT),
    )(links, taken)


class ShiftedRows:
    def __init__(self, ref, by):
        self.ref = ref
        self.by = by

    def __setitem__(self, at, value):
        self.ref[pl.ds(self.by + at[0].start, at[0].size, stride=at[0].stride), :] = value


def encode_rest_kernel(rest, rest_3, total_ref, out_ref, given, out_sem):
    out = given.reshape(16 * 72, 128)
    for n in range(16):
        given[n, pl.ds(64, 8), :] = total_ref[...]

    def copy_out(m, size, h):
        at = pl.ds(pl.multiple_of(m * 16, 8), size)
        return pltpu.make_async_copy(
            given.at[pl.ds(8 * h, 8), at], out_ref.at[pl.ds(block_half(h), 8), at], out_sem.at[h, m]
        )

    copy_out(4, 8, 0).start()
    copy_out(4, 8, 1).start()

    def one(source, m):
        encode_planes(source.reshape(12 * 32, 128), ShiftedRows(out, m * 16), 72)
        copy_out(m, 16, 0).start()
        copy_out(m, 16, 1).start()

    def first(m, carry):
        one(rest.at[m], m)
        return carry

    lax.fori_loop(0, 3, first, 0)
    one(rest_3.at[0], 3)
    for h in range(2):
        for m in range(4):
            copy_out(m, 16, h).wait()
        copy_out(4, 8, h).wait()


def encoded_rest(rest, rest_3, total):
    return pl.pallas_call(
        encode_rest_kernel,
        in_specs=[pl.BlockSpec(memory_space=pltpu.VMEM)] * 3,
        out_specs=pl.BlockSpec(memory_space=pltpu.HBM),
        out_shape=pltpu.HBM((16, 72, 128), jnp.float32),
        scratch_shapes=[pltpu.VMEM((16, 72, 128), jnp.float32), pltpu.SemaphoreType.DMA((2, 5))],
        compiler_params=pltpu.CompilerParams(vmem_limit_bytes=VMEM_LIMIT),
    )(rest, rest_3, total)


def take_kernel(links_ref, x_ref, y_ref, taken, rest, in_sem):
    order = (2, 1, 0)
    copies = {m: copies_in(links_ref, m, taken, rest, in_sem, m) for m in order}
    for m in order:
        for copy in copies[m]:
            copy.start()

    def rows(m, r, c, i, k, start, size):
        t, z = k // 4, k % 4
        at = pl.ds(start, size)
        if z == 2:
            return rest[m, r, c, i, t, at, :]
        if z == 3:
            return taken[3 * m + 2, r, c, i, t, at, :]
        return taken[3 * m + t, r, c, i, z, at, :]

    def row_face(m):
        parts = pairs([jnp.concatenate([rows(m, *e, k, 0, 1) for k in range(8)], axis=0) for e in ENTRIES])
        for p, value in enumerate(to_parameters(parts[:3], parts[3:])):
            y_ref[m // 2, p] = value

    lane = lax.broadcasted_iota(jnp.int32, (8, 128), 1)
    got = [None] * 3

    def column_face(m):
        for e, entry in enumerate(ENTRIES):
            n = 12 * (m - 1) + e
            for k in range(8):
                for h in range(2):
                    at = 16 * (n % 8) + 2 * k + h
                    value = rows(m, *entry, k, 8 * h, 8)
                    value = pltpu.roll(value, at, 1) if at else value
                    got[n // 8] = value if got[n // 8] is None else jnp.where(lane == at, value, got[n // 8])

    for m in order:
        for copy in copies[m]:
            copy.wait()
        if m in (1, 2):
            column_face(m)
        if m in (0, 2):
            row_face(m)
    for n in range(3):
        x_ref[n] = got[n]


def taken_links(links):
    kept = pl.BlockSpec(memory_space=pltpu.VMEM)
    return pl.pallas_call(
        take_kernel,
        in_specs=[pl.BlockSpec(memory_space=pltpu.HBM)],
        out_specs=[kept] * 4,
        out_shape=[
            pltpu.VMEM((3, 8, 128), jnp.float32),
            pltpu.VMEM((2, 8, 8, 128), jnp.float32),
            pltpu.VMEM((9, 2, 3, 2, 2, 16, 128), jnp.float32),
            pltpu.VMEM((3, 2, 3, 2, 2, 16, 128), jnp.float32),
        ],
        scratch_shapes=[pltpu.SemaphoreType.DMA((3, 4))],
        compiler_params=pltpu.CompilerParams(vmem_limit_bytes=VMEM_LIMIT),
    )(links)


def flat_rows(matrix):
    return [part for row in matrix for entry in row for part in entry]


def product_trace(a, b, c, d):
    total = None
    for i in range(3):
        for j in range(3):
            one = two = None
            for k in range(3):
                x = times(a[i][k], b[k][j])
                y = times(c[i][k], d[k][j])
                one = x if one is None else (one[0] + x[0], one[1] + x[1])
                two = y if two is None else (two[0] + y[0], two[1] + y[1])
            term = one[0] * two[0] + one[1] * two[1]
            total = term if total is None else total + term
    return total


class Sites:
    def __init__(self, unit, x_edge, y_edge, z_edge, out_ref):
        self.unit, self.x_edge, self.y_edge, self.z_edge = unit, x_edge, y_edge, z_edge
        self.out_ref = out_ref
        self.last_lane = lax.broadcasted_iota(jnp.int32, (8, 128), 1) == 127
        self.first_row = lax.broadcasted_iota(jnp.int32, (8, 128), 0) == 0

    def matrix(self, parts):
        parts = pairs(parts)
        return [parts[3 * i : 3 * i + 3] for i in range(3)]

    def here(self, m, t, z, h):
        return self.matrix([self.unit[m, c, t, z, pl.ds(8 * h, 8), :] for c in range(18)])

    def next_x(self, m, t, z, h):
        got = []
        for c in range(18):
            value = pltpu.roll(self.unit[m, c, t, z, pl.ds(8 * h, 8), :], 127, 1)
            beyond = pltpu.roll(self.x_edge[m - 1, c], 127 - 2 * (4 * t + z) - h, 1)
            got.append(jnp.where(self.last_lane, beyond, value))
        return self.matrix(got)

    def next_y(self, m, t, z, h):
        if h == 0:
            return self.matrix([self.unit[m, c, t, z, pl.ds(1, 8), :] for c in range(18)])
        got = []
        for c in range(18):
            value = self.unit[m, c, t, z, pl.ds(8, 8), :]
            beyond = self.y_edge[m // 2, c, pl.ds(4 * t + z, 1), :]
            value = jnp.where(self.first_row, beyond, value)
            got.append(pltpu.roll(value, 7, 0))
        return self.matrix(got)

    def next_z(self, m, t, z, h):
        if self.z_edge is None:
            return self.here(m, t, z + 1, h)
        return self.matrix([self.z_edge[m, c, t, pl.ds(8 * h, 8), :] for c in range(18)])

    def plane(self, t, z):
        total = None
        for h in range(2):
            at = (t, z, h)
            value = product_trace(self.here(0, *at), self.next_x(1, *at), self.here(1, *at), self.next_y(0, *at))
            value = value + product_trace(
                self.here(0, *at), self.next_x(2, *at), self.here(2, *at), self.next_z(0, *at)
            )
            value = value + product_trace(
                self.here(1, *at), self.next_y(2, *at), self.here(2, *at), self.next_z(1, *at)
            )
            value = value * (1.0 / 9.0)
            self.out_ref[t, z, pl.ds(8 * h, 8), :] = value
            total = value if total is None else total + value
        return total


def inner_kernel(links_ref, x_ref, y_ref, out_ref, sum_ref, unit, x_edge, y_edge, taken, sem):
    def copy_in(step):
        return pltpu.make_async_copy(
            links_ref.at[step // 2, pl.ds(0, 2), :, :, step % 2], taken.at[step], sem.at[step]
        )

    for step in range(6):
        copy_in(step).start()
    for m in range(2):
        for c, value in enumerate(flat_rows(from_parameters([y_ref[m, p] for p in range(8)]))):
            y_edge[m, c] = value
        parts = []
        for e in range(12):
            n = 12 * m + e
            value = x_ref[n // 8]
            parts.append(pltpu.roll(value, 128 - 16 * (n % 8), 1) if n % 8 else value)
        parts = pairs(parts)
        for c, value in enumerate(flat_rows(unit_rows(parts[:3], parts[3:]))):
            x_edge[m, c] = value

    def own(step, carry):
        part = step // 4
        z = step % 4

        @pl.when(z == 0)
        def _():
            copy_in(part).wait()

        for h in range(2):
            at = pl.ds(8 * h, 8)
            parts = pairs([taken[part, r, c, i, z, at, :] for r, c, i in ENTRIES])
            for c, value in enumerate(flat_rows(unit_rows(parts[:3], parts[3:]))):
                unit[part // 2, c, part % 2, z, at, :] = value
        return carry

    lax.fori_loop(0, 24, own, 0)
    sites = Sites(unit, x_edge, y_edge, None, out_ref)
    zero = jnp.zeros((8, 128), jnp.float32)
    sum_ref[...] = lax.fori_loop(0, 6, lambda step, total: total + sites.plane(step // 3, step % 3), zero)


def inner_plaquettes(links, x_face, y_face):
    kept = pl.BlockSpec(memory_space=pltpu.VMEM)
    return pl.pallas_call(
        inner_kernel,
        in_specs=[pl.BlockSpec(memory_space=pltpu.HBM)] + [kept] * 2,
        out_specs=[kept] * 5,
        out_shape=[
            pltpu.VMEM((2, 4, 16, 128), jnp.float32),
            pltpu.VMEM((8, 128), jnp.float32),
            pltpu.VMEM((3, 18, 2, 4, 16, 128), jnp.float32),
            pltpu.VMEM((2, 18, 8, 128), jnp.float32),
            pltpu.VMEM((2, 18, 8, 128), jnp.float32),
        ],
        scratch_shapes=[
            pltpu.VMEM((6, 2, 3, 2, 4, 16, 128), jnp.float32),
            pltpu.SemaphoreType.DMA((6,)),
        ],
        compiler_params=pltpu.CompilerParams(vmem_limit_bytes=VMEM_LIMIT),
    )(links, x_face, y_face)


def outer_kernel(inner_ref, part_ref, unit, x_edge, y_edge, z_ref, out_ref, sum_ref, z_edge):
    for t in range(2):
        for z in range(3):
            out_ref[t, z] = inner_ref[t, z]

    def above(step, carry):
        m = step // 2
        t = step % 2
        for h in range(2):
            at = pl.ds(8 * h, 8)
            parts = pairs([z_ref[m, r, c, i, t, at, :] for r, c, i in ENTRIES])
            for c, value in enumerate(flat_rows(unit_rows(parts[:3], parts[3:]))):
                z_edge[m, c, t, at, :] = value
        return carry

    lax.fori_loop(0, 4, above, 0)
    sites = Sites(unit, x_edge, y_edge, z_edge, out_ref)
    total = lax.fori_loop(0, 2, lambda t, total: total + sites.plane(t, 3), part_ref[...])
    sum_ref[...] = jnp.broadcast_to(jnp.sum(total, keepdims=True), (8, 128))


def outer_plaquettes(inner, part, unit, x_edge, y_edge, z_face):
    kept = pl.BlockSpec(memory_space=pltpu.VMEM)
    return pl.pallas_call(
        outer_kernel,
        in_specs=[kept] * 6,
        out_shape=[
            jax.ShapeDtypeStruct((2, 4, 16, 128), jnp.float32),
            jax.ShapeDtypeStruct((8, 128), jnp.float32),
        ],
        scratch_shapes=[pltpu.VMEM((2, 18, 2, 16, 128), jnp.float32)],
        compiler_params=pltpu.CompilerParams(vmem_limit_bytes=VMEM_LIMIT),
    )(inner, part, unit, x_edge, y_edge, z_face)


def put_planes(sources, bounds, placed, out_ref, planes, sem):
    def copy_out(places, part, m):
        t, j = places[part]
        return pltpu.make_async_copy(planes.at[part, m], out_ref.at[pl.ds(18 * m, 18), t, j], sem.at[part, m])

    def decode(part, m):
        rows, stride, start, step, half = sources[part]
        for h in range(2):
            at = half(h) * stride + start + m * step
            values = [rows[pl.ds(at + p, 8, stride=stride), :] for p in range(8)]
            for c, value in enumerate(flat_rows(from_parameters(values))):
                planes[part, m, c, pl.ds(8 * h, 8), :] = value

    parts = range(len(sources))
    for part in parts:
        decode(part, 0)
    if bounds is not None:
        bounds.wait()
    places = placed()
    for part in parts:
        copy_out(places, part, 0).start()

    def one(m, carry):
        for part in parts:
            decode(part, m)
            copy_out(places, part, m).start()
        return carry

    lax.fori_loop(1, 4, one, 0)
    for m in range(4):
        for part in parts:
            copy_out(places, part, m).wait()


PLANE_SCRATCH = [
    pltpu.VMEM((4, 4, 18, 16, 128), jnp.float32),
    pltpu.SemaphoreType.DMA((4, 4)),
    pltpu.SMEM((2, 9), jnp.int32),
    pltpu.SemaphoreType.DMA,
]


def decode_kernel(bounds_in, own_ref, out_ref, planes, sem, bounds_ref, bounds_sem, zeros, zero_sem):
    bounds = pltpu.make_async_copy(bounds_in, bounds_ref, bounds_sem)
    bounds.start()
    w = lax.axis_index("zt")
    zeros[...] = jnp.zeros((18, 16, 128), jnp.float32)

    def fill(t, j, m):
        return pltpu.make_async_copy(zeros, out_ref.at[pl.ds(18 * m, 18), t, j], zero_sem.at[t, j - 2])

    def every_empty(act):
        for t in range(2):
            depth = bounds_ref[t, w + 1] - bounds_ref[t, w]
            for j in range(2, 6):

                @pl.when(j >= depth)
                def _(t=t, j=j):
                    for m in range(4):
                        act(fill(t, j, m))

    bounds.wait()
    every_empty(lambda copy: copy.start())
    top, bottom = moving_times(bounds_ref, w)
    rows = own_ref.reshape(16 * 192, 128)
    planes_in = ((1 - top, 3, 5 - top), (1 - bottom, 0, 2 - 2 * bottom), (0, 1, 1), (1, 1, 3))
    sources = [(rows, 192, 8 * slot, 48, block_half) for t, z, slot in planes_in]
    places = [(t, z + 4 * w - bounds_ref[t, w]) for t, z, slot in planes_in]
    put_planes(sources, None, lambda: places, out_ref, planes, sem)
    every_empty(lambda copy: copy.wait())


def decoded(bounds, own):
    return pl.pallas_call(
        decode_kernel,
        in_specs=[pl.BlockSpec(memory_space=pl.ANY), pl.BlockSpec(memory_space=pltpu.VMEM)],
        out_specs=pl.BlockSpec(memory_space=pltpu.HBM),
        out_shape=jax.ShapeDtypeStruct((72, 2, 6, 16, 128), jnp.float32),
        scratch_shapes=PLANE_SCRATCH
        + [pltpu.VMEM((18, 16, 128), jnp.float32), pltpu.SemaphoreType.DMA((2, 4))],
        compiler_params=pltpu.CompilerParams(vmem_limit_bytes=VMEM_LIMIT),
    )(bounds, own)


def cut_kernel(bounds_ref, own_ref, first_ref, second_ref):
    w = lax.axis_index("zt")
    top, bottom = moving_times(bounds_ref, w)
    even = w % 2 == 0
    top = 32 + 8 * top
    bottom = 16 * bottom
    first = pl.multiple_of(jnp.where(even, top, bottom), 8)
    second = pl.multiple_of(jnp.where(even, bottom, top), 8)
    for h in range(2):
        here = pl.ds(8 * h, 8)
        there = pl.ds(block_half(h), 8)
        for m in range(4):
            first_ref[here, m] = own_ref[there, m, pl.ds(first, 8), :]
            second_ref[here, m] = own_ref[there, m, pl.ds(second, 8), :]


def cut_planes(bounds, own):
    return pl.pallas_call(
        cut_kernel,
        in_specs=[pl.BlockSpec(memory_space=pltpu.SMEM), pl.BlockSpec(memory_space=pltpu.VMEM)],
        out_shape=[jax.ShapeDtypeStruct((16, 4, 8, 128), jnp.float32)] * 2,
        compiler_params=pltpu.CompilerParams(vmem_limit_bytes=VMEM_LIMIT),
    )(bounds, own)


def rest_kernel(
    count,
    bounds_in,
    first_ref,
    second_ref,
    rest_ref,
    whole_ref,
    out_ref,
    mean_ref,
    planes,
    sem,
    bounds_ref,
    bounds_sem,
    mean,
    mean_sem,
):
    bounds = pltpu.make_async_copy(bounds_in, bounds_ref, bounds_sem)
    bounds.start()
    w = lax.axis_index("zt")
    totals = []
    for h in range(2):
        part = rest_ref[block_half(h), pl.ds(64, 8), :]
        for n in range(1, 8):
            part = part + rest_ref[block_half(h) + n, pl.ds(64, 8), :]
        totals.append(part)
    mean[0, 0] = jnp.max(totals[0] + totals[1]) * (1.0 / count)
    mean_out = pltpu.make_async_copy(mean, mean_ref, mean_sem)
    mean_out.start()
    rows = rest_ref.reshape(16 * 72, 128)
    sources = [(ref.reshape(16 * 32, 128), 32, 0, 8, lambda h: 8 * h) for ref in (first_ref, second_ref)]
    sources += [(rows, 72, 8 * t, 16, block_half) for t in range(2)]

    def placed():
        top, bottom = moving_times(bounds_ref, w)
        even = w % 2 == 0
        low_time = jnp.where(w == 0, bottom, 1 - bottom)
        high_time = jnp.where(w == 7, top, 1 - top)
        high_at = jnp.where(w == 7, 3, 4) + 4 * w - bounds_ref[high_time, w]
        low_at = jnp.int32(0)
        places = [
            (jnp.where(even, high_time, low_time), jnp.where(even, high_at, low_at)),
            (jnp.where(even, low_time, high_time), jnp.where(even, low_at, high_at)),
        ]
        return places + [(t, 2 + 4 * w - bounds_ref[t, w]) for t in range(2)]

    put_planes(sources, bounds, placed, out_ref, planes, sem)
    mean_out.wait()


def with_rest(bounds, first, second, rest, whole, count):
    kept = pl.BlockSpec(memory_space=pltpu.VMEM)
    there = pl.BlockSpec(memory_space=pltpu.HBM)
    return pl.pallas_call(
        lambda *refs: rest_kernel(count, *refs),
        in_specs=[pl.BlockSpec(memory_space=pl.ANY)] + [kept] * 3 + [there],
        out_specs=[there, there],
        out_shape=[
            jax.ShapeDtypeStruct((72, 2, 6, 16, 128), jnp.float32),
            jax.ShapeDtypeStruct((1, 1), jnp.float32),
        ],
        input_output_aliases={4: 0},
        scratch_shapes=PLANE_SCRATCH + [pltpu.SMEM((1, 1), jnp.float32), pltpu.SemaphoreType.DMA],
        compiler_params=pltpu.CompilerParams(vmem_limit_bytes=VMEM_LIMIT),
    )(bounds, first, second, rest, whole)


def summed(value, steps):
    for axis, by in steps:
        count = lax.axis_size(axis)
        value = value + lax.ppermute(value, axis, [(i, i ^ by) for i in range(count)])
    return value


def spread(payload):
    places = [(gx, gy) for gy in range(4) for gx in range(4)]
    groups = [[(gx * 4 + gy) * 8 + w for gx, gy in places[8 * (w % 2) :] + places[: 8 * (w % 2)]] for w in range(8)]
    return lax.all_to_all(
        payload, ("gx", "gy", "zt"), split_axis=0, concat_axis=0, axis_index_groups=groups, tiled=True
    )


def local(links, bounds):
    held = pltpu.with_memory_space_constraint(links, pltpu.HBM)
    x_face, y_face, taken, rest = taken_links(held)
    y_face = passed_along(y_face, "gy", -1)
    x_face = passed_along(x_face, "gx", -1)
    payload, z_face, rest_3 = encoded(held, taken)
    payload, links, x_face, y_face, z_face = lax.optimization_barrier((payload, links, x_face, y_face, z_face))
    held = pltpu.with_memory_space_constraint(links, pltpu.HBM)
    moved = spread(payload)
    z_face = passed_along(z_face, "zt", -1)
    plaquette, total = outer_plaquettes(*inner_plaquettes(held, x_face, y_face), z_face)
    total = summed(total, (("zt", 1), ("zt", 6), ("zt", 2)))
    rest = encoded_rest(rest, rest_3, total)
    moved, rest = lax.optimization_barrier((moved, rest))
    moved_rest = spread(rest)
    first, second = cut_planes(bounds, moved)
    first = lax.ppermute(first, "zt", [(i, i ^ 1) for i in range(8)])
    second = lax.ppermute(second, "zt", [(0, 0), (7, 7)] + [(i, (i + 1 ^ 1) - 1) for i in range(1, 7)])
    file_links = decoded(bounds, moved)
    file_links, mean = with_rest(bounds, first, second, moved_rest, file_links, plaquette.size * 128)
    return file_links.reshape(4, 3, 3, 2, 2, 6, 4, 1, 4, 1, 128), plaquette, mean[0, 0]


def solution(mesh):
    in_specs = (P(None, None, None, None, None, "zt", "gy", "gx"), P())
    out_specs = (
        P(None, None, None, None, None, "zt", None, "gx", None, "gy", None),
        P(None, "zt", "gy", "gx"),
        P(),
    )
    return jax.shard_map(local, mesh=mesh, in_specs=in_specs, out_specs=out_specs, check_vma=False)
```
